32 devices in a mesh: dp: 2 (over y), tensor: 4 (over x, core), expert: 4 (over z).
Axes of the slice: x: 2, y: 2, z: 4, core: 2. Of those that a mesh axis runs over, the one named last changes fastest.
Arguments:
- tokens: bfloat16 [1024, 2048], P('dp', 'tensor'), may hold values from -6 to 6
- grad_out: bfloat16 [1024, 2048], P('dp', 'tensor'), may hold values from -6 to 6
- routes: int32 [1024, 8], P('dp'), may hold values from 0 to 127, all different within a row; in each aligned block of 512 rows (0 to 511, 512 to 1023, ...) at most 48 rows name the same one
- gates: float32 [1024, 8], P('dp'), may hold values from 0.03 to 0.3
- gate_weight: bfloat16 [16, 1536, 2048], P(('expert', 'tensor'), 'dp'), may hold values from -0.125 to 0.125
- up_weight: bfloat16 [16, 1536, 2048], P(('expert', 'tensor'), 'dp'), may hold values from -0.125 to 0.125
- down_weight: bfloat16 [16, 1536, 2048], P(('expert', 'tensor'), 'dp'), may hold values from -0.15625 to 0.15625
Outputs:
- mixed: bfloat16 [1024, 2048], P('dp', 'tensor')
- grad_tokens: bfloat16 [1024, 2048], P('dp', 'tensor')
- grad_gates: float32 [1024, 8], P('dp')
The draws below stay inside these ranges and needn't reach their ends.
Inputs may be any that keep to these rules, and one draw needn't show every extreme that they name: `routes`: each row names 8 different experts. Among the 512 rows of one block no expert is named more than 48 times, a bound that some block reaches.
All inputs are finite; a program needn't handle non-finite values.
Results may differ from the reference program's by a relative error of at most 0.017.
Values may be sent and summed in bfloat16 or wider, within the bound.
No kernel may reach another device: no remote copies, remote signals or barrier semaphores. Data moves between devices by JAX's collectives and lax.ppermute only.
A program may use at most 64 MiB of HBM per device.

```python
import math
import jax
import jax.numpy as jnp
import numpy as np
from jax import lax

D = 2048
FF = 1536
ALL_EXPERTS = 128
TOPK = 8
TOK_DEV = 512
CAP = 48
EXPERTS = 16
TOKENS = 1024
N_DP = 2
N_TENSOR = 4
N_EXPERT = 4


def block_scale(own_key, shape, shards, smallest, high):
    level = 1.0
    for position, shards_of in shards:
        steps = jax.random.uniform(jax.random.fold_in(jax.random.fold_in(own_key, 6), position), (shards_of,), jnp.float32, smallest / len(shards), high / len(shards))
        level = level * jnp.repeat(jnp.exp(steps), shape[position] // shards_of).reshape((-1,) + (1,) * (len(shape) - 1 - position))
    return level


def deal_out(stream_key, own, number, rows, amount, top, limit, lean):
    order = jax.random.permutation(stream_key, amount)
    crowded, ordinary = portions_of(amount, rows * top, limit, lean, True), portions_of(amount, rows * top, limit, lean, False)
    places = jnp.arange(amount)

    def named(lengths, offset_by):
        used = int((lengths > 0).sum())
        fixed = max(1, used // 4)
        moved = fixed + (places - fixed + offset_by * (used - fixed)) % max(1, amount - fixed)
        return jnp.zeros((amount,), jnp.int32).at[order[jnp.where(places < fixed, places, moved)]].set(jnp.asarray(lengths, jnp.int32))

    lengths = jnp.where(number % 4 == 0, named(crowded, number // 4), named(ordinary, number - number // 4 - 1))
    mixed = jax.random.permutation(jax.random.fold_in(own, 3), amount)
    donor, taker = mixed[0:amount // 2 * 2:2], mixed[1:amount // 2 * 2:2]
    slack = jnp.minimum(lengths[donor] - 1, limit - lengths[taker]) // 2
    slack = jnp.where((donor == order[0]) | (taker == order[0]) | (lengths[taker] == 0), 0, jnp.maximum(slack, 0))
    moved = jax.random.randint(jax.random.fold_in(own, 4), (amount // 2,), 0, 1 << 20) % (slack + 1)
    lengths = lengths.at[donor].add(-moved).at[taker].add(moved)
    labels = jnp.searchsorted(jnp.cumsum(lengths), jnp.arange(rows * top), side="right").astype(jnp.int32)
    listing = labels.reshape(top, rows).T
    listing = listing[jax.random.permutation(jax.random.fold_in(own, 1), rows)]
    offset_by = jax.random.randint(jax.random.fold_in(own, 2), (rows, 1), 0, top)
    return jnp.take_along_axis(listing, (jnp.arange(top)[None, :] + offset_by) % top, axis=1)


def portions_of(count, total, bound, skew, full):
    weights = [(1 << 20) // math.isqrt(grade ** skew) + 1 for grade in range(1, count + 1)]
    largest = bound if full else min(bound, max(-(-total // count), total * weights[0] // sum(weights)))
    least = 1 if total - largest >= count - 1 else 0
    holding, surplus = [largest] + [least] * (count - 1), total - largest - least * (count - 1)
    while surplus > 0:
        candidates = [i for i in range(1, count) if holding[i] < largest] or [i for i in range(1, count) if holding[i] < bound]
        mass, remaining = sum([weights[i] for i in candidates]), surplus
        for i in candidates:
            addition = min(bound - holding[i], max(1, remaining * weights[i] // mass), surplus)
            holding[i] = holding[i] + addition
            surplus = surplus - addition
    return np.array(holding)


def gaussian(stream_key, shape, spread, bound, pieces=(), kind=jnp.bfloat16):
    gain = block_scale(stream_key, shape, pieces, -0.22, 0.18) if pieces else 1.0
    values = jax.random.normal(stream_key, shape, jnp.float32) * spread * gain
    return jnp.minimum(jnp.maximum(values, -bound), bound).astype(kind)


def setup_inputs(seed: int = 0) -> dict:
    keys = jax.random.split(jax.random.key(seed), 8)
    tokens = gaussian(keys[0], (TOKENS, D), 1.0, 6.0, ((0, 2), (1, 4)))
    grad_out = gaussian(keys[1], (TOKENS, D), 1.0, 6.0, ((0, 2), (1, 4)))
    routes_keys = jax.random.split(jax.random.fold_in(keys[2], 1), TOKENS // TOK_DEV)
    routes_turns = jax.random.permutation(jax.random.fold_in(keys[2], 3), TOKENS // TOK_DEV)
    routes = jax.vmap(lambda own, number: deal_out(jax.random.fold_in(keys[2], 2), own, number, TOK_DEV, ALL_EXPERTS, TOPK, CAP, 1))(routes_keys, routes_turns).reshape((TOKENS, TOPK))
    gates = jnp.clip(jnp.exp(math.log(0.3) - 2.3025852 * jax.random.uniform(keys[3], (TOKENS, TOPK), jnp.float32) ** block_scale(keys[3], (TOKENS, TOPK), ((0, 2),), -0.2, 0.2)), 0.03, 0.3)
    gate_weight = gaussian(keys[4], (EXPERTS, FF, D), D ** -0.5, 0.125, ((0, 16), (1, 2)))
    up_weight = gaussian(keys[5], (EXPERTS, FF, D), D ** -0.5, 0.125, ((0, 16), (1, 2)))
    down_weight = gaussian(keys[6], (EXPERTS, FF, D), FF ** -0.5, 0.15625, ((0, 16), (1, 2)))
    return dict(tokens=tokens, grad_out=grad_out, routes=routes, gates=gates, gate_weight=gate_weight, up_weight=up_weight, down_weight=down_weight)


def silu_parts(gate_pre):
    sigmoid_val = jax.nn.sigmoid(gate_pre)
    return gate_pre * sigmoid_val, sigmoid_val * (1.0 + gate_pre * (1.0 - sigmoid_val))


def slot_numbers(route_block):
    flat_ids = route_block.reshape(-1)
    onehot = (flat_ids[:, None] == jnp.arange(EXPERTS, dtype=jnp.int32)[None, :]).astype(jnp.int32)
    ranking = jnp.sum((jnp.cumsum(onehot, axis=0) - 1) * onehot, axis=1).astype(jnp.int32)
    slot_ids = jnp.where(flat_ids < EXPERTS, flat_ids * CAP + ranking, -1).astype(jnp.int32)
    return slot_ids.reshape(TOK_DEV, TOPK)


def selector(slot_ids, number):
    return slot_ids[None, :, :] == jnp.arange(number, dtype=jnp.int32)[:, None, None]


def rounded(values):
    return lax.optimization_barrier(values.astype(jnp.bfloat16)).astype(jnp.float32)


def reference(tokens, grad_out, routes, gates, gate_weight, up_weight, down_weight):
    hid_dev = FF // N_DP
    contract = (((1,), (1,)), ((), ()))
    slots_all = lax.map(slot_numbers, routes.reshape(N_DP, TOK_DEV, TOPK))

    def dispatch(operands):
        tok_block, grad_block, slot_block = operands
        picker = jnp.any(selector(slot_block, EXPERTS * CAP), axis=2).astype(jnp.bfloat16)
        sent_tok = jnp.dot(picker, tok_block, preferred_element_type=jnp.float32).astype(jnp.bfloat16)
        sent_grad = jnp.dot(picker, grad_block, preferred_element_type=jnp.float32).astype(jnp.bfloat16)
        return sent_tok, sent_grad

    sent_tok, sent_grad = lax.map(dispatch, (tokens.reshape(N_DP, TOK_DEV, D), grad_out.reshape(N_DP, TOK_DEV, D), slots_all))

    def to_experts(values):
        return values.reshape(N_DP, EXPERTS, CAP, D).transpose(1, 0, 2, 3).reshape(EXPERTS, N_DP * CAP, D)

    def expert(operands):
        rows_in, rows_grad, w_gate, w_up, w_down = operands
        gate_pre = lax.dot_general(rows_in, w_gate, contract, preferred_element_type=jnp.float32)
        up_pre = lax.dot_general(rows_in, w_up, contract, preferred_element_type=jnp.float32)
        activated, slope_val = silu_parts(gate_pre)
        hidden = (activated * up_pre).astype(jnp.bfloat16)
        hid_blocks = hidden.astype(jnp.float32).reshape(-1, N_DP, hid_dev)
        down_blocks = w_down.astype(jnp.float32).reshape(N_DP, hid_dev, D)
        partials = jnp.einsum("rjf,jfd->jrd", hid_blocks, down_blocks, precision=lax.Precision.HIGHEST)
        expert_out = jnp.sum(rounded(partials), axis=0).astype(jnp.bfloat16)
        grad_hid = lax.dot_general(rows_grad, w_down, contract, preferred_element_type=jnp.float32)
        grad_gate = (grad_hid * (up_pre * slope_val)).astype(jnp.bfloat16)
        grad_up = (grad_hid * activated).astype(jnp.bfloat16)
        gate_blocks = w_gate.astype(jnp.float32).reshape(N_DP, hid_dev, D)
        up_blocks = w_up.astype(jnp.float32).reshape(N_DP, hid_dev, D)
        back_parts = jnp.einsum("rjf,jfd->jrd", grad_gate.astype(jnp.float32).reshape(-1, N_DP, hid_dev), gate_blocks, precision=lax.Precision.HIGHEST)
        back_parts = back_parts + jnp.einsum("rjf,jfd->jrd", grad_up.astype(jnp.float32).reshape(-1, N_DP, hid_dev), up_blocks, precision=lax.Precision.HIGHEST)
        expert_back = jnp.sum(rounded(back_parts), axis=0).astype(jnp.bfloat16)
        slot_grads = jnp.sum(expert_out.astype(jnp.float32) * rows_grad.astype(jnp.float32), axis=1)
        return expert_out, expert_back, slot_grads

    outs, backs, slot_grads = lax.map(expert, (to_experts(sent_tok), to_experts(sent_grad), gate_weight, up_weight, down_weight))

    def to_blocks(values):
        return values.reshape(EXPERTS, N_DP, CAP, D).transpose(1, 0, 2, 3).reshape(N_DP, EXPERTS * CAP, D)

    grad_blocks = slot_grads.reshape(EXPERTS, N_DP, CAP).transpose(1, 0, 2).reshape(N_DP, EXPERTS * CAP)

    def combine(operands):
        slot_block, gate_block, out_block, back_block, grad_block = operands
        choose = selector(slot_block, EXPERTS * CAP).astype(jnp.float32)
        weighted = jnp.einsum("stk,tk->ts", choose, gate_block, precision=lax.Precision.HIGHEST).astype(jnp.bfloat16)
        grouped = weighted.astype(jnp.float32).reshape(TOK_DEV, N_EXPERT, N_TENSOR * CAP)

        def group_sum(slot_rows):
            rows_grouped = slot_rows.astype(jnp.float32).reshape(N_EXPERT, N_TENSOR * CAP, D)
            parts = jnp.einsum("tgs,gsd->gtd", grouped, rows_grouped, precision=lax.Precision.HIGHEST)
            return jnp.sum(rounded(parts), axis=0).astype(jnp.bfloat16)

        mixed = group_sum(out_block)
        grad_tokens = group_sum(back_block)
        grad_gates = jnp.einsum("stk,s->tk", choose, grad_block, precision=lax.Precision.HIGHEST)
        return mixed, grad_tokens, grad_gates

    mixed, grad_tokens, grad_gates = lax.map(combine, (slots_all, gates.reshape(N_DP, TOK_DEV, TOPK), to_blocks(outs), to_blocks(backs), grad_blocks))
    return mixed.reshape(TOKENS, D), grad_tokens.reshape(TOKENS, D), grad_gates.reshape(TOKENS, TOPK)
```

```python
import functools

import jax
import jax.numpy as jnp
from jax import lax
from jax.experimental import pallas as pl
from jax.experimental.pallas import tpu as pltpu
from jax.sharding import PartitionSpec as P

CAP = 48
LANES = 128
BF16 = jnp.bfloat16
F32 = jnp.float32
CONTRACT_LAST = (((1,), (1,)), ((), ()))


def vmem():
    return pl.BlockSpec(memory_space=pltpu.VMEM)


def cost(flops, moved):
    return pl.CostEstimate(flops=int(flops), bytes_accessed=int(moved), transcendentals=0)


def pick_rows(key_ref, source_ref, piece_refs):
    groups = len(piece_refs)
    rows = source_ref.shape[0]
    t, e = lax.axis_index("tensor"), lax.axis_index("expert")
    slot = lax.broadcasted_iota(jnp.int32, (CAP, rows), 0).astype(F32)
    masks = []
    for dt in range(groups):
        expert = e * groups + lax.rem(t + dt, groups)
        masks.append((key_ref[pl.ds(expert, 1), :] == slot).astype(BF16))
    picked = jnp.dot(jnp.concatenate(masks, axis=0), source_ref[...], preferred_element_type=F32).astype(BF16)
    for dt in range(groups):
        piece_refs[dt][...] = picked[dt * CAP : (dt + 1) * CAP]


def number_kernel(routes_ref, tokens_ref, key_ref, *piece_refs):
    experts, rows = key_ref.shape
    ids = lax.broadcasted_iota(jnp.int32, (experts, rows), 0)
    hit = jnp.zeros((experts, rows), F32)
    for r in range(routes_ref.shape[0]):
        hit = hit + (routes_ref[r : r + 1, :] == ids).astype(F32)
    before = (
        lax.broadcasted_iota(jnp.int32, (LANES, LANES), 0) < lax.broadcasted_iota(jnp.int32, (LANES, LANES), 1)
    ).astype(BF16)
    offset = jnp.zeros((experts, 1), F32)
    for start in range(0, rows, LANES):
        part = hit[:, start : start + LANES]
        rank = jnp.dot(part.astype(BF16), before, preferred_element_type=F32) + offset
        offset = offset + jnp.sum(part, axis=1, keepdims=True)
        key_ref[:, start : start + LANES] = jnp.where(part > 0.0, rank, -1.0)
    pick_rows(key_ref, tokens_ref, piece_refs)


def pick_kernel(key_ref, source_ref, *piece_refs):
    pick_rows(key_ref, source_ref, piece_refs)


def gather_pieces(x_ref, piece_refs, groups):
    t = lax.axis_index("tensor")
    width = piece_refs[0].shape[1]
    for index, piece in enumerate(piece_refs):
        db, dt = divmod(index, groups)
        owner = lax.rem(t - dt + groups, groups)
        x_ref[db * CAP : (db + 1) * CAP, pl.ds(pl.multiple_of(owner * width, width), width)] = piece[...]


def scatter_pieces(y_ref, piece_refs, groups):
    t = lax.axis_index("tensor")
    blocks = len(piece_refs) // groups
    width = piece_refs[0].shape[1]
    for index, piece in enumerate(piece_refs):
        db, dt = divmod(index, groups)
        row = (-db) % blocks * CAP
        owner = lax.rem(t + dt, groups)
        piece[...] = y_ref[row : row + CAP, pl.ds(pl.multiple_of(owner * width, width), width)].astype(BF16)


def forward_kernel(groups, count, *refs):
    pieces, (gate_ref, up_ref, down_ref) = refs[:count], refs[count : count + 3]
    act_ref, scale_ref, hid_ref = refs[count + 3 : count + 6]
    outs, (x_ref, y_ref) = refs[count + 6 : 2 * count + 6], refs[2 * count + 6 :]
    step = pl.program_id(0)

    @pl.when(step == 0)
    def _():
        gather_pieces(x_ref, pieces, groups)
        y_ref[...] = jnp.zeros_like(y_ref)

    gate_pre = lax.dot_general(x_ref[...], gate_ref[0], CONTRACT_LAST, preferred_element_type=F32)
    up_pre = lax.dot_general(x_ref[...], up_ref[0], CONTRACT_LAST, preferred_element_type=F32)
    sig = jax.nn.sigmoid(gate_pre)
    act = gate_pre * sig
    hidden = (act * up_pre).astype(BF16)
    act_ref[...] = act
    scale_ref[...] = up_pre * (sig * (1.0 + gate_pre * (1.0 - sig)))
    hid_ref[...] = hidden
    y_ref[...] += jnp.dot(hidden, down_ref[0], preferred_element_type=F32)

    @pl.when(step == pl.num_programs(0) - 1)
    def _():
        scatter_pieces(y_ref, outs, groups)


def backward_kernel(groups, count, *refs):
    pieces, (gate_ref, up_ref, down_ref) = refs[:count], refs[count : count + 3]
    act_ref, scale_ref, hid_ref = refs[count + 3 : count + 6]
    outs, sum_ref = refs[count + 6 : 2 * count + 6], refs[2 * count + 6]
    x_ref, y_ref = refs[2 * count + 7 :]
    step = pl.program_id(0)

    @pl.when(step == 0)
    def _():
        gather_pieces(x_ref, pieces, groups)
        y_ref[...] = jnp.zeros_like(y_ref)
        sum_ref[...] = jnp.zeros_like(sum_ref)

    grad_hid = lax.dot_general(x_ref[...], down_ref[0], CONTRACT_LAST, preferred_element_type=F32)
    grad_gate = (grad_hid * scale_ref[...]).astype(BF16)
    grad_up = (grad_hid * act_ref[...]).astype(BF16)
    sum_ref[...] += lax.dot_general(
        jnp.ones((sum_ref.shape[0], grad_hid.shape[1]), F32),
        grad_hid * hid_ref[...].astype(F32),
        CONTRACT_LAST,
        preferred_element_type=F32,
        precision=lax.Precision.HIGHEST,
    )
    y_ref[...] += jnp.dot(grad_gate, gate_ref[0], preferred_element_type=F32) + jnp.dot(
        grad_up, up_ref[0], preferred_element_type=F32
    )

    @pl.when(step == pl.num_programs(0) - 1)
    def _():
        scatter_pieces(y_ref, outs, groups)


def add_blocks_kernel(groups, *refs):
    pieces, out_ref = refs[:-1], refs[-1]
    for dt in range(groups):
        total = pieces[dt][...].astype(F32)
        for piece in pieces[groups + dt :: groups]:
            total = total + piece[...].astype(F32)
        out_ref[dt * CAP : (dt + 1) * CAP, :] = total.astype(BF16)


def weights_kernel(groups, columns, routes_ref, gates_ref, key_ref, out_ref, gate_ref):
    experts, rows = key_ref.shape
    t, e = lax.axis_index("tensor"), lax.axis_index("expert")
    ids = lax.broadcasted_iota(jnp.int32, (experts, rows), 0)
    gate = jnp.zeros((experts, rows), F32)
    for r in range(routes_ref.shape[0]):
        gate = gate + jnp.where(routes_ref[r : r + 1, :] == ids, gates_ref[r : r + 1, :], 0.0)
    gate_ref[...] = gate
    slot = lax.broadcasted_iota(jnp.int32, (CAP, rows), 0).astype(F32)
    for dz in range(columns):
        blocks = []
        for dt in range(groups):
            expert = lax.rem(e - dz + columns, columns) * groups + lax.rem(t - dt + groups, groups)
            same = key_ref[pl.ds(expert, 1), :] == slot
            blocks.append(jnp.where(same, gate_ref[pl.ds(expert, 1), :], 0.0))
        width = groups * CAP
        out_ref[dz * width : (dz + 1) * width, :] = jnp.concatenate(blocks, axis=0).astype(BF16)


def combine_kernel(weight_ref, *refs):
    parts, out_ref, all_ref = refs[:-2], refs[-2], refs[-1]
    height = parts[0].shape[0]
    for index, part in enumerate(parts):
        all_ref[index * height : (index + 1) * height, :] = part[...]
    out_ref[...] = lax.dot_general(
        weight_ref[...], all_ref[...], (((0,), (0,)), ((), ())), preferred_element_type=F32
    ).astype(BF16)


def gate_grad_kernel(routes_ref, key_ref, sums_ref, out_ref):
    experts, rows = key_ref.shape
    slot = lax.broadcasted_iota(jnp.int32, (CAP, rows), 0).astype(F32)
    total = jnp.zeros(out_ref.shape, F32)
    routes = routes_ref[...]
    for expert in range(experts):
        same = key_ref[expert : expert + 1, :] == slot
        row = jnp.sum(jnp.where(same, sums_ref[:, expert : expert + 1], 0.0), axis=0, keepdims=True)
        total = total + jnp.where(routes == expert, row, 0.0)
    out_ref[...] = total


def body(sizes, tokens, grad_out, routes, gates, gate_weight, up_weight, down_weight):
    n_dp, groups, columns = sizes
    experts = groups * columns
    rows, width = tokens.shape
    _, hid_dev, feats = gate_weight.shape
    count = n_dp * groups
    tall = n_dp * CAP
    chunk = 256 if hid_dev % 256 == 0 else hid_dev
    routes_t, gates_t = routes.T, gates.T

    piece = jax.ShapeDtypeStruct((CAP, width), BF16)
    key, *tok_pieces = pl.pallas_call(
        number_kernel,
        out_shape=[jax.ShapeDtypeStruct((experts, rows), F32)] + [piece] * groups,
        in_specs=[vmem()] * 2,
        out_specs=[vmem()] * (groups + 1),
        cost_estimate=cost(2 * groups * CAP * rows * width, 2 * rows * width),
        name="number",
    )(routes_t, tokens)
    grad_pieces = pl.pallas_call(
        pick_kernel,
        out_shape=[piece] * groups,
        in_specs=[vmem()] * 2,
        out_specs=[vmem()] * groups,
        cost_estimate=cost(2 * groups * CAP * rows * width, 2 * rows * width),
        name="pick",
    )(key, grad_out)

    def shift(value, db, dt):
        if (db, dt) == (0, 0):
            return value
        pairs = []
        for b in range(n_dp):
            for t in range(groups):
                pairs.append((b * groups + t, (b + db) % n_dp * groups + (t + dt) % groups))
        return lax.ppermute(value, ("dp", "tensor"), pairs)

    def spread(pieces):
        return [shift(pieces[dt], db, dt) for db in range(n_dp) for dt in range(groups)]

    def exchange(pieces):
        return [shift(pieces[db * groups + dt], db, dt) for db in range(n_dp) for dt in range(groups)]

    def whole_block(shape):
        return pl.BlockSpec(shape, lambda i: (0,) * len(shape))

    weight_block = pl.BlockSpec((1, chunk, feats), lambda i: (0, i, 0))
    hidden_block = pl.BlockSpec((tall, chunk), lambda i: (0, i))
    piece_block = whole_block((CAP, width))
    scratch = [pltpu.VMEM((tall, feats), BF16), pltpu.VMEM((tall, feats), F32)]
    matmul_flops = 2 * tall * hid_dev * feats

    tok_in = spread(tok_pieces)
    grad_in = spread(grad_pieces)
    act, scale, hidden, *outs = pl.pallas_call(
        functools.partial(forward_kernel, groups, count),
        grid=(hid_dev // chunk,),
        out_shape=[
            jax.ShapeDtypeStruct((tall, hid_dev), F32),
            jax.ShapeDtypeStruct((tall, hid_dev), F32),
            jax.ShapeDtypeStruct((tall, hid_dev), BF16),
        ]
        + [piece] * count,
        in_specs=[piece_block] * count + [weight_block] * 3,
        out_specs=[hidden_block] * 3 + [piece_block] * count,
        scratch_shapes=scratch,
        cost_estimate=cost(3 * matmul_flops, 6 * hid_dev * feats),
        name="forward",
    )(*tok_in, gate_weight, up_weight, down_weight)
    out_in = exchange(outs)
    *backs, sums = pl.pallas_call(
        functools.partial(backward_kernel, groups, count),
        grid=(hid_dev // chunk,),
        out_shape=[piece] * count + [jax.ShapeDtypeStruct((8, tall), F32)],
        in_specs=[piece_block] * count + [weight_block] * 3 + [hidden_block] * 3,
        out_specs=[piece_block] * count + [whole_block((8, tall))],
        scratch_shapes=scratch,
        cost_estimate=cost(3 * matmul_flops, 6 * hid_dev * feats),
        name="backward",
    )(*grad_in, gate_weight, up_weight, down_weight, act, scale, hidden)
    back_in = exchange(backs)

    weight_map = pl.pallas_call(
        functools.partial(weights_kernel, groups, columns),
        out_shape=jax.ShapeDtypeStruct((experts * CAP, rows), BF16),
        in_specs=[vmem()] * 3,
        out_specs=vmem(),
        scratch_shapes=[pltpu.VMEM((experts, rows), F32)],
        cost_estimate=cost(experts * CAP * rows, 2 * experts * CAP * rows),
        name="weights",
    )(routes_t, gates_t, key)

    def add_blocks(pieces):
        return pl.pallas_call(
            functools.partial(add_blocks_kernel, groups),
            out_shape=jax.ShapeDtypeStruct((groups * CAP, width), BF16),
            in_specs=[vmem()] * count,
            out_specs=vmem(),
            cost_estimate=cost(count * CAP * width, 4 * count * CAP * width),
            name="add_blocks",
        )(*pieces)

    def across(value):
        parts = [value]
        for dz in range(1, columns):
            parts.append(lax.ppermute(value, "expert", [(z, (z + dz) % columns) for z in range(columns)]))
        return parts

    def combine(parts):
        return pl.pallas_call(
            combine_kernel,
            out_shape=jax.ShapeDtypeStruct((rows, width), BF16),
            in_specs=[vmem()] * (columns + 1),
            out_specs=vmem(),
            scratch_shapes=[pltpu.VMEM((experts * CAP, width), BF16)],
            cost_estimate=cost(2 * experts * CAP * rows * width, 2 * experts * CAP * (rows + width)),
            name="combine",
        )(weight_map, *parts)

    mixed_parts = across(add_blocks(out_in))
    back_parts = across(add_blocks(back_in))
    mixed = combine(mixed_parts)
    grad_tokens = combine(back_parts)

    own = sums[0, :CAP]
    for db in range(1, n_dp):
        row = (-db) % n_dp * CAP
        own = own + lax.ppermute(sums[0, row : row + CAP], "dp", [(b, (b + db) % n_dp) for b in range(n_dp)])
    sums_all = lax.all_gather(own, ("expert", "tensor"), axis=0, tiled=False)
    grad_gates = pl.pallas_call(
        gate_grad_kernel,
        out_shape=jax.ShapeDtypeStruct(routes_t.shape, F32),
        in_specs=[vmem()] * 3,
        out_specs=vmem(),
        cost_estimate=cost(experts * CAP * rows, experts * CAP * rows),
        name="gate_grad",
    )(routes_t, key, sums_all.T)
    return (mixed, grad_tokens, grad_gates.T)


def solution(mesh):
    sizes = (mesh.shape["dp"], mesh.shape["tensor"], mesh.shape["expert"])
    return jax.shard_map(
        functools.partial(body, sizes),
        mesh=mesh,
        in_specs=(
            P("dp", "tensor"),
            P("dp", "tensor"),
            P("dp", None),
            P("dp", None),
            P(("expert", "tensor"), "dp", None),
            P(("expert", "tensor"), "dp", None),
            P(("expert", "tensor"), "dp", None),
        ),
        out_specs=(P("dp", "tensor"), P("dp", "tensor"), P("dp", None)),
        check_vma=False,
    )
```

```python
import functools

import jax
import jax.numpy as jnp
from jax import lax
from jax.experimental import pallas as pl
from jax.experimental.pallas import tpu as pltpu
from jax.sharding import PartitionSpec as P

CAP = 48
LANES = 128
BF16 = jnp.bfloat16
F32 = jnp.float32
CONTRACT_LAST = (((1,), (1,)), ((), ()))


def vmem():
    return pl.BlockSpec(memory_space=pltpu.VMEM)


def cost(flops, moved):
    return pl.CostEstimate(flops=int(flops), bytes_accessed=int(moved), transcendentals=0)


def pick_rows(key_ref, source_ref, piece_refs):
    groups = len(piece_refs)
    rows = source_ref.shape[0]
    t, e = lax.axis_index("tensor"), lax.axis_index("expert")
    slot = lax.broadcasted_iota(jnp.int32, (CAP, rows), 0).astype(F32)
    masks = []
    for dt in range(groups):
        expert = e * groups + lax.rem(t + dt, groups)
        masks.append((key_ref[pl.ds(expert, 1), :] == slot).astype(BF16))
    picked = jnp.dot(jnp.concatenate(masks, axis=0), source_ref[...], preferred_element_type=F32).astype(BF16)
    for dt in range(groups):
        piece_refs[dt][...] = picked[dt * CAP : (dt + 1) * CAP]


def number_kernel(routes_ref, tokens_ref, key_ref, *piece_refs):
    experts, rows = key_ref.shape
    ids = lax.broadcasted_iota(jnp.int32, (experts, rows), 0)
    hit = jnp.zeros((experts, rows), F32)
    for r in range(routes_ref.shape[0]):
        hit = hit + (routes_ref[r : r + 1, :] == ids).astype(F32)
    before = (
        lax.broadcasted_iota(jnp.int32, (LANES, LANES), 0) < lax.broadcasted_iota(jnp.int32, (LANES, LANES), 1)
    ).astype(BF16)
    offset = jnp.zeros((experts, 1), F32)
    for start in range(0, rows, LANES):
        part = hit[:, start : start + LANES]
        rank = jnp.dot(part.astype(BF16), before, preferred_element_type=F32) + offset
        offset = offset + jnp.sum(part, axis=1, keepdims=True)
        key_ref[:, start : start + LANES] = jnp.where(part > 0.0, rank, -1.0)
    pick_rows(key_ref, tokens_ref, piece_refs)


def pick_kernel(key_ref, source_ref, *piece_refs):
    pick_rows(key_ref, source_ref, piece_refs)


def gather_pieces(x_ref, piece_refs, groups):
    t = lax.axis_index("tensor")
    width = piece_refs[0].shape[1]
    for index, piece in enumerate(piece_refs):
        db, dt = divmod(index, groups)
        owner = lax.rem(t - dt + groups, groups)
        x_ref[db * CAP : (db + 1) * CAP, pl.ds(pl.multiple_of(owner * width, width), width)] = piece[...]


def scatter_pieces(y_ref, piece_refs, groups):
    t = lax.axis_index("tensor")
    blocks = len(piece_refs) // groups
    width = piece_refs[0].shape[1]
    for index, piece in enumerate(piece_refs):
        db, dt = divmod(index, groups)
        row = (-db) % blocks * CAP
        owner = lax.rem(t + dt, groups)
        piece[...] = y_ref[row : row + CAP, pl.ds(pl.multiple_of(owner * width, width), width)].astype(BF16)


def forward_kernel(groups, count, *refs):
    pieces, (gate_ref, up_ref, down_ref) = refs[:count], refs[count : count + 3]
    act_ref, scale_ref = refs[count + 3 : count + 5]
    outs, (x_ref, y_ref) = refs[count + 5 : 2 * count + 5], refs[2 * count + 5 :]
    step = pl.program_id(0)

    @pl.when(step == 0)
    def _():
        gather_pieces(x_ref, pieces, groups)
        y_ref[...] = jnp.zeros_like(y_ref)

    gate_pre = lax.dot_general(x_ref[...], gate_ref[0], CONTRACT_LAST, preferred_element_type=F32)
    up_pre = lax.dot_general(x_ref[...], up_ref[0], CONTRACT_LAST, preferred_element_type=F32)
    sig = jax.nn.sigmoid(gate_pre)
    act = gate_pre * sig
    hidden = (act * up_pre).astype(BF16)
    act_ref[...] = act
    scale_ref[...] = up_pre * (sig * (1.0 + gate_pre * (1.0 - sig)))
    y_ref[...] += jnp.dot(hidden, down_ref[0], preferred_element_type=F32)

    @pl.when(step == pl.num_programs(0) - 1)
    def _():
        scatter_pieces(y_ref, outs, groups)


def backward_kernel(groups, count, *refs):
    pieces, (gate_ref, up_ref, down_ref) = refs[:count], refs[count : count + 3]
    act_ref, scale_ref = refs[count + 3 : count + 5]
    outs, (x_ref, y_ref) = refs[count + 5 : 2 * count + 5], refs[2 * count + 5 :]
    step = pl.program_id(0)

    @pl.when(step == 0)
    def _():
        gather_pieces(x_ref, pieces, groups)
        y_ref[...] = jnp.zeros_like(y_ref)

    grad_hid = lax.dot_general(x_ref[...], down_ref[0], CONTRACT_LAST, preferred_element_type=F32)
    grad_gate = (grad_hid * scale_ref[...]).astype(BF16)
    grad_up = (grad_hid * act_ref[...]).astype(BF16)
    y_ref[...] += jnp.dot(grad_gate, gate_ref[0], preferred_element_type=F32) + jnp.dot(
        grad_up, up_ref[0], preferred_element_type=F32
    )

    @pl.when(step == pl.num_programs(0) - 1)
    def _():
        scatter_pieces(y_ref, outs, groups)


def add_blocks_kernel(groups, *refs):
    pieces, out_ref = refs[:-1], refs[-1]
    for dt in range(groups):
        total = pieces[dt][...].astype(F32)
        for piece in pieces[groups + dt :: groups]:
            total = total + piece[...].astype(F32)
        out_ref[dt * CAP : (dt + 1) * CAP, :] = total.astype(BF16)


def weights_kernel(groups, columns, routes_ref, gates_ref, key_ref, out_ref, gate_ref):
    experts, rows = key_ref.shape
    t, e = lax.axis_index("tensor"), lax.axis_index("expert")
    ids = lax.broadcasted_iota(jnp.int32, (experts, rows), 0)
    gate = jnp.zeros((experts, rows), F32)
    for r in range(routes_ref.shape[0]):
        gate = gate + jnp.where(routes_ref[r : r + 1, :] == ids, gates_ref[r : r + 1, :], 0.0)
    gate_ref[...] = gate
    slot = lax.broadcasted_iota(jnp.int32, (CAP, rows), 0).astype(F32)
    for dz in range(columns):
        blocks = []
        for dt in range(groups):
            expert = lax.rem(e - dz + columns, columns) * groups + lax.rem(t - dt + groups, groups)
            same = key_ref[pl.ds(expert, 1), :] == slot
            blocks.append(jnp.where(same, gate_ref[pl.ds(expert, 1), :], 0.0))
        width = groups * CAP
        out_ref[dz * width : (dz + 1) * width, :] = jnp.concatenate(blocks, axis=0).astype(BF16)


def combine_kernel(weight_ref, *refs):
    parts, out_ref, all_ref = refs[:-2], refs[-2], refs[-1]
    height = parts[0].shape[0]
    for index, part in enumerate(parts):
        all_ref[index * height : (index + 1) * height, :] = part[...]
    out_ref[...] = lax.dot_general(
        weight_ref[...], all_ref[...], (((0,), (0,)), ((), ())), preferred_element_type=F32
    ).astype(BF16)


def gate_grad_kernel(groups, columns, routes_ref, key_ref, grads_ref, *refs):
    parts, (out_ref, sum_ref) = refs[:-2], refs[-2:]
    rows = key_ref.shape[1]
    t, e = lax.axis_index("tensor"), lax.axis_index("expert")
    slot = lax.broadcasted_iota(jnp.int32, (CAP, rows), 0).astype(F32)
    routes = routes_ref[...]
    total = jnp.zeros(out_ref.shape, F32)
    for dz, part in enumerate(parts):
        sum_ref[...] = lax.dot_general(part[...], grads_ref[...], CONTRACT_LAST, preferred_element_type=F32)
        for dt in range(groups):
            expert = lax.rem(e - dz + columns, columns) * groups + lax.rem(t - dt + groups, groups)
            same = key_ref[pl.ds(expert, 1), :] == slot
            row = jnp.sum(jnp.where(same, sum_ref[dt * CAP : (dt + 1) * CAP, :], 0.0), axis=0, keepdims=True)
            total = total + jnp.where(routes == expert, row, 0.0)
    out_ref[...] = total


def body(sizes, tokens, grad_out, routes, gates, gate_weight, up_weight, down_weight):
    n_dp, groups, columns = sizes
    experts = groups * columns
    rows, width = tokens.shape
    _, hid_dev, feats = gate_weight.shape
    count = n_dp * groups
    tall = n_dp * CAP
    chunk = 256 if hid_dev % 256 == 0 else hid_dev
    routes_t, gates_t = routes.T, gates.T

    piece = jax.ShapeDtypeStruct((CAP, width), BF16)
    key, *tok_pieces = pl.pallas_call(
        number_kernel,
        out_shape=[jax.ShapeDtypeStruct((experts, rows), F32)] + [piece] * groups,
        in_specs=[vmem()] * 2,
        out_specs=[vmem()] * (groups + 1),
        cost_estimate=cost(2 * groups * CAP * rows * width, 2 * rows * width),
        name="number",
    )(routes_t, tokens)
    grad_pieces = pl.pallas_call(
        pick_kernel,
        out_shape=[piece] * groups,
        in_specs=[vmem()] * 2,
        out_specs=[vmem()] * groups,
        cost_estimate=cost(2 * groups * CAP * rows * width, 2 * rows * width),
        name="pick",
    )(key, grad_out)

    def shift(value, db, dt):
        if (db, dt) == (0, 0):
            return value
        pairs = []
        for b in range(n_dp):
            for t in range(groups):
                pairs.append((b * groups + t, (b + db) % n_dp * groups + (t + dt) % groups))
        return lax.ppermute(value, ("dp", "tensor"), pairs)

    def spread(pieces):
        return [shift(pieces[dt], db, dt) for db in range(n_dp) for dt in range(groups)]

    def exchange(pieces):
        return [shift(pieces[db * groups + dt], db, dt) for db in range(n_dp) for dt in range(groups)]

    def whole_block(shape):
        return pl.BlockSpec(shape, lambda i: (0,) * len(shape))

    weight_block = pl.BlockSpec((1, chunk, feats), lambda i: (0, i, 0))
    hidden_block = pl.BlockSpec((tall, chunk), lambda i: (0, i))
    piece_block = whole_block((CAP, width))
    scratch = [pltpu.VMEM((tall, feats), BF16), pltpu.VMEM((tall, feats), F32)]
    matmul_flops = 2 * tall * hid_dev * feats

    tok_in = spread(tok_pieces)
    grad_in = spread(grad_pieces)
    act, scale, *outs = pl.pallas_call(
        functools.partial(forward_kernel, groups, count),
        grid=(hid_dev // chunk,),
        out_shape=[
            jax.ShapeDtypeStruct((tall, hid_dev), F32),
            jax.ShapeDtypeStruct((tall, hid_dev), F32),
        ]
        + [piece] * count,
        in_specs=[piece_block] * count + [weight_block] * 3,
        out_specs=[hidden_block] * 2 + [piece_block] * count,
        scratch_shapes=scratch,
        cost_estimate=cost(3 * matmul_flops, 6 * hid_dev * feats),
        name="forward",
    )(*tok_in, gate_weight, up_weight, down_weight)
    out_in = exchange(outs)
    backs = pl.pallas_call(
        functools.partial(backward_kernel, groups, count),
        grid=(hid_dev // chunk,),
        out_shape=[piece] * count,
        in_specs=[piece_block] * count + [weight_block] * 3 + [hidden_block] * 2,
        out_specs=[piece_block] * count,
        scratch_shapes=scratch,
        cost_estimate=cost(3 * matmul_flops, 6 * hid_dev * feats),
        name="backward",
    )(*grad_in, gate_weight, up_weight, down_weight, act, scale)
    back_in = exchange(backs)

    weight_map = pl.pallas_call(
        functools.partial(weights_kernel, groups, columns),
        out_shape=jax.ShapeDtypeStruct((experts * CAP, rows), BF16),
        in_specs=[vmem()] * 3,
        out_specs=vmem(),
        scratch_shapes=[pltpu.VMEM((experts, rows), F32)],
        cost_estimate=cost(experts * CAP * rows, 2 * experts * CAP * rows),
        name="weights",
    )(routes_t, gates_t, key)

    def add_blocks(pieces):
        return pl.pallas_call(
            functools.partial(add_blocks_kernel, groups),
            out_shape=jax.ShapeDtypeStruct((groups * CAP, width), BF16),
            in_specs=[vmem()] * count,
            out_specs=vmem(),
            cost_estimate=cost(count * CAP * width, 4 * count * CAP * width),
            name="add_blocks",
        )(*pieces)

    def across(value):
        if columns != 4:
            return [value] + [
                lax.ppermute(value, "expert", [(z, (z + dz) % columns) for z in range(columns)])
                for dz in range(1, columns)
            ]
        far = lax.ppermute(value, "expert", [(z, (z + 2) % columns) for z in range(columns)])
        up = lax.ppermute(value, "expert", [(z, z + 1) for z in range(columns - 1)])
        down = lax.ppermute(value, "expert", [(z + 1, z) for z in range(columns - 1)])
        ends = lax.ppermute(far, "expert", [(2, 3), (1, 0)])
        e = lax.axis_index("expert")
        return [value, jnp.where(e == 0, ends, up), far, jnp.where(e == columns - 1, ends, down)]

    def combine(parts):
        return pl.pallas_call(
            combine_kernel,
            out_shape=jax.ShapeDtypeStruct((rows, width), BF16),
            in_specs=[vmem()] * (columns + 1),
            out_specs=vmem(),
            scratch_shapes=[pltpu.VMEM((experts * CAP, width), BF16)],
            cost_estimate=cost(2 * experts * CAP * rows * width, 2 * experts * CAP * (rows + width)),
            name="combine",
        )(weight_map, *parts)

    mixed_parts = across(add_blocks(out_in))
    back_parts = across(add_blocks(back_in))
    mixed = combine(mixed_parts)
    grad_tokens = combine(back_parts)

    gate_part = pl.pallas_call(
        functools.partial(gate_grad_kernel, groups, columns),
        out_shape=jax.ShapeDtypeStruct(routes_t.shape, F32),
        in_specs=[vmem()] * (columns + 3),
        out_specs=vmem(),
        scratch_shapes=[pltpu.VMEM((groups * CAP, rows), F32)],
        cost_estimate=cost(2 * experts * CAP * rows * width, 2 * experts * CAP * width),
        name="gate_grad",
    )(routes_t, key, grad_out, *mixed_parts)
    grad_gates = lax.psum(gate_part, "tensor")
    return (mixed, grad_tokens, grad_gates.T)


def solution(mesh):
    sizes = (mesh.shape["dp"], mesh.shape["tensor"], mesh.shape["expert"])
    return jax.shard_map(
        functools.partial(body, sizes),
        mesh=mesh,
        in_specs=(
            P("dp", "tensor"),
            P("dp", "tensor"),
            P("dp", None),
            P("dp", None),
            P(("expert", "tensor"), "dp", None),
            P(("expert", "tensor"), "dp", None),
            P(("expert", "tensor"), "dp", None),
        ),
        out_specs=(P("dp", "tensor"), P("dp", "tensor"), P("dp", None)),
        check_vma=False,
    )
```

```python
import functools

import jax
import jax.numpy as jnp
from jax import lax
from jax.experimental import pallas as pl
from jax.experimental.pallas import tpu as pltpu
from jax.sharding import PartitionSpec as P

CAP = 48
LANES = 128
MIB = 2**20
BF16 = jnp.bfloat16
F32 = jnp.float32
CONTRACT_LAST = (((1,), (1,)), ((), ()))


def call(kernel, name, out_shape, operands, flops, scratch=(), limit=8):
    outs = out_shape if isinstance(out_shape, list) else [out_shape]
    moved = sum(a.size * a.dtype.itemsize for a in [*operands, *outs])
    spec = pl.BlockSpec(memory_space=pltpu.VMEM)
    return pl.pallas_call(
        kernel,
        out_shape=out_shape,
        in_specs=[spec] * len(operands),
        out_specs=[spec] * len(outs) if isinstance(out_shape, list) else spec,
        scratch_shapes=list(scratch),
        compiler_params=pltpu.CompilerParams(vmem_limit_bytes=limit * MIB),
        cost_estimate=pl.CostEstimate(flops=int(flops), bytes_accessed=int(moved), transcendentals=0),
        name=name,
    )(*operands)


def number_kernel(routes_ref, key_ref):
    experts, rows = key_ref.shape
    ids = lax.broadcasted_iota(jnp.int32, (experts, rows), 0)
    hit = jnp.zeros((experts, rows), F32)
    for r in range(routes_ref.shape[0]):
        hit = hit + (routes_ref[r : r + 1, :] == ids).astype(F32)
    before = (
        lax.broadcasted_iota(jnp.int32, (LANES, LANES), 0) < lax.broadcasted_iota(jnp.int32, (LANES, LANES), 1)
    ).astype(BF16)
    offset = jnp.zeros((experts, 1), F32)
    for start in range(0, rows, LANES):
        part = hit[:, start : start + LANES]
        rank = jnp.dot(part.astype(BF16), before, preferred_element_type=F32) + offset
        offset = offset + jnp.sum(part, axis=1, keepdims=True)
        key_ref[:, start : start + LANES] = jnp.where(part > 0.0, rank, -1.0)


def position(cores):
    t = lax.axis_index("tensor")
    return lax.div(t, cores), lax.rem(t, cores), lax.axis_index("expert")


def pick_kernel(cores, key_ref, *refs):
    sources, pieces = refs[:cores], refs[cores:]
    chips = len(pieces)
    rows, width = sources[0].shape
    chip, core, e = position(cores)
    slot = lax.broadcasted_iota(jnp.int32, (CAP, rows), 0).astype(F32)
    masks = []
    for dh in range(chips):
        expert = (e * chips + lax.rem(chip + dh, chips)) * cores + core
        masks.append((key_ref[pl.ds(expert, 1), :] == slot).astype(BF16))
    mask = jnp.concatenate(masks, axis=0)
    for dc, source in enumerate(sources):
        picked = jnp.dot(mask, source[...], preferred_element_type=F32).astype(BF16)
        column = pl.multiple_of(lax.rem(core - dc + cores, cores) * width, width)
        for dh, piece in enumerate(pieces):
            piece[:, pl.ds(column, width)] = picked[dh * CAP : (dh + 1) * CAP]


def gather_pieces(x_ref, pieces, chips, cores):
    chip, _, _ = position(cores)
    width = pieces[0].shape[1]
    for index, piece in enumerate(pieces):
        db, dh = divmod(index, chips)
        column = pl.multiple_of(lax.rem(chip - dh + chips, chips) * width, width)
        x_ref[db * CAP : (db + 1) * CAP, pl.ds(column, width)] = piece[...]


def project_back(terms, pieces, chips, cores):
    chip, _, _ = position(cores)
    blocks = len(pieces) // chips
    width = pieces[0].shape[1]
    for dh in range(chips):
        column = pl.ds(pl.multiple_of(lax.rem(chip + dh, chips) * width, width), width)
        total = None
        for h_ref, w_ref in terms:
            term = jnp.dot(h_ref[...], w_ref[0, :, column], preferred_element_type=F32)
            total = term if total is None else total + term
        total = total.astype(BF16)
        for db in range(blocks):
            row = (-db) % blocks * CAP
            pieces[db * chips + dh][...] = total[row : row + CAP]


def chunks_of(hid_dev):
    size = 256 if hid_dev % 256 == 0 else hid_dev
    return [slice(start, start + size) for start in range(0, hid_dev, size)]


def forward_kernel(chips, cores, count, *refs):
    pieces, (gate_ref, up_ref, down_ref) = refs[:count], refs[count : count + 3]
    act_ref, scale_ref = refs[count + 3 : count + 5]
    outs, (x_ref, hid_ref) = refs[count + 5 : 2 * count + 5], refs[2 * count + 5 :]
    gather_pieces(x_ref, pieces, chips, cores)
    for part in chunks_of(gate_ref.shape[1]):
        gate_pre = lax.dot_general(x_ref[...], gate_ref[0, part, :], CONTRACT_LAST, preferred_element_type=F32)
        up_pre = lax.dot_general(x_ref[...], up_ref[0, part, :], CONTRACT_LAST, preferred_element_type=F32)
        sig = jax.nn.sigmoid(gate_pre)
        act = gate_pre * sig
        hid_ref[:, part] = (act * up_pre).astype(BF16)
        act_ref[:, part] = act
        scale_ref[:, part] = up_pre * (sig * (1.0 + gate_pre * (1.0 - sig)))
    project_back([(hid_ref, down_ref)], outs, chips, cores)


def backward_kernel(chips, cores, count, *refs):
    pieces, (gate_ref, up_ref, down_ref) = refs[:count], refs[count : count + 3]
    act_ref, scale_ref = refs[count + 3 : count + 5]
    outs, (x_ref, grad_gate_ref, grad_up_ref) = refs[count + 5 : 2 * count + 5], refs[2 * count + 5 :]
    gather_pieces(x_ref, pieces, chips, cores)
    for part in chunks_of(gate_ref.shape[1]):
        grad_hid = lax.dot_general(x_ref[...], down_ref[0, part, :], CONTRACT_LAST, preferred_element_type=F32)
        grad_gate_ref[:, part] = (grad_hid * scale_ref[:, part]).astype(BF16)
        grad_up_ref[:, part] = (grad_hid * act_ref[:, part]).astype(BF16)
    project_back([(grad_gate_ref, gate_ref), (grad_up_ref, up_ref)], outs, chips, cores)


def add_blocks_kernel(chips, cores, *refs):
    pieces, out_ref = refs[:-1], refs[-1]
    width = out_ref.shape[1]
    count = len(pieces) // cores
    _, core, _ = position(cores)
    column = pl.ds(pl.multiple_of(core * width, width), width)
    for dh in range(chips):
        for dc in range(cores):
            total = None
            for piece in pieces[dc * count + dh : (dc + 1) * count : chips]:
                term = piece[:, column].astype(F32)
                total = term if total is None else total + term
            row = (dh * cores + dc) * CAP
            out_ref[row : row + CAP, :] = total.astype(BF16)


def slot_experts(chips, cores, columns):
    chip, core, e = position(cores)
    experts = []
    for dz in range(columns):
        for dh in range(chips):
            for dc in range(cores):
                column = lax.rem(e - dz + columns, columns)
                owner = lax.rem(chip - dh + chips, chips)
                experts.append((column * chips + owner) * cores + lax.rem(core - dc + cores, cores))
    return experts


def weights_kernel(chips, cores, columns, routes_ref, gates_ref, key_ref, out_ref, gate_ref, all_ref):
    experts, rows = key_ref.shape
    ids = lax.broadcasted_iota(jnp.int32, (experts, rows), 0)
    gate = jnp.zeros((experts, rows), F32)
    for r in range(routes_ref.shape[0]):
        gate = gate + jnp.where(routes_ref[r : r + 1, :] == ids, gates_ref[r : r + 1, :], 0.0)
    gate_ref[...] = gate
    slot = lax.broadcasted_iota(jnp.int32, (CAP, rows), 0).astype(F32)
    for index, expert in enumerate(slot_experts(chips, cores, columns)):
        same = key_ref[pl.ds(expert, 1), :] == slot
        all_ref[index * CAP : (index + 1) * CAP, :] = jnp.where(same, gate_ref[pl.ds(expert, 1), :], 0.0)
    slots = all_ref.shape[0]
    step = LANES if slots % LANES == 0 else slots
    for start in range(0, slots, step):
        out_ref[:, start : start + step] = all_ref[start : start + step, :].T.astype(BF16)


def place_parts(parts, all_ref, columns):
    height = parts[0].shape[0]
    if len(parts) == columns:
        for index, part in enumerate(parts):
            all_ref[index * height : (index + 1) * height, :] = part[...]
        return
    own, far, up, down, ends = parts
    e = lax.axis_index("expert")
    all_ref[0:height, :] = own[...]
    all_ref[2 * height : 3 * height, :] = far[...]
    all_ref[height : 2 * height, :] = jnp.where(e == 0, ends[...], up[...])
    all_ref[3 * height : 4 * height, :] = jnp.where(e == columns - 1, ends[...], down[...])


def combine_kernel(columns, weight_ref, *refs):
    parts, (out_ref, all_ref) = refs[:-2], refs[-2:]
    place_parts(parts, all_ref, columns)
    out_ref[...] = jnp.dot(weight_ref[...], all_ref[...], preferred_element_type=F32).astype(BF16)


def combine_gate_kernel(chips, cores, columns, weight_ref, routes_ref, key_ref, grads_ref, *refs):
    parts, (out_ref, gate_ref, all_ref, sum_ref) = refs[:-4], refs[-4:]
    place_parts(parts, all_ref, columns)
    out_ref[...] = jnp.dot(weight_ref[...], all_ref[...], preferred_element_type=F32).astype(BF16)
    rows = key_ref.shape[1]
    slot = lax.broadcasted_iota(jnp.int32, (CAP, rows), 0).astype(F32)
    routes = routes_ref[...]
    sum_ref[...] = lax.dot_general(all_ref[...], grads_ref[...], CONTRACT_LAST, preferred_element_type=F32)
    total = jnp.zeros(gate_ref.shape, F32)
    for index, expert in enumerate(slot_experts(chips, cores, columns)):
        same = key_ref[pl.ds(expert, 1), :] == slot
        row = jnp.where(same, sum_ref[index * CAP : (index + 1) * CAP, :], 0.0)
        total = total + jnp.where(routes == expert, jnp.sum(row, axis=0, keepdims=True), 0.0)
    gate_ref[...] = total


def body(sizes, tokens, grad_out, routes, gates, gate_weight, up_weight, down_weight):
    n_dp, groups, columns = sizes
    cores = 2 if groups % 2 == 0 else 1
    chips = groups // cores
    experts = groups * columns
    rows, width = tokens.shape
    _, hid_dev, feats = gate_weight.shape
    count = n_dp * chips
    tall = n_dp * CAP
    slots = groups * CAP
    routes_t, gates_t = routes.T, gates.T

    def shape(height, length, dtype=BF16):
        return jax.ShapeDtypeStruct((height, length), dtype)

    def to_core(value, dc):
        if dc == 0:
            return value
        pairs = [(t, t // cores * cores + (t + dc) % cores) for t in range(groups)]
        return lax.ppermute(value, "tensor", pairs)

    def to_chip(value, db, dh):
        if (db, dh) == (0, 0):
            return value
        pairs = []
        for b in range(n_dp):
            for t in range(groups):
                target = (t // cores + dh) % chips * cores + t % cores
                pairs.append((b * groups + t, (b + db) % n_dp * groups + target))
        return lax.ppermute(value, ("dp", "tensor"), pairs)

    hops = [(db, dh) for db in range(n_dp) for dh in range(chips)]
    order = sorted(range(count), key=lambda index: (hops[index][0] == 0, -hops[index][1]))

    def dispatch(key, sources):
        pieces = call(
            functools.partial(pick_kernel, cores),
            "pick",
            [shape(CAP, cores * width)] * chips,
            [key, *sources],
            2 * slots * rows * width,
        )
        arrived = {index: to_chip(pieces[hops[index][1]], *hops[index]) for index in order}
        return [arrived[index] for index in range(count)]

    def give_back(pieces):
        arrived = {index: to_chip(pieces[index], *hops[index]) for index in order}
        pairs = [[to_core(arrived[index], dc) for index in range(count)] for dc in range(cores)]
        return call(
            functools.partial(add_blocks_kernel, chips, cores),
            "add_blocks",
            shape(slots, width),
            sum(pairs, []),
            2 * slots * width,
        )

    token_sources = [to_core(tokens, dc) for dc in range(cores)]
    grad_sources = [to_core(grad_out, dc) for dc in range(cores)]
    key = call(number_kernel, "number", shape(experts, rows, F32), [routes_t], experts * rows * LANES)
    tok_in = dispatch(key, token_sources)
    grad_in = dispatch(key, grad_sources)

    matmul_flops = 2 * tall * hid_dev * feats
    saved = [shape(tall, hid_dev, F32)] * 2
    piece = [shape(CAP, cores * width)] * count
    act, scale, *outs = call(
        functools.partial(forward_kernel, chips, cores, count),
        "forward",
        saved + piece,
        [*tok_in, gate_weight, up_weight, down_weight],
        3 * matmul_flops,
        [pltpu.VMEM((tall, feats), BF16), pltpu.VMEM((tall, hid_dev), BF16)],
        limit=24,
    )
    out_rows = give_back(outs)
    backs = call(
        functools.partial(backward_kernel, chips, cores, count),
        "backward",
        piece,
        [*grad_in, gate_weight, up_weight, down_weight, act, scale],
        3 * matmul_flops,
        [pltpu.VMEM((tall, feats), BF16)] + [pltpu.VMEM((tall, hid_dev), BF16)] * 2,
        limit=24,
    )
    back_rows = give_back(backs)

    weight_map = call(
        functools.partial(weights_kernel, chips, cores, columns),
        "weights",
        shape(rows, experts * CAP),
        [routes_t, gates_t, key],
        experts * CAP * rows,
        [pltpu.VMEM((experts, rows), F32), pltpu.VMEM((experts * CAP, rows), F32)],
        limit=16,
    )

    def across(value):
        if columns != 4:
            return [value] + [
                lax.ppermute(value, "expert", [(z, (z + dz) % columns) for z in range(columns)])
                for dz in range(1, columns)
            ]
        far = lax.ppermute(value, "expert", [(z, (z + 2) % columns) for z in range(columns)])
        up = lax.ppermute(value, "expert", [(z, z + 1) for z in range(columns - 1)])
        down = lax.ppermute(value, "expert", [(z + 1, z) for z in range(columns - 1)])
        ends = lax.ppermute(far, "expert", [(2, 3), (1, 0)])
        return [value, far, up, down, ends]

    out_parts = across(out_rows)
    back_parts = across(back_rows)
    combine_flops = 2 * experts * CAP * rows * width
    all_rows = pltpu.VMEM((experts * CAP, width), BF16)
    mixed, gate_part = call(
        functools.partial(combine_gate_kernel, chips, cores, columns),
        "combine_gate",
        [shape(rows, width), shape(routes_t.shape[0], rows, F32)],
        [weight_map, routes_t, key, grad_out, *out_parts],
        2 * combine_flops,
        [all_rows, pltpu.VMEM((experts * CAP, rows), F32)],
        limit=24,
    )
    for dc in range(1, cores):
        gate_part = gate_part + to_core(gate_part, dc)
    total = gate_part
    for dh in range(1, chips):
        total = total + to_chip(gate_part, 0, dh)
    grad_tokens = call(
        functools.partial(combine_kernel, columns),
        "combine",
        shape(rows, width),
        [weight_map, *back_parts],
        combine_flops,
        [all_rows],
        limit=16,
    )
    return (mixed, grad_tokens, total.T)


def solution(mesh):
    sizes = (mesh.shape["dp"], mesh.shape["tensor"], mesh.shape["expert"])
    return jax.shard_map(
        functools.partial(body, sizes),
        mesh=mesh,
        in_specs=(
            P("dp", "tensor"),
            P("dp", "tensor"),
            P("dp", None),
            P("dp", None),
            P(("expert", "tensor"), "dp", None),
            P(("expert", "tensor"), "dp", None),
            P(("expert", "tensor"), "dp", None),
        ),
        out_specs=(P("dp", "tensor"), P("dp", "tensor"), P("dp", None)),
        check_vma=False,
    )
```

```python
import functools

import jax
import jax.numpy as jnp
from jax import lax
from jax.experimental import pallas as pl
from jax.experimental.pallas import tpu as pltpu
from jax.sharding import PartitionSpec as P

CAP = 48
LANES = 128
MIB = 2**20
EARLY = 6e9
BF16 = jnp.bfloat16
F32 = jnp.float32
CONTRACT_LAST = (((1,), (1,)), ((), ()))


def call(kernel, name, out_shape, operands, flops, scratch=(), limit=8):
    outs = out_shape if isinstance(out_shape, list) else [out_shape]
    moved = sum(a.size * a.dtype.itemsize for a in [*operands, *outs])
    spec = pl.BlockSpec(memory_space=pltpu.VMEM)
    return pl.pallas_call(
        kernel,
        out_shape=out_shape,
        in_specs=[spec] * len(operands),
        out_specs=[spec] * len(outs) if isinstance(out_shape, list) else spec,
        scratch_shapes=list(scratch),
        compiler_params=pltpu.CompilerParams(vmem_limit_bytes=limit * MIB),
        cost_estimate=pl.CostEstimate(flops=int(flops), bytes_accessed=int(moved), transcendentals=0),
        name=name,
    )(*operands)


def number_kernel(routes_ref, key_ref):
    experts, rows = key_ref.shape
    ids = lax.broadcasted_iota(jnp.int32, (experts, rows), 0)
    hit = jnp.zeros((experts, rows), F32)
    for r in range(routes_ref.shape[0]):
        hit = hit + (routes_ref[r : r + 1, :] == ids).astype(F32)
    before = (
        lax.broadcasted_iota(jnp.int32, (LANES, LANES), 0) < lax.broadcasted_iota(jnp.int32, (LANES, LANES), 1)
    ).astype(BF16)
    offset = jnp.zeros((experts, 1), F32)
    for start in range(0, rows, LANES):
        part = hit[:, start : start + LANES]
        rank = jnp.dot(part.astype(BF16), before, preferred_element_type=F32) + offset
        offset = offset + jnp.sum(part, axis=1, keepdims=True)
        key_ref[:, start : start + LANES] = jnp.where(part > 0.0, rank, -1.0)


def position(cores):
    t = lax.axis_index("tensor")
    return lax.div(t, cores), lax.rem(t, cores), lax.axis_index("expert")


def pick_kernel(cores, key_ref, *refs):
    sources, pieces = refs[:cores], refs[cores:]
    chips = len(pieces)
    rows, width = sources[0].shape
    chip, core, e = position(cores)
    slot = lax.broadcasted_iota(jnp.int32, (CAP, rows), 0).astype(F32)
    masks = []
    for dh in range(chips):
        expert = (e * chips + lax.rem(chip + dh, chips)) * cores + core
        masks.append((key_ref[pl.ds(expert, 1), :] == slot).astype(BF16))
    mask = jnp.concatenate(masks, axis=0)
    for dc, source in enumerate(sources):
        picked = jnp.dot(mask, source[...], preferred_element_type=F32).astype(BF16)
        column = pl.multiple_of(lax.rem(core - dc + cores, cores) * width, width)
        for dh, piece in enumerate(pieces):
            piece[:, pl.ds(column, width)] = picked[dh * CAP : (dh + 1) * CAP]


def gather_pieces(x_ref, pieces, chips, cores):
    chip, _, _ = position(cores)
    width = pieces[0].shape[1]
    for index, piece in enumerate(pieces):
        db, dh = divmod(index, chips)
        column = pl.multiple_of(lax.rem(chip - dh + chips, chips) * width, width)
        x_ref[db * CAP : (db + 1) * CAP, pl.ds(column, width)] = piece[...]


def project_back(terms, pieces, chips, cores):
    chip, _, _ = position(cores)
    blocks = len(pieces) // chips
    width = pieces[0].shape[1]
    for dh in range(chips):
        column = pl.ds(pl.multiple_of(lax.rem(chip + dh, chips) * width, width), width)
        total = None
        for h_ref, w_ref in terms:
            term = jnp.dot(h_ref[...], w_ref[0, :, column], preferred_element_type=F32)
            total = term if total is None else total + term
        total = total.astype(BF16)
        for db in range(blocks):
            row = (-db) % blocks * CAP
            pieces[db * chips + dh][...] = total[row : row + CAP]


def chunks_of(hid_dev):
    size = 256 if hid_dev % 256 == 0 else hid_dev
    return [slice(start, start + size) for start in range(0, hid_dev, size)]


def forward_kernel(chips, cores, count, *refs):
    pieces, (gate_ref, up_ref, down_ref) = refs[:count], refs[count : count + 3]
    act_ref, scale_ref = refs[count + 3 : count + 5]
    outs, (x_ref, hid_ref) = refs[count + 5 : 2 * count + 5], refs[2 * count + 5 :]
    gather_pieces(x_ref, pieces, chips, cores)
    for part in chunks_of(gate_ref.shape[1]):
        gate_pre = lax.dot_general(x_ref[...], gate_ref[0, part, :], CONTRACT_LAST, preferred_element_type=F32)
        up_pre = lax.dot_general(x_ref[...], up_ref[0, part, :], CONTRACT_LAST, preferred_element_type=F32)
        sig = jax.nn.sigmoid(gate_pre)
        act = gate_pre * sig
        hid_ref[:, part] = (act * up_pre).astype(BF16)
        act_ref[:, part] = act
        scale_ref[:, part] = up_pre * (sig * (1.0 + gate_pre * (1.0 - sig)))
    project_back([(hid_ref, down_ref)], outs, chips, cores)


def backward_kernel(chips, cores, count, *refs):
    pieces, (gate_ref, up_ref, down_ref) = refs[:count], refs[count : count + 3]
    act_ref, scale_ref = refs[count + 3 : count + 5]
    outs, (x_ref, grad_gate_ref, grad_up_ref) = refs[count + 5 : 2 * count + 5], refs[2 * count + 5 :]
    gather_pieces(x_ref, pieces, chips, cores)
    for part in chunks_of(gate_ref.shape[1]):
        grad_hid = lax.dot_general(x_ref[...], down_ref[0, part, :], CONTRACT_LAST, preferred_element_type=F32)
        grad_gate_ref[:, part] = (grad_hid * scale_ref[:, part]).astype(BF16)
        grad_up_ref[:, part] = (grad_hid * act_ref[:, part]).astype(BF16)
    project_back([(grad_gate_ref, gate_ref), (grad_up_ref, up_ref)], outs, chips, cores)


def add_blocks_kernel(chips, cores, *refs):
    pieces, out_ref = refs[:-1], refs[-1]
    width = out_ref.shape[1]
    count = len(pieces) // cores
    _, core, _ = position(cores)
    column = pl.ds(pl.multiple_of(core * width, width), width)
    for dh in range(chips):
        for dc in range(cores):
            total = None
            for piece in pieces[dc * count + dh : (dc + 1) * count : chips]:
                term = piece[:, column].astype(F32)
                total = term if total is None else total + term
            row = (dh * cores + dc) * CAP
            out_ref[row : row + CAP, :] = total.astype(BF16)


def slot_experts(chips, cores, columns):
    chip, core, e = position(cores)
    experts = []
    for dz in range(columns):
        for dh in range(chips):
            for dc in range(cores):
                column = lax.rem(e - dz + columns, columns)
                owner = lax.rem(chip - dh + chips, chips)
                experts.append((column * chips + owner) * cores + lax.rem(core - dc + cores, cores))
    return experts


def weights_kernel(chips, cores, columns, routes_ref, gates_ref, key_ref, out_ref, gate_ref, all_ref):
    experts, rows = key_ref.shape
    ids = lax.broadcasted_iota(jnp.int32, (experts, rows), 0)
    gate = jnp.zeros((experts, rows), F32)
    for r in range(routes_ref.shape[0]):
        gate = gate + jnp.where(routes_ref[r : r + 1, :] == ids, gates_ref[r : r + 1, :], 0.0)
    gate_ref[...] = gate
    slot = lax.broadcasted_iota(jnp.int32, (CAP, rows), 0).astype(F32)
    for index, expert in enumerate(slot_experts(chips, cores, columns)):
        same = key_ref[pl.ds(expert, 1), :] == slot
        all_ref[index * CAP : (index + 1) * CAP, :] = jnp.where(same, gate_ref[pl.ds(expert, 1), :], 0.0)
    slots = all_ref.shape[0]
    step = LANES if slots % LANES == 0 else slots
    for start in range(0, slots, step):
        out_ref[:, start : start + step] = all_ref[start : start + step, :].T.astype(BF16)


def place_parts(parts, all_ref, columns):
    height = parts[0].shape[0]
    if len(parts) == columns:
        for index, part in enumerate(parts):
            all_ref[index * height : (index + 1) * height, :] = part[...]
        return
    own, far, up, down, ends = parts
    e = lax.axis_index("expert")
    all_ref[0:height, :] = own[...]
    all_ref[2 * height : 3 * height, :] = far[...]
    all_ref[height : 2 * height, :] = jnp.where(e == 0, ends[...], up[...])
    all_ref[3 * height : 4 * height, :] = jnp.where(e == columns - 1, ends[...], down[...])


def combine_kernel(columns, weight_ref, *refs):
    parts, (out_ref, all_ref) = refs[:-2], refs[-2:]
    place_parts(parts, all_ref, columns)
    out_ref[...] = jnp.dot(weight_ref[...], all_ref[...], preferred_element_type=F32).astype(BF16)


def combine_gate_kernel(chips, cores, columns, weight_ref, routes_ref, key_ref, grads_ref, *refs):
    parts, (out_ref, gate_ref, all_ref, sum_ref) = refs[:-4], refs[-4:]
    place_parts(parts, all_ref, columns)
    out_ref[...] = jnp.dot(weight_ref[...], all_ref[...], preferred_element_type=F32).astype(BF16)
    rows = key_ref.shape[1]
    slot = lax.broadcasted_iota(jnp.int32, (CAP, rows), 0).astype(F32)
    routes = routes_ref[...]
    sum_ref[...] = lax.dot_general(all_ref[...], grads_ref[...], CONTRACT_LAST, preferred_element_type=F32)
    total = jnp.zeros(gate_ref.shape, F32)
    for index, expert in enumerate(slot_experts(chips, cores, columns)):
        same = key_ref[pl.ds(expert, 1), :] == slot
        row = jnp.where(same, sum_ref[index * CAP : (index + 1) * CAP, :], 0.0)
        total = total + jnp.where(routes == expert, jnp.sum(row, axis=0, keepdims=True), 0.0)
    gate_ref[...] = total


def body(sizes, tokens, grad_out, routes, gates, gate_weight, up_weight, down_weight):
    n_dp, groups, columns = sizes
    cores = 2 if groups % 2 == 0 else 1
    chips = groups // cores
    experts = groups * columns
    rows, width = tokens.shape
    _, hid_dev, feats = gate_weight.shape
    count = n_dp * chips
    tall = n_dp * CAP
    slots = groups * CAP
    routes_t, gates_t = routes.T, gates.T

    def shape(height, length, dtype=BF16):
        return jax.ShapeDtypeStruct((height, length), dtype)

    def to_core(value, dc):
        if dc == 0:
            return value
        pairs = [(t, t // cores * cores + (t + dc) % cores) for t in range(groups)]
        return lax.ppermute(value, "tensor", pairs)

    def to_chip(value, db, dh):
        if (db, dh) == (0, 0):
            return value
        pairs = []
        for b in range(n_dp):
            for t in range(groups):
                target = (t // cores + dh) % chips * cores + t % cores
                pairs.append((b * groups + t, (b + db) % n_dp * groups + target))
        return lax.ppermute(value, ("dp", "tensor"), pairs)

    hops = [(db, dh) for db in range(n_dp) for dh in range(chips)]
    order = sorted(range(count), key=lambda index: (hops[index][0] == 0, -hops[index][1]))

    def dispatch(key, sources):
        pieces = call(
            functools.partial(pick_kernel, cores),
            "pick",
            [shape(CAP, cores * width)] * chips,
            [key, *sources],
            EARLY,
        )
        arrived = {index: to_chip(pieces[hops[index][1]], *hops[index]) for index in order}
        return [arrived[index] for index in range(count)]

    def give_back(pieces):
        arrived = {index: to_chip(pieces[index], *hops[index]) for index in order}
        pairs = [[to_core(arrived[index], dc) for index in range(count)] for dc in range(cores)]
        return call(
            functools.partial(add_blocks_kernel, chips, cores),
            "add_blocks",
            shape(slots, width),
            sum(pairs, []),
            2 * slots * width,
        )

    def across(value):
        if columns != 4:
            return [value] + [
                lax.ppermute(value, "expert", [(z, (z + dz) % columns) for z in range(columns)])
                for dz in range(1, columns)
            ]
        far = lax.ppermute(value, "expert", [(z, (z + 2) % columns) for z in range(columns)])
        up = lax.ppermute(value, "expert", [(z, z + 1) for z in range(columns - 1)])
        down = lax.ppermute(value, "expert", [(z + 1, z) for z in range(columns - 1)])
        ends = lax.ppermute(far, "expert", [(2, 3), (1, 0)])
        return [value, far, up, down, ends]

    token_sources = [to_core(tokens, dc) for dc in range(cores)]
    grad_sources = [to_core(grad_out, dc) for dc in range(cores)]
    key = call(number_kernel, "number", shape(experts, rows, F32), [routes_t], EARLY)
    tok_in = dispatch(key, token_sources)
    grad_in = dispatch(key, grad_sources)

    matmul_flops = 2 * tall * hid_dev * feats
    saved = [shape(tall, hid_dev, F32)] * 2
    piece = [shape(CAP, cores * width)] * count
    act, scale, *outs = call(
        functools.partial(forward_kernel, chips, cores, count),
        "forward",
        saved + piece,
        [*tok_in, gate_weight, up_weight, down_weight],
        3 * matmul_flops,
        [pltpu.VMEM((tall, feats), BF16), pltpu.VMEM((tall, hid_dev), BF16)],
        limit=24,
    )
    out_rows = give_back(outs)
    backs = call(
        functools.partial(backward_kernel, chips, cores, count),
        "backward",
        piece,
        [*grad_in, gate_weight, up_weight, down_weight, act, scale],
        3 * matmul_flops,
        [pltpu.VMEM((tall, feats), BF16)] + [pltpu.VMEM((tall, hid_dev), BF16)] * 2,
        limit=24,
    )
    out_parts = across(out_rows)
    out_parts[1], backs = lax.optimization_barrier((out_parts[1], backs))
    back_rows = give_back(backs)

    weight_map = call(
        functools.partial(weights_kernel, chips, cores, columns),
        "weights",
        shape(rows, experts * CAP),
        [routes_t, gates_t, key],
        experts * CAP * rows,
        [pltpu.VMEM((experts, rows), F32), pltpu.VMEM((experts * CAP, rows), F32)],
        limit=16,
    )

    back_parts = across(back_rows)
    combine_flops = 2 * experts * CAP * rows * width
    all_rows = pltpu.VMEM((experts * CAP, width), BF16)
    mixed, gate_part = call(
        functools.partial(combine_gate_kernel, chips, cores, columns),
        "combine_gate",
        [shape(rows, width), shape(routes_t.shape[0], rows, F32)],
        [weight_map, routes_t, key, grad_out, *out_parts],
        2 * combine_flops,
        [all_rows, pltpu.VMEM((experts * CAP, rows), F32)],
        limit=24,
    )
    for dc in range(1, cores):
        gate_part = gate_part + to_core(gate_part, dc)
    total = gate_part
    for dh in range(1, chips):
        total = total + to_chip(gate_part, 0, dh)
    grad_tokens = call(
        functools.partial(combine_kernel, columns),
        "combine",
        shape(rows, width),
        [weight_map, *back_parts],
        combine_flops,
        [all_rows],
        limit=16,
    )
    return (mixed, grad_tokens, total.T)


def solution(mesh):
    sizes = (mesh.shape["dp"], mesh.shape["tensor"], mesh.shape["expert"])
    return jax.shard_map(
        functools.partial(body, sizes),
        mesh=mesh,
        in_specs=(
            P("dp", "tensor"),
            P("dp", "tensor"),
            P("dp", None),
            P("dp", None),
            P(("expert", "tensor"), "dp", None),
            P(("expert", "tensor"), "dp", None),
            P(("expert", "tensor"), "dp", None),
        ),
        out_specs=(P("dp", "tensor"), P("dp", "tensor"), P("dp", None)),
        check_vma=False,
    )
```

```python
import functools

import jax
import jax.numpy as jnp
from jax import lax
from jax.experimental import pallas as pl
from jax.experimental.pallas import tpu as pltpu
from jax.sharding import PartitionSpec as P

CAP = 48
LANES = 128
MIB = 2**20
EARLY = 6e9
BF16 = jnp.bfloat16
F32 = jnp.float32
CONTRACT_LAST = (((1,), (1,)), ((), ()))


def call(kernel, name, out_shape, operands, flops, scratch=(), limit=8):
    outs = out_shape if isinstance(out_shape, list) else [out_shape]
    moved = sum(a.size * a.dtype.itemsize for a in [*operands, *outs])
    spec = pl.BlockSpec(memory_space=pltpu.VMEM)
    return pl.pallas_call(
        kernel,
        out_shape=out_shape,
        in_specs=[spec] * len(operands),
        out_specs=[spec] * len(outs) if isinstance(out_shape, list) else spec,
        scratch_shapes=list(scratch),
        compiler_params=pltpu.CompilerParams(vmem_limit_bytes=limit * MIB),
        cost_estimate=pl.CostEstimate(flops=int(flops), bytes_accessed=int(moved), transcendentals=0),
        name=name,
    )(*operands)


def number_kernel(routes_ref, key_ref):
    experts, rows = key_ref.shape
    ids = lax.broadcasted_iota(jnp.int32, (experts, rows), 0)
    hit = jnp.zeros((experts, rows), F32)
    for r in range(routes_ref.shape[0]):
        hit = hit + (routes_ref[r : r + 1, :] == ids).astype(F32)
    before = (
        lax.broadcasted_iota(jnp.int32, (LANES, LANES), 0) < lax.broadcasted_iota(jnp.int32, (LANES, LANES), 1)
    ).astype(BF16)
    offset = jnp.zeros((experts, 1), F32)
    for start in range(0, rows, LANES):
        part = hit[:, start : start + LANES]
        rank = jnp.dot(part.astype(BF16), before, preferred_element_type=F32) + offset
        offset = offset + jnp.sum(part, axis=1, keepdims=True)
        key_ref[:, start : start + LANES] = jnp.where(part > 0.0, rank, -1.0)


def position(cores):
    t = lax.axis_index("tensor")
    return lax.div(t, cores), lax.rem(t, cores), lax.axis_index("expert")


def pick_kernel(cores, key_ref, *refs):
    sources, pieces = refs[:cores], refs[cores:]
    chips = len(pieces)
    rows, width = sources[0].shape
    chip, core, e = position(cores)
    slot = lax.broadcasted_iota(jnp.int32, (CAP, rows), 0).astype(F32)
    masks = []
    for dh in range(chips):
        expert = (e * chips + lax.rem(chip + dh, chips)) * cores + core
        masks.append((key_ref[pl.ds(expert, 1), :] == slot).astype(BF16))
    mask = jnp.concatenate(masks, axis=0)
    for dc, source in enumerate(sources):
        picked = jnp.dot(mask, source[...], preferred_element_type=F32).astype(BF16)
        column = pl.multiple_of(lax.rem(core - dc + cores, cores) * width, width)
        for dh, piece in enumerate(pieces):
            piece[:, pl.ds(column, width)] = picked[dh * CAP : (dh + 1) * CAP]


def gather_pieces(x_ref, pieces, chips, cores):
    chip, _, _ = position(cores)
    width = pieces[0].shape[1]
    for index, piece in enumerate(pieces):
        db, dh = divmod(index, chips)
        column = pl.multiple_of(lax.rem(chip - dh + chips, chips) * width, width)
        x_ref[db * CAP : (db + 1) * CAP, pl.ds(column, width)] = piece[...]


def project_back(terms, pieces, chips, cores):
    chip, _, _ = position(cores)
    blocks = len(pieces) // chips
    width = pieces[0].shape[1]
    for dh in range(chips):
        column = pl.ds(pl.multiple_of(lax.rem(chip + dh, chips) * width, width), width)
        total = None
        for h_ref, w_ref in terms:
            term = jnp.dot(h_ref[...], w_ref[0, :, column], preferred_element_type=F32)
            total = term if total is None else total + term
        total = total.astype(BF16)
        for db in range(blocks):
            row = (-db) % blocks * CAP
            pieces[db * chips + dh][...] = total[row : row + CAP]


def chunks_of(hid_dev):
    size = 256 if hid_dev % 256 == 0 else hid_dev
    return [slice(start, start + size) for start in range(0, hid_dev, size)]


def forward_kernel(chips, cores, count, *refs):
    pieces, (gate_ref, up_ref, down_ref) = refs[:count], refs[count : count + 3]
    act_ref, scale_ref = refs[count + 3 : count + 5]
    outs, (x_ref, hid_ref) = refs[count + 5 : 2 * count + 5], refs[2 * count + 5 :]
    gather_pieces(x_ref, pieces, chips, cores)
    for part in chunks_of(gate_ref.shape[1]):
        gate_pre = lax.dot_general(x_ref[...], gate_ref[0, part, :], CONTRACT_LAST, preferred_element_type=F32)
        up_pre = lax.dot_general(x_ref[...], up_ref[0, part, :], CONTRACT_LAST, preferred_element_type=F32)
        sig = jax.nn.sigmoid(gate_pre)
        act = gate_pre * sig
        hid_ref[:, part] = (act * up_pre).astype(BF16)
        act_ref[:, part] = act
        scale_ref[:, part] = up_pre * (sig * (1.0 + gate_pre * (1.0 - sig)))
    project_back([(hid_ref, down_ref)], outs, chips, cores)


def backward_kernel(chips, cores, count, *refs):
    pieces, (gate_ref, up_ref, down_ref) = refs[:count], refs[count : count + 3]
    act_ref, scale_ref = refs[count + 3 : count + 5]
    outs, (x_ref, grad_gate_ref, grad_up_ref) = refs[count + 5 : 2 * count + 5], refs[2 * count + 5 :]
    gather_pieces(x_ref, pieces, chips, cores)
    for part in chunks_of(gate_ref.shape[1]):
        grad_hid = lax.dot_general(x_ref[...], down_ref[0, part, :], CONTRACT_LAST, preferred_element_type=F32)
        grad_gate_ref[:, part] = (grad_hid * scale_ref[:, part]).astype(BF16)
        grad_up_ref[:, part] = (grad_hid * act_ref[:, part]).astype(BF16)
    project_back([(grad_gate_ref, gate_ref), (grad_up_ref, up_ref)], outs, chips, cores)


def add_blocks_kernel(chips, cores, *refs):
    pieces, out_ref = refs[:-1], refs[-1]
    width = out_ref.shape[1]
    count = len(pieces) // cores
    _, core, _ = position(cores)
    column = pl.ds(pl.multiple_of(core * width, width), width)
    for dh in range(chips):
        for dc in range(cores):
            total = None
            for piece in pieces[dc * count + dh : (dc + 1) * count : chips]:
                term = piece[:, column].astype(F32)
                total = term if total is None else total + term
            row = (dh * cores + dc) * CAP
            out_ref[row : row + CAP, :] = total.astype(BF16)


def slot_experts(chips, cores, columns):
    chip, core, _ = position(cores)
    experts = []
    for dz in range(columns):
        for dh in range(chips):
            for dc in range(cores):
                owner = lax.rem(chip - dh + chips, chips)
                experts.append((dz * chips + owner) * cores + lax.rem(core - dc + cores, cores))
    return experts


def weights_kernel(chips, cores, columns, routes_ref, gates_ref, key_ref, out_ref, gate_ref, all_ref):
    experts, rows = key_ref.shape
    ids = lax.broadcasted_iota(jnp.int32, (experts, rows), 0)
    gate = jnp.zeros((experts, rows), F32)
    for r in range(routes_ref.shape[0]):
        gate = gate + jnp.where(routes_ref[r : r + 1, :] == ids, gates_ref[r : r + 1, :], 0.0)
    gate_ref[...] = gate
    slot = lax.broadcasted_iota(jnp.int32, (CAP, rows), 0).astype(F32)
    for index, expert in enumerate(slot_experts(chips, cores, columns)):
        same = key_ref[pl.ds(expert, 1), :] == slot
        all_ref[index * CAP : (index + 1) * CAP, :] = jnp.where(same, gate_ref[pl.ds(expert, 1), :], 0.0)
    slots = all_ref.shape[0]
    step = LANES if slots % LANES == 0 else slots
    for start in range(0, slots, step):
        out_ref[:, start : start + step] = all_ref[start : start + step, :].T.astype(BF16)


def combine_kernel(weight_ref, all_ref, out_ref):
    out_ref[...] = jnp.dot(weight_ref[...], all_ref[...], preferred_element_type=F32).astype(BF16)


def combine_gate_kernel(chips, cores, columns, weight_ref, routes_ref, key_ref, grads_ref, all_ref, out_ref, gate_ref, sum_ref):
    out_ref[...] = jnp.dot(weight_ref[...], all_ref[...], preferred_element_type=F32).astype(BF16)
    rows = key_ref.shape[1]
    slot = lax.broadcasted_iota(jnp.int32, (CAP, rows), 0).astype(F32)
    routes = routes_ref[...]
    sum_ref[...] = lax.dot_general(all_ref[...], grads_ref[...], CONTRACT_LAST, preferred_element_type=F32)
    total = jnp.zeros(gate_ref.shape, F32)
    for index, expert in enumerate(slot_experts(chips, cores, columns)):
        same = key_ref[pl.ds(expert, 1), :] == slot
        row = jnp.where(same, sum_ref[index * CAP : (index + 1) * CAP, :], 0.0)
        total = total + jnp.where(routes == expert, jnp.sum(row, axis=0, keepdims=True), 0.0)
    gate_ref[...] = total


def body(sizes, tokens, grad_out, routes, gates, gate_weight, up_weight, down_weight):
    n_dp, groups, columns = sizes
    cores = 2 if groups % 2 == 0 else 1
    chips = groups // cores
    experts = groups * columns
    rows, width = tokens.shape
    _, hid_dev, feats = gate_weight.shape
    count = n_dp * chips
    tall = n_dp * CAP
    slots = groups * CAP
    routes_t, gates_t = routes.T, gates.T

    def shape(height, length, dtype=BF16):
        return jax.ShapeDtypeStruct((height, length), dtype)

    def to_core(value, dc):
        if dc == 0:
            return value
        pairs = [(t, t // cores * cores + (t + dc) % cores) for t in range(groups)]
        return lax.ppermute(value, "tensor", pairs)

    def to_chip(value, db, dh):
        if (db, dh) == (0, 0):
            return value
        pairs = []
        for b in range(n_dp):
            for t in range(groups):
                target = (t // cores + dh) % chips * cores + t % cores
                pairs.append((b * groups + t, (b + db) % n_dp * groups + target))
        return lax.ppermute(value, ("dp", "tensor"), pairs)

    hops = [(db, dh) for db in range(n_dp) for dh in range(chips)]
    order = sorted(range(count), key=lambda index: (hops[index][0] == 0, -hops[index][1]))

    def pick(key, sources):
        return call(
            functools.partial(pick_kernel, cores),
            "pick",
            [shape(CAP, cores * width)] * chips,
            [key, *sources],
            EARLY,
        )

    def dispatch(pieces):
        arrived = {index: to_chip(pieces[hops[index][1]], *hops[index]) for index in order}
        return [arrived[index] for index in range(count)]

    def give_back(pieces):
        arrived = {index: to_chip(pieces[index], *hops[index]) for index in order}
        return [to_core(arrived[index], dc) for dc in range(cores) for index in range(count)]

    def add_blocks(pieces):
        return call(
            functools.partial(add_blocks_kernel, chips, cores),
            "add_blocks",
            shape(slots, width),
            pieces,
            2 * slots * width,
        )

    def across(value):
        return lax.all_gather(value, "expert", axis=0, tiled=True)

    token_sources = [to_core(tokens, dc) for dc in range(cores)]
    grad_sources = [to_core(grad_out, dc) for dc in range(cores)]
    key = call(number_kernel, "number", shape(experts, rows, F32), [routes_t], EARLY)
    tok_in = dispatch(pick(key, token_sources))
    tok_in[0], grad_pieces = lax.optimization_barrier((tok_in[0], pick(key, grad_sources)))
    grad_in = dispatch(grad_pieces)

    matmul_flops = 2 * tall * hid_dev * feats
    saved = [shape(tall, hid_dev, F32)] * 2
    piece = [shape(CAP, cores * width)] * count
    act, scale, *outs = call(
        functools.partial(forward_kernel, chips, cores, count),
        "forward",
        saved + piece,
        [*tok_in, gate_weight, up_weight, down_weight],
        3 * matmul_flops,
        [pltpu.VMEM((tall, feats), BF16), pltpu.VMEM((tall, hid_dev), BF16)],
        limit=24,
    )
    out_pieces = give_back(outs)
    backs = call(
        functools.partial(backward_kernel, chips, cores, count),
        "backward",
        piece,
        [*grad_in, gate_weight, up_weight, down_weight, act, scale],
        3 * matmul_flops,
        [pltpu.VMEM((tall, feats), BF16)] + [pltpu.VMEM((tall, hid_dev), BF16)] * 2,
        limit=24,
    )
    out_pieces, backs = lax.optimization_barrier((out_pieces, backs))
    out_all = across(add_blocks(out_pieces))
    back_all = across(add_blocks(give_back(backs)))

    weight_map = call(
        functools.partial(weights_kernel, chips, cores, columns),
        "weights",
        shape(rows, experts * CAP),
        [routes_t, gates_t, key],
        experts * CAP * rows,
        [pltpu.VMEM((experts, rows), F32), pltpu.VMEM((experts * CAP, rows), F32)],
        limit=16,
    )

    combine_flops = 2 * experts * CAP * rows * width
    mixed, gate_part = call(
        functools.partial(combine_gate_kernel, chips, cores, columns),
        "combine_gate",
        [shape(rows, width), shape(routes_t.shape[0], rows, F32)],
        [weight_map, routes_t, key, grad_out, out_all],
        2 * combine_flops,
        [pltpu.VMEM((experts * CAP, rows), F32)],
        limit=24,
    )
    for dc in range(1, cores):
        gate_part = gate_part + to_core(gate_part, dc)
    total = gate_part
    for dh in range(1, chips):
        total = total + to_chip(gate_part, 0, dh)
    grad_tokens = call(
        combine_kernel,
        "combine",
        shape(rows, width),
        [weight_map, back_all],
        combine_flops,
        limit=16,
    )
    return (mixed, grad_tokens, total.T)


def solution(mesh):
    sizes = (mesh.shape["dp"], mesh.shape["tensor"], mesh.shape["expert"])
    return jax.shard_map(
        functools.partial(body, sizes),
        mesh=mesh,
        in_specs=(
            P("dp", "tensor"),
            P("dp", "tensor"),
            P("dp", None),
            P("dp", None),
            P(("expert", "tensor"), "dp", None),
            P(("expert", "tensor"), "dp", None),
            P(("expert", "tensor"), "dp", None),
        ),
        out_specs=(P("dp", "tensor"), P("dp", "tensor"), P("dp", None)),
        check_vma=False,
    )
```

```python
import functools

import jax
import jax.numpy as jnp
from jax import lax
from jax.experimental import pallas as pl
from jax.experimental.pallas import tpu as pltpu
from jax.sharding import PartitionSpec as P

CAP = 48
LANES = 128
MIB = 2**20
EARLY = 6e9
BF16 = jnp.bfloat16
F32 = jnp.float32
CONTRACT_LAST = (((1,), (1,)), ((), ()))


def call(kernel, name, out_shape, operands, flops, scratch=(), limit=8):
    outs = out_shape if isinstance(out_shape, list) else [out_shape]
    moved = sum(a.size * a.dtype.itemsize for a in [*operands, *outs])
    spec = pl.BlockSpec(memory_space=pltpu.VMEM)
    return pl.pallas_call(
        kernel,
        out_shape=out_shape,
        in_specs=[spec] * len(operands),
        out_specs=[spec] * len(outs) if isinstance(out_shape, list) else spec,
        scratch_shapes=list(scratch),
        compiler_params=pltpu.CompilerParams(vmem_limit_bytes=limit * MIB),
        cost_estimate=pl.CostEstimate(flops=int(flops), bytes_accessed=int(moved), transcendentals=0),
        name=name,
    )(*operands)


def after(values, earlier):
    return lax.optimization_barrier((values, earlier))


def number_kernel(routes_ref, key_ref):
    experts, rows = key_ref.shape
    ids = lax.broadcasted_iota(jnp.int32, (experts, rows), 0)
    hit = jnp.zeros((experts, rows), F32)
    for r in range(routes_ref.shape[0]):
        hit = hit + (routes_ref[r : r + 1, :] == ids).astype(F32)
    before = (
        lax.broadcasted_iota(jnp.int32, (LANES, LANES), 0) < lax.broadcasted_iota(jnp.int32, (LANES, LANES), 1)
    ).astype(BF16)
    offset = jnp.zeros((experts, 1), F32)
    for start in range(0, rows, LANES):
        part = hit[:, start : start + LANES]
        rank = jnp.dot(part.astype(BF16), before, preferred_element_type=F32) + offset
        offset = offset + jnp.sum(part, axis=1, keepdims=True)
        key_ref[:, start : start + LANES] = jnp.where(part > 0.0, rank, -1.0)


def position(cores):
    t = lax.axis_index("tensor")
    return lax.div(t, cores), lax.rem(t, cores), lax.axis_index("expert")


def pick_kernel(cores, key_ref, *refs):
    sources, pieces = refs[:cores], refs[cores:]
    chips = len(pieces)
    rows, width = sources[0].shape
    chip, core, e = position(cores)
    slot = lax.broadcasted_iota(jnp.int32, (CAP, rows), 0).astype(F32)
    masks = []
    for dh in range(chips):
        expert = (e * chips + lax.rem(chip + dh, chips)) * cores + core
        masks.append((key_ref[pl.ds(expert, 1), :] == slot).astype(BF16))
    mask = jnp.concatenate(masks, axis=0)
    for dc, source in enumerate(sources):
        picked = jnp.dot(mask, source[...], preferred_element_type=F32).astype(BF16)
        column = pl.multiple_of(lax.rem(core - dc + cores, cores) * width, width)
        for dh, piece in enumerate(pieces):
            piece[:, pl.ds(column, width)] = picked[dh * CAP : (dh + 1) * CAP]


def gather_pieces(x_ref, pieces, chips, cores):
    chip, _, _ = position(cores)
    width = pieces[0].shape[1]
    for index, piece in enumerate(pieces):
        db, dh = divmod(index, chips)
        column = pl.multiple_of(lax.rem(chip - dh + chips, chips) * width, width)
        x_ref[db * CAP : (db + 1) * CAP, pl.ds(column, width)] = piece[...]


def project_back(terms, pieces, chips, cores):
    chip, _, _ = position(cores)
    blocks = len(pieces) // chips
    width = pieces[0].shape[1]
    for dh in range(chips):
        column = pl.ds(pl.multiple_of(lax.rem(chip + dh, chips) * width, width), width)
        total = None
        for h_ref, w_ref in terms:
            term = jnp.dot(h_ref[...], w_ref[0, :, column], preferred_element_type=F32)
            total = term if total is None else total + term
        total = total.astype(BF16)
        for db in range(blocks):
            row = (-db) % blocks * CAP
            pieces[db * chips + dh][...] = total[row : row + CAP]


def chunks_of(hid_dev):
    size = 256 if hid_dev % 256 == 0 else hid_dev
    return [slice(start, start + size) for start in range(0, hid_dev, size)]


def forward_kernel(chips, cores, count, *refs):
    pieces, (gate_ref, up_ref, down_ref) = refs[:count], refs[count : count + 3]
    act_ref, scale_ref = refs[count + 3 : count + 5]
    outs, (x_ref, hid_ref) = refs[count + 5 : 2 * count + 5], refs[2 * count + 5 :]
    gather_pieces(x_ref, pieces, chips, cores)
    for part in chunks_of(gate_ref.shape[1]):
        gate_pre = lax.dot_general(x_ref[...], gate_ref[0, part, :], CONTRACT_LAST, preferred_element_type=F32)
        up_pre = lax.dot_general(x_ref[...], up_ref[0, part, :], CONTRACT_LAST, preferred_element_type=F32)
        sig = jax.nn.sigmoid(gate_pre)
        act = gate_pre * sig
        hid_ref[:, part] = (act * up_pre).astype(BF16)
        act_ref[:, part] = act
        scale_ref[:, part] = up_pre * (sig * (1.0 + gate_pre * (1.0 - sig)))
    project_back([(hid_ref, down_ref)], outs, chips, cores)


def backward_kernel(chips, cores, count, *refs):
    pieces, (gate_ref, up_ref, down_ref) = refs[:count], refs[count : count + 3]
    act_ref, scale_ref = refs[count + 3 : count + 5]
    outs, (x_ref, grad_gate_ref, grad_up_ref) = refs[count + 5 : 2 * count + 5], refs[2 * count + 5 :]
    gather_pieces(x_ref, pieces, chips, cores)
    for part in chunks_of(gate_ref.shape[1]):
        grad_hid = lax.dot_general(x_ref[...], down_ref[0, part, :], CONTRACT_LAST, preferred_element_type=F32)
        grad_gate_ref[:, part] = (grad_hid * scale_ref[:, part]).astype(BF16)
        grad_up_ref[:, part] = (grad_hid * act_ref[:, part]).astype(BF16)
    project_back([(grad_gate_ref, gate_ref), (grad_up_ref, up_ref)], outs, chips, cores)


def add_blocks_kernel(chips, cores, *refs):
    pieces, out_ref = refs[:-1], refs[-1]
    width = out_ref.shape[1]
    count = len(pieces) // cores
    _, core, _ = position(cores)
    column = pl.ds(pl.multiple_of(core * width, width), width)
    for dh in range(chips):
        for dc in range(cores):
            total = None
            for piece in pieces[dc * count + dh : (dc + 1) * count : chips]:
                term = piece[:, column].astype(F32)
                total = term if total is None else total + term
            row = (dh * cores + dc) * CAP
            out_ref[row : row + CAP, :] = total.astype(BF16)


def slot_experts(chips, cores, columns):
    chip, core, e = position(cores)
    experts = []
    for dz in range(columns):
        for dh in range(chips):
            for dc in range(cores):
                column = lax.rem(e - dz + columns, columns)
                owner = lax.rem(chip - dh + chips, chips)
                experts.append((column * chips + owner) * cores + lax.rem(core - dc + cores, cores))
    return experts


def weights_kernel(chips, cores, columns, routes_ref, gates_ref, key_ref, out_ref, gate_ref, all_ref):
    experts, rows = key_ref.shape
    ids = lax.broadcasted_iota(jnp.int32, (experts, rows), 0)
    gate = jnp.zeros((experts, rows), F32)
    for r in range(routes_ref.shape[0]):
        gate = gate + jnp.where(routes_ref[r : r + 1, :] == ids, gates_ref[r : r + 1, :], 0.0)
    gate_ref[...] = gate
    slot = lax.broadcasted_iota(jnp.int32, (CAP, rows), 0).astype(F32)
    for index, expert in enumerate(slot_experts(chips, cores, columns)):
        same = key_ref[pl.ds(expert, 1), :] == slot
        all_ref[index * CAP : (index + 1) * CAP, :] = jnp.where(same, gate_ref[pl.ds(expert, 1), :], 0.0)
    slots = all_ref.shape[0]
    step = LANES if slots % LANES == 0 else slots
    for start in range(0, slots, step):
        out_ref[:, start : start + step] = all_ref[start : start + step, :].T.astype(BF16)


def place_parts(parts, all_ref, columns):
    height = parts[0].shape[0]
    if len(parts) == columns:
        for index, part in enumerate(parts):
            all_ref[index * height : (index + 1) * height, :] = part[...]
        return
    own, far, up, down, ends = parts
    e = lax.axis_index("expert")
    all_ref[0:height, :] = own[...]
    all_ref[2 * height : 3 * height, :] = far[...]
    all_ref[height : 2 * height, :] = jnp.where(e == 0, ends[...], up[...])
    all_ref[3 * height : 4 * height, :] = jnp.where(e == columns - 1, ends[...], down[...])


def combine_kernel(columns, weight_ref, *refs):
    parts, (out_ref, all_ref) = refs[:-2], refs[-2:]
    place_parts(parts, all_ref, columns)
    out_ref[...] = jnp.dot(weight_ref[...], all_ref[...], preferred_element_type=F32).astype(BF16)


def combine_gate_kernel(chips, cores, columns, weight_ref, routes_ref, key_ref, grads_ref, *refs):
    parts, (out_ref, gate_ref, all_ref, sum_ref) = refs[:-4], refs[-4:]
    place_parts(parts, all_ref, columns)
    out_ref[...] = jnp.dot(weight_ref[...], all_ref[...], preferred_element_type=F32).astype(BF16)
    rows = key_ref.shape[1]
    slot = lax.broadcasted_iota(jnp.int32, (CAP, rows), 0).astype(F32)
    routes = routes_ref[...]
    sum_ref[...] = lax.dot_general(all_ref[...], grads_ref[...], CONTRACT_LAST, preferred_element_type=F32)
    total = jnp.zeros(gate_ref.shape, F32)
    for index, expert in enumerate(slot_experts(chips, cores, columns)):
        same = key_ref[pl.ds(expert, 1), :] == slot
        row = jnp.where(same, sum_ref[index * CAP : (index + 1) * CAP, :], 0.0)
        total = total + jnp.where(routes == expert, jnp.sum(row, axis=0, keepdims=True), 0.0)
    gate_ref[...] = total


def body(sizes, tokens, grad_out, routes, gates, gate_weight, up_weight, down_weight):
    n_dp, groups, columns = sizes
    cores = 2 if groups % 2 == 0 else 1
    chips = groups // cores
    experts = groups * columns
    rows, width = tokens.shape
    _, hid_dev, feats = gate_weight.shape
    count = n_dp * chips
    tall = n_dp * CAP
    slots = groups * CAP
    routes_t, gates_t = routes.T, gates.T

    def shape(height, length, dtype=BF16):
        return jax.ShapeDtypeStruct((height, length), dtype)

    def to_core(value, dc):
        if dc == 0:
            return value
        pairs = [(t, t // cores * cores + (t + dc) % cores) for t in range(groups)]
        return lax.ppermute(value, "tensor", pairs)

    def to_chip(value, db, dh):
        if (db, dh) == (0, 0):
            return value
        pairs = []
        for b in range(n_dp):
            for t in range(groups):
                target = (t // cores + dh) % chips * cores + t % cores
                pairs.append((b * groups + t, (b + db) % n_dp * groups + target))
        return lax.ppermute(value, ("dp", "tensor"), pairs)

    hops = [(db, dh) for db in range(n_dp) for dh in range(chips)]
    order = sorted(range(count), key=lambda index: (hops[index][0] == 0, -hops[index][1]))

    def pick(key, sources):
        return call(
            functools.partial(pick_kernel, cores),
            "pick",
            [shape(CAP, cores * width)] * chips,
            [key, *sources],
            EARLY,
        )

    def dispatch(pieces):
        arrived = {index: to_chip(pieces[hops[index][1]], *hops[index]) for index in order}
        return [arrived[index] for index in range(count)]

    def give_back(pieces):
        arrived = {index: to_chip(pieces[index], *hops[index]) for index in order}
        return [to_core(arrived[index], dc) for dc in range(cores) for index in range(count)]

    def add_blocks(pieces):
        return call(
            functools.partial(add_blocks_kernel, chips, cores),
            "add_blocks",
            shape(slots, width),
            pieces,
            2 * slots * width,
        )

    def across(value):
        if columns != 4:
            return [value] + [
                lax.ppermute(value, "expert", [(z, (z + dz) % columns) for z in range(columns)])
                for dz in range(1, columns)
            ]
        far = lax.ppermute(value, "expert", [(z, (z + 2) % columns) for z in range(columns)])
        up = lax.ppermute(value, "expert", [(z, z + 1) for z in range(columns - 1)])
        down = lax.ppermute(value, "expert", [(z + 1, z) for z in range(columns - 1)])
        ends = lax.ppermute(far, "expert", [(2, 3), (1, 0)])
        return [value, far, up, down, ends]

    token_sources = [to_core(tokens, dc) for dc in range(cores)]
    grad_sources = [to_core(grad_out, dc) for dc in range(cores)]
    key = call(number_kernel, "number", shape(experts, rows, F32), [routes_t], EARLY)
    tok_in = dispatch(pick(key, token_sources))
    tok_in[0], grad_pieces = lax.optimization_barrier((tok_in[0], pick(key, grad_sources)))
    grad_in = dispatch(grad_pieces)

    matmul_flops = 2 * tall * hid_dev * feats
    saved = [shape(tall, hid_dev, F32)] * 2
    piece = [shape(CAP, cores * width)] * count
    act, scale, *outs = call(
        functools.partial(forward_kernel, chips, cores, count),
        "forward",
        saved + piece,
        [*tok_in, gate_weight, up_weight, down_weight],
        3 * matmul_flops,
        [pltpu.VMEM((tall, feats), BF16), pltpu.VMEM((tall, hid_dev), BF16)],
        limit=24,
    )
    outs, grad_in = after(outs, grad_in)
    out_pieces = give_back(outs)
    backs = call(
        functools.partial(backward_kernel, chips, cores, count),
        "backward",
        piece,
        [*grad_in, gate_weight, up_weight, down_weight, act, scale],
        3 * matmul_flops,
        [pltpu.VMEM((tall, feats), BF16)] + [pltpu.VMEM((tall, hid_dev), BF16)] * 2,
        limit=24,
    )
    out_pieces, backs = after(out_pieces, backs)
    out_parts = across(add_blocks(out_pieces))
    back_pieces = give_back(backs)
    back_pieces, out_parts[1:4] = after(back_pieces, out_parts[1:4])
    back_parts = across(add_blocks(back_pieces))
    out_parts, back_parts[1:2] = after(out_parts, back_parts[1:2])

    weight_map = call(
        functools.partial(weights_kernel, chips, cores, columns),
        "weights",
        shape(rows, experts * CAP),
        [routes_t, gates_t, key],
        experts * CAP * rows,
        [pltpu.VMEM((experts, rows), F32), pltpu.VMEM((experts * CAP, rows), F32)],
        limit=16,
    )

    all_rows = pltpu.VMEM((experts * CAP, width), BF16)
    combine_flops = 2 * experts * CAP * rows * width
    mixed, gate_part = call(
        functools.partial(combine_gate_kernel, chips, cores, columns),
        "combine_gate",
        [shape(rows, width), shape(routes_t.shape[0], rows, F32)],
        [weight_map, routes_t, key, grad_out, *out_parts],
        0,
        [all_rows, pltpu.VMEM((experts * CAP, rows), F32)],
        limit=24,
    )
    gate_part, back_parts[2:4] = after(gate_part, back_parts[2:4])
    for dc in range(1, cores):
        gate_part = gate_part + to_core(gate_part, dc)
    total = gate_part
    for dh in range(1, chips):
        total = total + to_chip(gate_part, 0, dh)
    grad_tokens = call(
        functools.partial(combine_kernel, columns),
        "combine",
        shape(rows, width),
        [weight_map, *back_parts],
        combine_flops,
        [all_rows],
        limit=16,
    )
    return (mixed, grad_tokens, total.T)


def solution(mesh):
    sizes = (mesh.shape["dp"], mesh.shape["tensor"], mesh.shape["expert"])
    return jax.shard_map(
        functools.partial(body, sizes),
        mesh=mesh,
        in_specs=(
            P("dp", "tensor"),
            P("dp", "tensor"),
            P("dp", None),
            P("dp", None),
            P(("expert", "tensor"), "dp", None),
            P(("expert", "tensor"), "dp", None),
            P(("expert", "tensor"), "dp", None),
        ),
        out_specs=(P("dp", "tensor"), P("dp", "tensor"), P("dp", None)),
        check_vma=False,
    )
```

```python
import functools

import jax
import jax.numpy as jnp
from jax import lax
from jax.experimental import pallas as pl
from jax.experimental.pallas import tpu as pltpu
from jax.sharding import PartitionSpec as P

CAP = 48
LANES = 128
MIB = 2**20
EARLY = 6e9
BF16 = jnp.bfloat16
F32 = jnp.float32
CONTRACT_LAST = (((1,), (1,)), ((), ()))


def call(kernel, name, out_shape, operands, flops, scratch=(), limit=8):
    outs = out_shape if isinstance(out_shape, list) else [out_shape]
    moved = sum(a.size * a.dtype.itemsize for a in [*operands, *outs])
    spec = pl.BlockSpec(memory_space=pltpu.VMEM)
    return pl.pallas_call(
        kernel,
        out_shape=out_shape,
        in_specs=[spec] * len(operands),
        out_specs=[spec] * len(outs) if isinstance(out_shape, list) else spec,
        scratch_shapes=list(scratch),
        compiler_params=pltpu.CompilerParams(vmem_limit_bytes=limit * MIB),
        cost_estimate=pl.CostEstimate(flops=int(flops), bytes_accessed=int(moved), transcendentals=0),
        name=name,
    )(*operands)


def after(values, earlier):
    return lax.optimization_barrier((values, earlier))


def number_kernel(routes_ref, key_ref):
    experts, rows = key_ref.shape
    ids = lax.broadcasted_iota(jnp.int32, (experts, rows), 0)
    hit = jnp.zeros((experts, rows), F32)
    for r in range(routes_ref.shape[0]):
        hit = hit + (routes_ref[r : r + 1, :] == ids).astype(F32)
    before = (
        lax.broadcasted_iota(jnp.int32, (LANES, LANES), 0) < lax.broadcasted_iota(jnp.int32, (LANES, LANES), 1)
    ).astype(BF16)
    offset = jnp.zeros((experts, 1), F32)
    for start in range(0, rows, LANES):
        part = hit[:, start : start + LANES]
        rank = jnp.dot(part.astype(BF16), before, preferred_element_type=F32) + offset
        offset = offset + jnp.sum(part, axis=1, keepdims=True)
        key_ref[:, start : start + LANES] = jnp.where(part > 0.0, rank, -1.0)


def position(cores):
    t = lax.axis_index("tensor")
    return lax.div(t, cores), lax.rem(t, cores), lax.axis_index("expert")


def pick_kernel(cores, key_ref, *refs):
    sources, pieces = refs[: 2 * cores], refs[2 * cores :]
    chips = len(pieces)
    rows, width = sources[0].shape
    chip, core, e = position(cores)
    slot = lax.broadcasted_iota(jnp.int32, (CAP, rows), 0).astype(F32)
    masks = []
    for dh in range(chips):
        expert = (e * chips + lax.rem(chip + dh, chips)) * cores + core
        masks.append((key_ref[pl.ds(expert, 1), :] == slot).astype(BF16))
    mask = jnp.concatenate(masks, axis=0)
    for index, source in enumerate(sources):
        kind, dc = divmod(index, cores)
        picked = jnp.dot(mask, source[...], preferred_element_type=F32).astype(BF16)
        column = pl.multiple_of(lax.rem(core - dc + cores, cores) * width, width)
        for dh, piece in enumerate(pieces):
            piece[kind * CAP : (kind + 1) * CAP, pl.ds(column, width)] = picked[dh * CAP : (dh + 1) * CAP]


def gather_pieces(x_ref, pieces, kind, chips, cores):
    chip, _, _ = position(cores)
    width = pieces[0].shape[1]
    for index, piece in enumerate(pieces):
        db, dh = divmod(index, chips)
        column = pl.multiple_of(lax.rem(chip - dh + chips, chips) * width, width)
        x_ref[db * CAP : (db + 1) * CAP, pl.ds(column, width)] = piece[kind * CAP : (kind + 1) * CAP, :]


def project_back(terms, pieces, chips, cores):
    chip, _, _ = position(cores)
    blocks = len(pieces) // chips
    width = pieces[0].shape[1]
    for dh in range(chips):
        column = pl.ds(pl.multiple_of(lax.rem(chip + dh, chips) * width, width), width)
        total = None
        for h_ref, w_ref in terms:
            term = jnp.dot(h_ref[...], w_ref[0, :, column], preferred_element_type=F32)
            total = term if total is None else total + term
        total = total.astype(BF16)
        for db in range(blocks):
            row = (-db) % blocks * CAP
            pieces[db * chips + dh][...] = total[row : row + CAP]


def chunks_of(hid_dev):
    size = 256 if hid_dev % 256 == 0 else hid_dev
    return [slice(start, start + size) for start in range(0, hid_dev, size)]


def forward_kernel(chips, cores, count, *refs):
    pieces, (gate_ref, up_ref, down_ref) = refs[:count], refs[count : count + 3]
    act_ref, scale_ref = refs[count + 3 : count + 5]
    outs, (x_ref, hid_ref) = refs[count + 5 : 2 * count + 5], refs[2 * count + 5 :]
    gather_pieces(x_ref, pieces, 0, chips, cores)
    for part in chunks_of(gate_ref.shape[1]):
        gate_pre = lax.dot_general(x_ref[...], gate_ref[0, part, :], CONTRACT_LAST, preferred_element_type=F32)
        up_pre = lax.dot_general(x_ref[...], up_ref[0, part, :], CONTRACT_LAST, preferred_element_type=F32)
        sig = jax.nn.sigmoid(gate_pre)
        act = gate_pre * sig
        hid_ref[:, part] = (act * up_pre).astype(BF16)
        act_ref[:, part] = act
        scale_ref[:, part] = up_pre * (sig * (1.0 + gate_pre * (1.0 - sig)))
    project_back([(hid_ref, down_ref)], outs, chips, cores)


def backward_kernel(chips, cores, count, *refs):
    pieces, (gate_ref, up_ref, down_ref) = refs[:count], refs[count : count + 3]
    act_ref, scale_ref = refs[count + 3 : count + 5]
    outs, (x_ref, grad_gate_ref, grad_up_ref) = refs[count + 5 : 2 * count + 5], refs[2 * count + 5 :]
    gather_pieces(x_ref, pieces, 1, chips, cores)
    for part in chunks_of(gate_ref.shape[1]):
        grad_hid = lax.dot_general(x_ref[...], down_ref[0, part, :], CONTRACT_LAST, preferred_element_type=F32)
        grad_gate_ref[:, part] = (grad_hid * scale_ref[:, part]).astype(BF16)
        grad_up_ref[:, part] = (grad_hid * act_ref[:, part]).astype(BF16)
    project_back([(grad_gate_ref, gate_ref), (grad_up_ref, up_ref)], outs, chips, cores)


def add_blocks_kernel(chips, cores, *refs):
    pieces, out_ref = refs[:-1], refs[-1]
    width = out_ref.shape[1]
    count = len(pieces) // cores
    _, core, _ = position(cores)
    column = pl.ds(pl.multiple_of(core * width, width), width)
    for dh in range(chips):
        for dc in range(cores):
            total = None
            for piece in pieces[dc * count + dh : (dc + 1) * count : chips]:
                term = piece[:, column].astype(F32)
                total = term if total is None else total + term
            row = (dh * cores + dc) * CAP
            out_ref[row : row + CAP, :] = total.astype(BF16)


def slot_experts(chips, cores, columns):
    chip, core, e = position(cores)
    experts = []
    for dz in range(columns):
        for dh in range(chips):
            for dc in range(cores):
                column = lax.rem(e - dz + columns, columns)
                owner = lax.rem(chip - dh + chips, chips)
                experts.append((column * chips + owner) * cores + lax.rem(core - dc + cores, cores))
    return experts


def weights_kernel(chips, cores, columns, routes_ref, gates_ref, key_ref, out_ref, gate_ref, all_ref):
    experts, rows = key_ref.shape
    ids = lax.broadcasted_iota(jnp.int32, (experts, rows), 0)
    gate = jnp.zeros((experts, rows), F32)
    for r in range(routes_ref.shape[0]):
        gate = gate + jnp.where(routes_ref[r : r + 1, :] == ids, gates_ref[r : r + 1, :], 0.0)
    gate_ref[...] = gate
    slot = lax.broadcasted_iota(jnp.int32, (CAP, rows), 0).astype(F32)
    for index, expert in enumerate(slot_experts(chips, cores, columns)):
        same = key_ref[pl.ds(expert, 1), :] == slot
        all_ref[index * CAP : (index + 1) * CAP, :] = jnp.where(same, gate_ref[pl.ds(expert, 1), :], 0.0)
    slots = all_ref.shape[0]
    step = LANES if slots % LANES == 0 else slots
    for start in range(0, slots, step):
        out_ref[:, start : start + step] = all_ref[start : start + step, :].T.astype(BF16)


def place_parts(parts, all_ref, columns):
    height = parts[0].shape[0]
    if len(parts) == columns:
        for index, part in enumerate(parts):
            all_ref[index * height : (index + 1) * height, :] = part[...]
        return
    own, far, up, down, ends = parts
    e = lax.axis_index("expert")
    all_ref[0:height, :] = own[...]
    all_ref[2 * height : 3 * height, :] = far[...]
    all_ref[height : 2 * height, :] = jnp.where(e == 0, ends[...], up[...])
    all_ref[3 * height : 4 * height, :] = jnp.where(e == columns - 1, ends[...], down[...])


def combine_kernel(columns, weight_ref, *refs):
    parts, gates = refs[:columns], refs[columns:-3]
    out_ref, total_ref, all_ref = refs[-3:]
    place_parts(parts, all_ref, columns)
    out_ref[...] = jnp.dot(weight_ref[...], all_ref[...], preferred_element_type=F32).astype(BF16)
    total = gates[0][...]
    for gate in gates[1:]:
        total = total + gate[...]
    total_ref[...] = total


def combine_gate_kernel(chips, cores, columns, weight_ref, routes_ref, key_ref, grads_ref, *refs):
    parts, (out_ref, gate_ref, all_ref, sum_ref) = refs[:-4], refs[-4:]
    place_parts(parts, all_ref, columns)
    out_ref[...] = jnp.dot(weight_ref[...], all_ref[...], preferred_element_type=F32).astype(BF16)
    rows = key_ref.shape[1]
    slot = lax.broadcasted_iota(jnp.int32, (CAP, rows), 0).astype(F32)
    routes = routes_ref[...]
    sum_ref[...] = lax.dot_general(all_ref[...], grads_ref[...], CONTRACT_LAST, preferred_element_type=F32)
    total = jnp.zeros(gate_ref.shape, F32)
    for index, expert in enumerate(slot_experts(chips, cores, columns)):
        same = key_ref[pl.ds(expert, 1), :] == slot
        row = jnp.where(same, sum_ref[index * CAP : (index + 1) * CAP, :], 0.0)
        total = total + jnp.where(routes == expert, jnp.sum(row, axis=0, keepdims=True), 0.0)
    gate_ref[...] = total


def body(sizes, tokens, grad_out, routes, gates, gate_weight, up_weight, down_weight):
    n_dp, groups, columns = sizes
    cores = 2 if groups % 2 == 0 else 1
    chips = groups // cores
    experts = groups * columns
    rows, width = tokens.shape
    _, hid_dev, feats = gate_weight.shape
    count = n_dp * chips
    tall = n_dp * CAP
    slots = groups * CAP
    routes_t, gates_t = routes.T, gates.T

    def shape(height, length, dtype=BF16):
        return jax.ShapeDtypeStruct((height, length), dtype)

    def to_core(value, dc):
        if dc == 0:
            return value
        pairs = [(t, t // cores * cores + (t + dc) % cores) for t in range(groups)]
        return lax.ppermute(value, "tensor", pairs)

    def to_chip(value, db, dh):
        if (db, dh) == (0, 0):
            return value
        pairs = []
        for b in range(n_dp):
            for t in range(groups):
                target = (t // cores + dh) % chips * cores + t % cores
                pairs.append((b * groups + t, (b + db) % n_dp * groups + target))
        return lax.ppermute(value, ("dp", "tensor"), pairs)

    hops = [(db, dh) for db in range(n_dp) for dh in range(chips)]
    order = sorted(range(count), key=lambda index: (hops[index][0] == 0, -hops[index][1]))

    def dispatch(pieces):
        arrived = {index: to_chip(pieces[hops[index][1]], *hops[index]) for index in order}
        return [arrived[index] for index in range(count)]

    def give_back(pieces):
        arrived = {index: to_chip(pieces[index], *hops[index]) for index in order}
        return [to_core(arrived[index], dc) for dc in range(cores) for index in range(count)]

    def add_blocks(pieces):
        return call(
            functools.partial(add_blocks_kernel, chips, cores),
            "add_blocks",
            shape(slots, width),
            pieces,
            2 * slots * width,
        )

    def across(value):
        parts = [value]
        for dz in range(1, columns):
            parts.append(lax.ppermute(value, "expert", [(z, (z + dz) % columns) for z in range(columns)]))
        return parts

    def along(value):
        if columns != 4:
            return across(value)
        far = lax.ppermute(value, "expert", [(z, (z + 2) % columns) for z in range(columns)])
        up = lax.ppermute(value, "expert", [(z, z + 1) for z in range(columns - 1)])
        down = lax.ppermute(value, "expert", [(z + 1, z) for z in range(columns - 1)])
        ends = lax.ppermute(far, "expert", [(2, 3), (1, 0)])
        return [value, far, up, down, ends]

    sources = [to_core(tokens, dc) for dc in range(cores)] + [to_core(grad_out, dc) for dc in range(cores)]
    key = call(number_kernel, "number", shape(experts, rows, F32), [routes_t], EARLY)
    picked = call(
        functools.partial(pick_kernel, cores),
        "pick",
        [shape(2 * CAP, cores * width)] * chips,
        [key, *sources],
        EARLY,
    )
    rows_in = dispatch(picked)

    matmul_flops = 2 * tall * hid_dev * feats
    saved = [shape(tall, hid_dev, F32)] * 2
    piece = [shape(CAP, cores * width)] * count
    act, scale, *outs = call(
        functools.partial(forward_kernel, chips, cores, count),
        "forward",
        saved + piece,
        [*rows_in, gate_weight, up_weight, down_weight],
        3 * matmul_flops,
        [pltpu.VMEM((tall, feats), BF16), pltpu.VMEM((tall, hid_dev), BF16)],
        limit=24,
    )
    out_pieces = give_back(outs)
    backs = call(
        functools.partial(backward_kernel, chips, cores, count),
        "backward",
        piece,
        [*rows_in, gate_weight, up_weight, down_weight, act, scale],
        3 * matmul_flops,
        [pltpu.VMEM((tall, feats), BF16)] + [pltpu.VMEM((tall, hid_dev), BF16)] * 2,
        limit=24,
    )
    out_pieces, backs = after(out_pieces, backs)
    out_rows = add_blocks(out_pieces)
    out_rows, backs = after(out_rows, backs)
    out_parts = along(out_rows)
    back_pieces = give_back(backs)
    back_pieces, out_parts[1:4] = after(back_pieces, out_parts[1:4])
    back_rows = add_blocks(back_pieces)
    back_parts = across(back_rows)
    _, out_parts = after(back_rows, out_parts)

    weight_map = call(
        functools.partial(weights_kernel, chips, cores, columns),
        "weights",
        shape(rows, experts * CAP),
        [routes_t, gates_t, key],
        experts * CAP * rows,
        [pltpu.VMEM((experts, rows), F32), pltpu.VMEM((experts * CAP, rows), F32)],
        limit=16,
    )

    all_rows = pltpu.VMEM((experts * CAP, width), BF16)
    combine_flops = 2 * experts * CAP * rows * width
    mixed, gate_part = call(
        functools.partial(combine_gate_kernel, chips, cores, columns),
        "combine_gate",
        [shape(rows, width), shape(routes_t.shape[0], rows, F32)],
        [weight_map, routes_t, key, grad_out, *out_parts],
        0,
        [all_rows, pltpu.VMEM((experts * CAP, rows), F32)],
        limit=24,
    )
    gate_parts = [gate_part]
    for dt in range(1, groups):
        pairs = [(t, (t + dt) % groups) for t in range(groups)]
        gate_parts.append(lax.ppermute(gate_part, "tensor", pairs))
    grad_tokens, grad_gates = call(
        functools.partial(combine_kernel, columns),
        "combine",
        [shape(rows, width), shape(*gate_part.shape, F32)],
        [weight_map, *back_parts, *gate_parts],
        combine_flops,
        [all_rows],
        limit=16,
    )
    return (mixed, grad_tokens, grad_gates.T)


def solution(mesh):
    sizes = (mesh.shape["dp"], mesh.shape["tensor"], mesh.shape["expert"])
    return jax.shard_map(
        functools.partial(body, sizes),
        mesh=mesh,
        in_specs=(
            P("dp", "tensor"),
            P("dp", "tensor"),
            P("dp", None),
            P("dp", None),
            P(("expert", "tensor"), "dp", None),
            P(("expert", "tensor"), "dp", None),
            P(("expert", "tensor"), "dp", None),
        ),
        out_specs=(P("dp", "tensor"), P("dp", "tensor"), P("dp", None)),
        check_vma=False,
    )
```

```python
import functools

import jax
import jax.numpy as jnp
from jax import lax
from jax.experimental import pallas as pl
from jax.experimental.pallas import tpu as pltpu
from jax.sharding import PartitionSpec as P

CAP = 48
LANES = 128
MIB = 2**20
EARLY = 6e9
BF16 = jnp.bfloat16
F32 = jnp.float32
CONTRACT_LAST = (((1,), (1,)), ((), ()))


def call(kernel, name, out_shape, operands, flops, scratch=(), limit=8):
    outs = out_shape if isinstance(out_shape, list) else [out_shape]
    moved = sum(a.size * a.dtype.itemsize for a in [*operands, *outs])
    spec = pl.BlockSpec(memory_space=pltpu.VMEM)
    return pl.pallas_call(
        kernel,
        out_shape=out_shape,
        in_specs=[spec] * len(operands),
        out_specs=[spec] * len(outs) if isinstance(out_shape, list) else spec,
        scratch_shapes=list(scratch),
        compiler_params=pltpu.CompilerParams(vmem_limit_bytes=limit * MIB),
        cost_estimate=pl.CostEstimate(flops=int(flops), bytes_accessed=int(moved), transcendentals=0),
        name=name,
    )(*operands)


def after(values, earlier):
    return lax.optimization_barrier((values, earlier))


def number_kernel(routes_ref, key_ref):
    experts, rows = key_ref.shape
    ids = lax.broadcasted_iota(jnp.int32, (experts, rows), 0)
    hit = jnp.zeros((experts, rows), F32)
    for r in range(routes_ref.shape[0]):
        hit = hit + (routes_ref[r : r + 1, :] == ids).astype(F32)
    before = (
        lax.broadcasted_iota(jnp.int32, (LANES, LANES), 0) < lax.broadcasted_iota(jnp.int32, (LANES, LANES), 1)
    ).astype(BF16)
    offset = jnp.zeros((experts, 1), F32)
    for start in range(0, rows, LANES):
        part = hit[:, start : start + LANES]
        rank = jnp.dot(part.astype(BF16), before, preferred_element_type=F32) + offset
        offset = offset + jnp.sum(part, axis=1, keepdims=True)
        key_ref[:, start : start + LANES] = jnp.where(part > 0.0, rank, -1.0)


def position(cores):
    t = lax.axis_index("tensor")
    return lax.div(t, cores), lax.rem(t, cores), lax.axis_index("expert")


def pick_kernel(cores, key_ref, *refs):
    sources, pieces = refs[: 2 * cores], refs[2 * cores :]
    chips = len(pieces)
    rows, width = sources[0].shape
    chip, core, e = position(cores)
    slot = lax.broadcasted_iota(jnp.int32, (CAP, rows), 0).astype(F32)
    masks = []
    for dh in range(chips):
        expert = (e * chips + lax.rem(chip + dh, chips)) * cores + core
        masks.append((key_ref[pl.ds(expert, 1), :] == slot).astype(BF16))
    mask = jnp.concatenate(masks, axis=0)
    for index, source in enumerate(sources):
        kind, dc = divmod(index, cores)
        picked = jnp.dot(mask, source[...], preferred_element_type=F32).astype(BF16)
        column = pl.multiple_of(lax.rem(core - dc + cores, cores) * width, width)
        for dh, piece in enumerate(pieces):
            piece[kind * CAP : (kind + 1) * CAP, pl.ds(column, width)] = picked[dh * CAP : (dh + 1) * CAP]


def gather_pieces(x_ref, pieces, kind, chips, cores):
    chip, _, _ = position(cores)
    width = pieces[0].shape[1]
    for index, piece in enumerate(pieces):
        db, dh = divmod(index, chips)
        column = pl.multiple_of(lax.rem(chip - dh + chips, chips) * width, width)
        x_ref[db * CAP : (db + 1) * CAP, pl.ds(column, width)] = piece[kind * CAP : (kind + 1) * CAP, :]


def project_back(terms, pieces, chips, cores):
    chip, _, _ = position(cores)
    blocks = len(pieces) // chips
    width = pieces[0].shape[1]
    for dh in range(chips):
        column = pl.ds(pl.multiple_of(lax.rem(chip + dh, chips) * width, width), width)
        total = None
        for h_ref, w_ref in terms:
            term = jnp.dot(h_ref[...], w_ref[0, :, column], preferred_element_type=F32)
            total = term if total is None else total + term
        total = total.astype(BF16)
        for db in range(blocks):
            row = (-db) % blocks * CAP
            pieces[db * chips + dh][...] = total[row : row + CAP]


def chunks_of(hid_dev):
    size = 256 if hid_dev % 256 == 0 else hid_dev
    return [slice(start, start + size) for start in range(0, hid_dev, size)]


def forward_kernel(chips, cores, count, *refs):
    pieces, (gate_ref, up_ref, down_ref) = refs[:count], refs[count : count + 3]
    act_ref, scale_ref = refs[count + 3 : count + 5]
    outs, (x_ref, hid_ref) = refs[count + 5 : 2 * count + 5], refs[2 * count + 5 :]
    gather_pieces(x_ref, pieces, 0, chips, cores)
    for part in chunks_of(gate_ref.shape[1]):
        gate_pre = lax.dot_general(x_ref[...], gate_ref[0, part, :], CONTRACT_LAST, preferred_element_type=F32)
        up_pre = lax.dot_general(x_ref[...], up_ref[0, part, :], CONTRACT_LAST, preferred_element_type=F32)
        sig = jax.nn.sigmoid(gate_pre)
        act = gate_pre * sig
        hid_ref[:, part] = (act * up_pre).astype(BF16)
        act_ref[:, part] = act
        scale_ref[:, part] = up_pre * (sig * (1.0 + gate_pre * (1.0 - sig)))
    project_back([(hid_ref, down_ref)], outs, chips, cores)


def backward_kernel(chips, cores, count, *refs):
    pieces, (gate_ref, up_ref, down_ref) = refs[:count], refs[count : count + 3]
    act_ref, scale_ref = refs[count + 3 : count + 5]
    outs, (x_ref, grad_gate_ref, grad_up_ref) = refs[count + 5 : 2 * count + 5], refs[2 * count + 5 :]
    gather_pieces(x_ref, pieces, 1, chips, cores)
    for part in chunks_of(gate_ref.shape[1]):
        grad_hid = lax.dot_general(x_ref[...], down_ref[0, part, :], CONTRACT_LAST, preferred_element_type=F32)
        grad_gate_ref[:, part] = (grad_hid * scale_ref[:, part]).astype(BF16)
        grad_up_ref[:, part] = (grad_hid * act_ref[:, part]).astype(BF16)
    project_back([(grad_gate_ref, gate_ref), (grad_up_ref, up_ref)], outs, chips, cores)


def add_blocks_kernel(chips, cores, *refs):
    pieces, out_ref = refs[:-1], refs[-1]
    width = out_ref.shape[1]
    count = len(pieces) // cores
    _, core, _ = position(cores)
    column = pl.ds(pl.multiple_of(core * width, width), width)
    for dh in range(chips):
        for dc in range(cores):
            total = None
            for piece in pieces[dc * count + dh : (dc + 1) * count : chips]:
                term = piece[:, column].astype(F32)
                total = term if total is None else total + term
            row = (dh * cores + dc) * CAP
            out_ref[row : row + CAP, :] = total.astype(BF16)


def slot_experts(chips, cores, columns):
    chip, core, e = position(cores)
    experts = []
    for dz in range(columns):
        for dh in range(chips):
            for dc in range(cores):
                column = lax.rem(e - dz + columns, columns)
                owner = lax.rem(chip - dh + chips, chips)
                experts.append((column * chips + owner) * cores + lax.rem(core - dc + cores, cores))
    return experts


def weights_kernel(chips, cores, columns, routes_ref, gates_ref, key_ref, out_ref, gate_ref, all_ref):
    experts, rows = key_ref.shape
    ids = lax.broadcasted_iota(jnp.int32, (experts, rows), 0)
    gate = jnp.zeros((experts, rows), F32)
    for r in range(routes_ref.shape[0]):
        gate = gate + jnp.where(routes_ref[r : r + 1, :] == ids, gates_ref[r : r + 1, :], 0.0)
    gate_ref[...] = gate
    slot = lax.broadcasted_iota(jnp.int32, (CAP, rows), 0).astype(F32)
    for index, expert in enumerate(slot_experts(chips, cores, columns)):
        same = key_ref[pl.ds(expert, 1), :] == slot
        all_ref[index * CAP : (index + 1) * CAP, :] = jnp.where(same, gate_ref[pl.ds(expert, 1), :], 0.0)
    slots = all_ref.shape[0]
    step = LANES if slots % LANES == 0 else slots
    for start in range(0, slots, step):
        out_ref[:, start : start + step] = all_ref[start : start + step, :].T.astype(BF16)


def place_parts(parts, all_ref, columns):
    height = parts[0].shape[0]
    if len(parts) == columns:
        for index, part in enumerate(parts):
            all_ref[index * height : (index + 1) * height, :] = part[...]
        return
    own, far, up, down, ends = parts
    e = lax.axis_index("expert")
    all_ref[0:height, :] = own[...]
    all_ref[2 * height : 3 * height, :] = far[...]
    all_ref[height : 2 * height, :] = jnp.where(e == 0, ends[...], up[...])
    all_ref[3 * height : 4 * height, :] = jnp.where(e == columns - 1, ends[...], down[...])


def combine_kernel(columns, weight_ref, *refs):
    parts, gates = refs[:columns], refs[columns:-3]
    out_ref, total_ref, all_ref = refs[-3:]
    place_parts(parts, all_ref, columns)
    out_ref[...] = jnp.dot(weight_ref[...], all_ref[...], preferred_element_type=F32).astype(BF16)
    total = gates[0][...]
    for gate in gates[1:]:
        total = total + gate[...]
    total_ref[...] = total


def combine_gate_kernel(chips, cores, columns, weight_ref, routes_ref, key_ref, grads_ref, *refs):
    parts, (out_ref, gate_ref, all_ref, sum_ref) = refs[:-4], refs[-4:]
    place_parts(parts, all_ref, columns)
    out_ref[...] = jnp.dot(weight_ref[...], all_ref[...], preferred_element_type=F32).astype(BF16)
    rows = key_ref.shape[1]
    slot = lax.broadcasted_iota(jnp.int32, (CAP, rows), 0).astype(F32)
    routes = routes_ref[...]
    sum_ref[...] = lax.dot_general(all_ref[...], grads_ref[...], CONTRACT_LAST, preferred_element_type=F32)
    total = jnp.zeros(gate_ref.shape, F32)
    for index, expert in enumerate(slot_experts(chips, cores, columns)):
        same = key_ref[pl.ds(expert, 1), :] == slot
        row = jnp.where(same, sum_ref[index * CAP : (index + 1) * CAP, :], 0.0)
        total = total + jnp.where(routes == expert, jnp.sum(row, axis=0, keepdims=True), 0.0)
    gate_ref[...] = total


def body(sizes, tokens, grad_out, routes, gates, gate_weight, up_weight, down_weight):
    n_dp, groups, columns = sizes
    cores = 2 if groups % 2 == 0 else 1
    chips = groups // cores
    experts = groups * columns
    rows, width = tokens.shape
    _, hid_dev, feats = gate_weight.shape
    count = n_dp * chips
    tall = n_dp * CAP
    slots = groups * CAP
    routes_t, gates_t = routes.T, gates.T

    def shape(height, length, dtype=BF16):
        return jax.ShapeDtypeStruct((height, length), dtype)

    def to_core(value, dc):
        if dc == 0:
            return value
        pairs = [(t, t // cores * cores + (t + dc) % cores) for t in range(groups)]
        return lax.ppermute(value, "tensor", pairs)

    def to_chip(value, db, dh):
        if (db, dh) == (0, 0):
            return value
        pairs = []
        for b in range(n_dp):
            for t in range(groups):
                target = (t // cores + dh) % chips * cores + t % cores
                pairs.append((b * groups + t, (b + db) % n_dp * groups + target))
        return lax.ppermute(value, ("dp", "tensor"), pairs)

    hops = [(db, dh) for db in range(n_dp) for dh in range(chips)]
    order = sorted(range(count), key=lambda index: (hops[index][0] == 0, -hops[index][1]))

    def dispatch(pieces):
        arrived = {index: to_chip(pieces[hops[index][1]], *hops[index]) for index in order}
        return [arrived[index] for index in range(count)]

    def give_back(pieces):
        arrived = {index: to_chip(pieces[index], *hops[index]) for index in order}
        return [arrived[index] for index in range(count)]

    def swap(pieces):
        return [to_core(piece, dc) for dc in range(cores) for piece in pieces]

    def add_blocks(pieces):
        return call(
            functools.partial(add_blocks_kernel, chips, cores),
            "add_blocks",
            shape(slots, width),
            pieces,
            2 * slots * width,
        )

    def across(value):
        parts = [value]
        for dz in range(1, columns):
            parts.append(lax.ppermute(value, "expert", [(z, (z + dz) % columns) for z in range(columns)]))
        return parts

    def along(value):
        if columns != 4:
            return across(value)
        far = lax.ppermute(value, "expert", [(z, (z + 2) % columns) for z in range(columns)])
        up = lax.ppermute(value, "expert", [(z, z + 1) for z in range(columns - 1)])
        down = lax.ppermute(value, "expert", [(z + 1, z) for z in range(columns - 1)])
        ends = lax.ppermute(far, "expert", [(2, 3), (1, 0)])
        return [value, far, up, down, ends]

    sources = [to_core(tokens, dc) for dc in range(cores)] + [to_core(grad_out, dc) for dc in range(cores)]
    key = call(number_kernel, "number", shape(experts, rows, F32), [routes_t], EARLY)
    picked = call(
        functools.partial(pick_kernel, cores),
        "pick",
        [shape(2 * CAP, cores * width)] * chips,
        [key, *sources],
        EARLY,
    )
    rows_in = dispatch(picked)

    matmul_flops = 2 * tall * hid_dev * feats
    saved = [shape(tall, hid_dev, F32)] * 2
    piece = [shape(CAP, cores * width)] * count
    act, scale, *outs = call(
        functools.partial(forward_kernel, chips, cores, count),
        "forward",
        saved + piece,
        [*rows_in, gate_weight, up_weight, down_weight],
        3 * matmul_flops,
        [pltpu.VMEM((tall, feats), BF16), pltpu.VMEM((tall, hid_dev), BF16)],
        limit=24,
    )
    out_pieces = give_back(outs)
    backs = call(
        functools.partial(backward_kernel, chips, cores, count),
        "backward",
        piece,
        [*rows_in, gate_weight, up_weight, down_weight, act, scale],
        3 * matmul_flops,
        [pltpu.VMEM((tall, feats), BF16)] + [pltpu.VMEM((tall, hid_dev), BF16)] * 2,
        limit=24,
    )
    out_pieces, backs = after(out_pieces, backs)
    out_rows = add_blocks(swap(out_pieces))
    out_rows, backs = after(out_rows, backs)
    out_parts = along(out_rows)
    back_pieces = give_back(backs)
    back_pieces, out_parts[1:4] = after(back_pieces, out_parts[1:4])
    back_rows = add_blocks(swap(back_pieces))
    back_parts = across(back_rows)
    _, out_parts = after(back_rows, out_parts)

    weight_map = call(
        functools.partial(weights_kernel, chips, cores, columns),
        "weights",
        shape(rows, experts * CAP),
        [routes_t, gates_t, key],
        experts * CAP * rows,
        [pltpu.VMEM((experts, rows), F32), pltpu.VMEM((experts * CAP, rows), F32)],
        limit=16,
    )

    all_rows = pltpu.VMEM((experts * CAP, width), BF16)
    combine_flops = 2 * experts * CAP * rows * width
    mixed, gate_part = call(
        functools.partial(combine_gate_kernel, chips, cores, columns),
        "combine_gate",
        [shape(rows, width), shape(routes_t.shape[0], rows, F32)],
        [weight_map, routes_t, key, grad_out, *out_parts],
        0,
        [all_rows, pltpu.VMEM((experts * CAP, rows), F32)],
        limit=24,
    )
    gate_parts = [gate_part]
    for dt in range(1, groups):
        pairs = [(t, (t + dt) % groups) for t in range(groups)]
        gate_parts.append(lax.ppermute(gate_part, "tensor", pairs))
    grad_tokens, grad_gates = call(
        functools.partial(combine_kernel, columns),
        "combine",
        [shape(rows, width), shape(*gate_part.shape, F32)],
        [weight_map, *back_parts, *gate_parts],
        combine_flops,
        [all_rows],
        limit=16,
    )
    return (mixed, grad_tokens, grad_gates.T)


def solution(mesh):
    sizes = (mesh.shape["dp"], mesh.shape["tensor"], mesh.shape["expert"])
    return jax.shard_map(
        functools.partial(body, sizes),
        mesh=mesh,
        in_specs=(
            P("dp", "tensor"),
            P("dp", "tensor"),
            P("dp", None),
            P("dp", None),
            P(("expert", "tensor"), "dp", None),
            P(("expert", "tensor"), "dp", None),
            P(("expert", "tensor"), "dp", None),
        ),
        out_specs=(P("dp", "tensor"), P("dp", "tensor"), P("dp", None)),
        check_vma=False,
    )
```

```python
import functools

import jax
import jax.numpy as jnp
from jax import lax
from jax.experimental import pallas as pl
from jax.experimental.pallas import tpu as pltpu
from jax.sharding import PartitionSpec as P

CAP = 48
LANES = 128
MIB = 2**20
EARLY = 6e9
BF16 = jnp.bfloat16
F32 = jnp.float32
CONTRACT_LAST = (((1,), (1,)), ((), ()))


def call(kernel, name, out_shape, operands, flops, scratch=(), limit=8):
    outs = out_shape if isinstance(out_shape, list) else [out_shape]
    moved = sum(a.size * a.dtype.itemsize for a in [*operands, *outs])
    spec = pl.BlockSpec(memory_space=pltpu.VMEM)
    return pl.pallas_call(
        kernel,
        out_shape=out_shape,
        in_specs=[spec] * len(operands),
        out_specs=[spec] * len(outs) if isinstance(out_shape, list) else spec,
        scratch_shapes=list(scratch),
        compiler_params=pltpu.CompilerParams(vmem_limit_bytes=limit * MIB),
        cost_estimate=pl.CostEstimate(flops=int(flops), bytes_accessed=int(moved), transcendentals=0),
        name=name,
    )(*operands)


def after(values, earlier):
    return lax.optimization_barrier((values, earlier))


def number_kernel(routes_ref, key_ref):
    experts, rows = key_ref.shape
    ids = lax.broadcasted_iota(jnp.int32, (experts, rows), 0)
    hit = jnp.zeros((experts, rows), F32)
    for r in range(routes_ref.shape[0]):
        hit = hit + (routes_ref[r : r + 1, :] == ids).astype(F32)
    before = (
        lax.broadcasted_iota(jnp.int32, (LANES, LANES), 0) < lax.broadcasted_iota(jnp.int32, (LANES, LANES), 1)
    ).astype(BF16)
    offset = jnp.zeros((experts, 1), F32)
    for start in range(0, rows, LANES):
        part = hit[:, start : start + LANES]
        rank = jnp.dot(part.astype(BF16), before, preferred_element_type=F32) + offset
        offset = offset + jnp.sum(part, axis=1, keepdims=True)
        key_ref[:, start : start + LANES] = jnp.where(part > 0.0, rank, -1.0)


def position(cores):
    t = lax.axis_index("tensor")
    return lax.div(t, cores), lax.rem(t, cores), lax.axis_index("expert")


def pick_kernel(cores, key_ref, *refs):
    sources, pieces = refs[:cores], refs[cores:]
    chips = len(pieces)
    rows, width = sources[0].shape
    chip, core, e = position(cores)
    slot = lax.broadcasted_iota(jnp.int32, (CAP, rows), 0).astype(F32)
    masks = []
    for dh in range(chips):
        expert = (e * chips + lax.rem(chip + dh, chips)) * cores + core
        masks.append((key_ref[pl.ds(expert, 1), :] == slot).astype(BF16))
    mask = jnp.concatenate(masks, axis=0)
    for dc, source in enumerate(sources):
        picked = jnp.dot(mask, source[...], preferred_element_type=F32).astype(BF16)
        column = pl.multiple_of(lax.rem(core - dc + cores, cores) * width, width)
        for dh, piece in enumerate(pieces):
            piece[:, pl.ds(column, width)] = picked[dh * CAP : (dh + 1) * CAP]


def gather_pieces(x_ref, pieces, chips, cores):
    chip, _, _ = position(cores)
    width = pieces[0].shape[1]
    for index, piece in enumerate(pieces):
        db, dh = divmod(index, chips)
        column = pl.multiple_of(lax.rem(chip - dh + chips, chips) * width, width)
        x_ref[db * CAP : (db + 1) * CAP, pl.ds(column, width)] = piece[...]


def project_back(terms, pieces, chips, cores):
    chip, _, _ = position(cores)
    blocks = len(pieces) // chips
    width = pieces[0].shape[1]
    for dh in range(chips):
        column = pl.ds(pl.multiple_of(lax.rem(chip + dh, chips) * width, width), width)
        total = None
        for h_ref, w_ref in terms:
            term = jnp.dot(h_ref[...], w_ref[0, :, column], preferred_element_type=F32)
            total = term if total is None else total + term
        total = total.astype(BF16)
        for db in range(blocks):
            row = (-db) % blocks * CAP
            pieces[db * chips + dh][...] = total[row : row + CAP]


def chunks_of(hid_dev):
    size = 256 if hid_dev % 256 == 0 else hid_dev
    return [slice(start, start + size) for start in range(0, hid_dev, size)]


def forward_kernel(chips, cores, count, *refs):
    pieces, (gate_ref, up_ref, down_ref) = refs[:count], refs[count : count + 3]
    act_ref, scale_ref = refs[count + 3 : count + 5]
    outs, (x_ref, hid_ref) = refs[count + 5 : 2 * count + 5], refs[2 * count + 5 :]
    gather_pieces(x_ref, pieces, chips, cores)
    for part in chunks_of(gate_ref.shape[1]):
        gate_pre = lax.dot_general(x_ref[...], gate_ref[0, part, :], CONTRACT_LAST, preferred_element_type=F32)
        up_pre = lax.dot_general(x_ref[...], up_ref[0, part, :], CONTRACT_LAST, preferred_element_type=F32)
        sig = jax.nn.sigmoid(gate_pre)
        act = gate_pre * sig
        hid_ref[:, part] = (act * up_pre).astype(BF16)
        act_ref[:, part] = act
        scale_ref[:, part] = up_pre * (sig * (1.0 + gate_pre * (1.0 - sig)))
    project_back([(hid_ref, down_ref)], outs, chips, cores)


def backward_kernel(chips, cores, count, *refs):
    pieces, (gate_ref, up_ref, down_ref) = refs[:count], refs[count : count + 3]
    act_ref, scale_ref = refs[count + 3 : count + 5]
    outs, (x_ref, grad_gate_ref, grad_up_ref) = refs[count + 5 : 2 * count + 5], refs[2 * count + 5 :]
    gather_pieces(x_ref, pieces, chips, cores)
    for part in chunks_of(gate_ref.shape[1]):
        grad_hid = lax.dot_general(x_ref[...], down_ref[0, part, :], CONTRACT_LAST, preferred_element_type=F32)
        grad_gate_ref[:, part] = (grad_hid * scale_ref[:, part]).astype(BF16)
        grad_up_ref[:, part] = (grad_hid * act_ref[:, part]).astype(BF16)
    project_back([(grad_gate_ref, gate_ref), (grad_up_ref, up_ref)], outs, chips, cores)


def add_blocks_kernel(chips, cores, *refs):
    pieces, out_ref = refs[:-1], refs[-1]
    width = out_ref.shape[1]
    count = len(pieces) // cores
    _, core, _ = position(cores)
    column = pl.ds(pl.multiple_of(core * width, width), width)
    for dh in range(chips):
        for dc in range(cores):
            total = None
            for piece in pieces[dc * count + dh : (dc + 1) * count : chips]:
                term = piece[:, column].astype(F32)
                total = term if total is None else total + term
            row = (dh * cores + dc) * CAP
            out_ref[row : row + CAP, :] = total.astype(BF16)


def slot_experts(chips, cores, columns):
    chip, core, e = position(cores)
    experts = []
    for dz in range(columns):
        for dh in range(chips):
            for dc in range(cores):
                column = lax.rem(e - dz + columns, columns)
                owner = lax.rem(chip - dh + chips, chips)
                experts.append((column * chips + owner) * cores + lax.rem(core - dc + cores, cores))
    return experts


def weights_kernel(chips, cores, columns, routes_ref, gates_ref, key_ref, out_ref, gate_ref, all_ref):
    experts, rows = key_ref.shape
    ids = lax.broadcasted_iota(jnp.int32, (experts, rows), 0)
    gate = jnp.zeros((experts, rows), F32)
    for r in range(routes_ref.shape[0]):
        gate = gate + jnp.where(routes_ref[r : r + 1, :] == ids, gates_ref[r : r + 1, :], 0.0)
    gate_ref[...] = gate
    slot = lax.broadcasted_iota(jnp.int32, (CAP, rows), 0).astype(F32)
    for index, expert in enumerate(slot_experts(chips, cores, columns)):
        same = key_ref[pl.ds(expert, 1), :] == slot
        all_ref[index * CAP : (index + 1) * CAP, :] = jnp.where(same, gate_ref[pl.ds(expert, 1), :], 0.0)
    slots = all_ref.shape[0]
    step = LANES if slots % LANES == 0 else slots
    for start in range(0, slots, step):
        out_ref[:, start : start + step] = all_ref[start : start + step, :].T.astype(BF16)


def place_parts(parts, all_ref, columns):
    height = parts[0].shape[0]
    if len(parts) == columns:
        for index, part in enumerate(parts):
            all_ref[index * height : (index + 1) * height, :] = part[...]
        return
    own, far, up, down, ends = parts
    e = lax.axis_index("expert")
    all_ref[0:height, :] = own[...]
    all_ref[2 * height : 3 * height, :] = far[...]
    all_ref[height : 2 * height, :] = jnp.where(e == 0, ends[...], up[...])
    all_ref[3 * height : 4 * height, :] = jnp.where(e == columns - 1, ends[...], down[...])


def combine_kernel(columns, weight_ref, *refs):
    parts, gates = refs[:columns], refs[columns:-3]
    out_ref, total_ref, all_ref = refs[-3:]
    place_parts(parts, all_ref, columns)
    out_ref[...] = jnp.dot(weight_ref[...], all_ref[...], preferred_element_type=F32).astype(BF16)
    total = gates[0][...]
    for gate in gates[1:]:
        total = total + gate[...]
    total_ref[...] = total


def combine_gate_kernel(chips, cores, columns, weight_ref, routes_ref, key_ref, grads_ref, *refs):
    parts, (out_ref, gate_ref, all_ref, sum_ref) = refs[:-4], refs[-4:]
    place_parts(parts, all_ref, columns)
    out_ref[...] = jnp.dot(weight_ref[...], all_ref[...], preferred_element_type=F32).astype(BF16)
    rows = key_ref.shape[1]
    slot = lax.broadcasted_iota(jnp.int32, (CAP, rows), 0).astype(F32)
    routes = routes_ref[...]
    sum_ref[...] = lax.dot_general(all_ref[...], grads_ref[...], CONTRACT_LAST, preferred_element_type=F32)
    total = jnp.zeros(gate_ref.shape, F32)
    for index, expert in enumerate(slot_experts(chips, cores, columns)):
        same = key_ref[pl.ds(expert, 1), :] == slot
        row = jnp.where(same, sum_ref[index * CAP : (index + 1) * CAP, :], 0.0)
        total = total + jnp.where(routes == expert, jnp.sum(row, axis=0, keepdims=True), 0.0)
    gate_ref[...] = total


def body(sizes, tokens, grad_out, routes, gates, gate_weight, up_weight, down_weight):
    n_dp, groups, columns = sizes
    cores = 2 if groups % 2 == 0 else 1
    chips = groups // cores
    experts = groups * columns
    rows, width = tokens.shape
    _, hid_dev, feats = gate_weight.shape
    count = n_dp * chips
    tall = n_dp * CAP
    slots = groups * CAP
    routes_t, gates_t = routes.T, gates.T

    def shape(height, length, dtype=BF16):
        return jax.ShapeDtypeStruct((height, length), dtype)

    def to_core(value, dc):
        if dc == 0:
            return value
        pairs = [(t, t // cores * cores + (t + dc) % cores) for t in range(groups)]
        return lax.ppermute(value, "tensor", pairs)

    def to_chip(value, db, dh):
        if (db, dh) == (0, 0):
            return value
        pairs = []
        for b in range(n_dp):
            for t in range(groups):
                target = (t // cores + dh) % chips * cores + t % cores
                pairs.append((b * groups + t, (b + db) % n_dp * groups + target))
        return lax.ppermute(value, ("dp", "tensor"), pairs)

    hops = [(db, dh) for db in range(n_dp) for dh in range(chips)]
    first = (n_dp - 1) * chips
    order = sorted(range(count), key=lambda index: (hops[index][0] == 0, -hops[index][1]))

    def dispatch(pieces):
        arrived = {index: to_chip(pieces[hops[index][1]], *hops[index]) for index in order}
        return [arrived[index] for index in range(count)]

    def give_back(pieces):
        arrived = {index: to_chip(pieces[index], *hops[index]) for index in order}
        return [arrived[index] for index in range(count)]

    def swap(pieces):
        return [to_core(piece, dc) for dc in range(cores) for piece in pieces]

    def add_blocks(pieces):
        return call(
            functools.partial(add_blocks_kernel, chips, cores),
            "add_blocks",
            shape(slots, width),
            pieces,
            2 * slots * width,
        )

    def across(value):
        parts = [value]
        for dz in range(1, columns):
            parts.append(lax.ppermute(value, "expert", [(z, (z + dz) % columns) for z in range(columns)]))
        return parts

    def along(value):
        if columns != 4:
            return across(value)
        far = lax.ppermute(value, "expert", [(z, (z + 2) % columns) for z in range(columns)])
        up = lax.ppermute(value, "expert", [(z, z + 1) for z in range(columns - 1)])
        down = lax.ppermute(value, "expert", [(z + 1, z) for z in range(columns - 1)])
        ends = lax.ppermute(far, "expert", [(2, 3), (1, 0)])
        return [value, far, up, down, ends]

    def pick(key, sources):
        return call(
            functools.partial(pick_kernel, cores),
            "pick",
            [shape(CAP, cores * width)] * chips,
            [key, *sources],
            EARLY,
        )

    token_sources = [to_core(tokens, dc) for dc in range(cores)]
    grad_sources = [to_core(grad_out, dc) for dc in range(cores)]
    key = call(number_kernel, "number", shape(experts, rows, F32), [routes_t], EARLY)
    tok_in = dispatch(pick(key, token_sources))
    tok_in[0], grad_pieces = lax.optimization_barrier((tok_in[0], pick(key, grad_sources)))
    grad_in = dispatch(grad_pieces)

    matmul_flops = 2 * tall * hid_dev * feats
    saved = [shape(tall, hid_dev, F32)] * 2
    piece = [shape(CAP, cores * width)] * count
    act, scale, *outs = call(
        functools.partial(forward_kernel, chips, cores, count),
        "forward",
        saved + piece,
        [*tok_in, gate_weight, up_weight, down_weight],
        3 * matmul_flops,
        [pltpu.VMEM((tall, feats), BF16), pltpu.VMEM((tall, hid_dev), BF16)],
        limit=24,
    )
    outs, grad_in = after(outs, grad_in)
    out_pieces = give_back(outs)
    backs = call(
        functools.partial(backward_kernel, chips, cores, count),
        "backward",
        piece,
        [*grad_in, gate_weight, up_weight, down_weight, act, scale],
        3 * matmul_flops,
        [pltpu.VMEM((tall, feats), BF16)] + [pltpu.VMEM((tall, hid_dev), BF16)] * 2,
        limit=24,
    )
    out_pieces[first], backs = after(out_pieces[first], backs)
    out_rows = add_blocks(swap(out_pieces))
    out_rows, backs = after(out_rows, backs)
    out_parts = along(out_rows)
    back_pieces = give_back(backs)
    back_pieces[0], out_parts[1:4] = after(back_pieces[0], out_parts[1:4])
    back_rows = add_blocks(swap(back_pieces))
    back_parts = across(back_rows)
    _, out_parts = after(back_rows, out_parts)

    weight_map = call(
        functools.partial(weights_kernel, chips, cores, columns),
        "weights",
        shape(rows, experts * CAP),
        [routes_t, gates_t, key],
        experts * CAP * rows,
        [pltpu.VMEM((experts, rows), F32), pltpu.VMEM((experts * CAP, rows), F32)],
        limit=16,
    )

    all_rows = pltpu.VMEM((experts * CAP, width), BF16)
    combine_flops = 2 * experts * CAP * rows * width
    mixed, gate_part = call(
        functools.partial(combine_gate_kernel, chips, cores, columns),
        "combine_gate",
        [shape(rows, width), shape(routes_t.shape[0], rows, F32)],
        [weight_map, routes_t, key, grad_out, *out_parts],
        0,
        [all_rows, pltpu.VMEM((experts * CAP, rows), F32)],
        limit=24,
    )
    gate_parts = [gate_part]
    for dt in range(1, groups):
        pairs = [(t, (t + dt) % groups) for t in range(groups)]
        gate_parts.append(lax.ppermute(gate_part, "tensor", pairs))
    grad_tokens, grad_gates = call(
        functools.partial(combine_kernel, columns),
        "combine",
        [shape(rows, width), shape(*gate_part.shape, F32)],
        [weight_map, *back_parts, *gate_parts],
        combine_flops,
        [all_rows],
        limit=16,
    )
    return (mixed, grad_tokens, grad_gates.T)


def solution(mesh):
    sizes = (mesh.shape["dp"], mesh.shape["tensor"], mesh.shape["expert"])
    return jax.shard_map(
        functools.partial(body, sizes),
        mesh=mesh,
        in_specs=(
            P("dp", "tensor"),
            P("dp", "tensor"),
            P("dp", None),
            P("dp", None),
            P(("expert", "tensor"), "dp", None),
            P(("expert", "tensor"), "dp", None),
            P(("expert", "tensor"), "dp", None),
        ),
        out_specs=(P("dp", "tensor"), P("dp", "tensor"), P("dp", None)),
        check_vma=False,
    )
```

```python
import functools

import jax
import jax.numpy as jnp
from jax import lax
from jax.experimental import pallas as pl
from jax.experimental.pallas import tpu as pltpu
from jax.sharding import PartitionSpec as P

CAP = 48
LANES = 128
MIB = 2**20
EARLY = 6e9
BF16 = jnp.bfloat16
F32 = jnp.float32
CONTRACT_LAST = (((1,), (1,)), ((), ()))


def call(kernel, name, out_shape, operands, flops, scratch=(), limit=8):
    outs = out_shape if isinstance(out_shape, list) else [out_shape]
    moved = sum(a.size * a.dtype.itemsize for a in [*operands, *outs])
    spec = pl.BlockSpec(memory_space=pltpu.VMEM)
    return pl.pallas_call(
        kernel,
        out_shape=out_shape,
        in_specs=[spec] * len(operands),
        out_specs=[spec] * len(outs) if isinstance(out_shape, list) else spec,
        scratch_shapes=list(scratch),
        compiler_params=pltpu.CompilerParams(vmem_limit_bytes=limit * MIB),
        cost_estimate=pl.CostEstimate(flops=int(flops), bytes_accessed=int(moved), transcendentals=0),
        name=name,
    )(*operands)


def after(values, earlier):
    return lax.optimization_barrier((values, earlier))


def number_kernel(routes_ref, key_ref):
    experts, rows = key_ref.shape
    ids = lax.broadcasted_iota(jnp.int32, (experts, rows), 0)
    hit = jnp.zeros((experts, rows), F32)
    for r in range(routes_ref.shape[0]):
        hit = hit + (routes_ref[r : r + 1, :] == ids).astype(F32)
    before = (
        lax.broadcasted_iota(jnp.int32, (LANES, LANES), 0) < lax.broadcasted_iota(jnp.int32, (LANES, LANES), 1)
    ).astype(BF16)
    offset = jnp.zeros((experts, 1), F32)
    for start in range(0, rows, LANES):
        part = hit[:, start : start + LANES]
        rank = jnp.dot(part.astype(BF16), before, preferred_element_type=F32) + offset
        offset = offset + jnp.sum(part, axis=1, keepdims=True)
        key_ref[:, start : start + LANES] = jnp.where(part > 0.0, rank, -1.0)


def position(cores):
    t = lax.axis_index("tensor")
    return lax.div(t, cores), lax.rem(t, cores), lax.axis_index("expert")


def pick_kernel(cores, key_ref, *refs):
    sources, pieces = refs[:cores], refs[cores:]
    chips = len(pieces)
    rows, width = sources[0].shape
    chip, core, e = position(cores)
    slot = lax.broadcasted_iota(jnp.int32, (CAP, rows), 0).astype(F32)
    masks = []
    for dh in range(chips):
        expert = (e * chips + lax.rem(chip + dh, chips)) * cores + core
        masks.append((key_ref[pl.ds(expert, 1), :] == slot).astype(BF16))
    mask = jnp.concatenate(masks, axis=0)
    for dc, source in enumerate(sources):
        picked = jnp.dot(mask, source[...], preferred_element_type=F32).astype(BF16)
        column = pl.multiple_of(lax.rem(core - dc + cores, cores) * width, width)
        for dh, piece in enumerate(pieces):
            piece[:, pl.ds(column, width)] = picked[dh * CAP : (dh + 1) * CAP]


def gather_pieces(x_ref, pieces, chips, cores):
    chip, _, _ = position(cores)
    width = pieces[0].shape[1]
    for index, piece in enumerate(pieces):
        db, dh = divmod(index, chips)
        column = pl.multiple_of(lax.rem(chip - dh + chips, chips) * width, width)
        x_ref[db * CAP : (db + 1) * CAP, pl.ds(column, width)] = piece[...]


def project_back(terms, pieces, chips, cores):
    chip, _, _ = position(cores)
    blocks = len(pieces) // chips
    width = pieces[0].shape[1]
    for dh in range(chips):
        column = pl.ds(pl.multiple_of(lax.rem(chip + dh, chips) * width, width), width)
        total = None
        for h_ref, w_ref in terms:
            term = jnp.dot(h_ref[...], w_ref[0, :, column], preferred_element_type=F32)
            total = term if total is None else total + term
        total = total.astype(BF16)
        for db in range(blocks):
            row = (-db) % blocks * CAP
            pieces[db * chips + dh][...] = total[row : row + CAP]


def chunks_of(hid_dev):
    size = 256 if hid_dev % 256 == 0 else hid_dev
    return [slice(start, start + size) for start in range(0, hid_dev, size)]


def forward_kernel(chips, cores, count, *refs):
    pieces, (gate_ref, up_ref, down_ref) = refs[:count], refs[count : count + 3]
    act_ref, scale_ref = refs[count + 3 : count + 5]
    outs, (x_ref, hid_ref) = refs[count + 5 : 2 * count + 5], refs[2 * count + 5 :]
    gather_pieces(x_ref, pieces, chips, cores)
    for part in chunks_of(gate_ref.shape[1]):
        gate_pre = lax.dot_general(x_ref[...], gate_ref[0, part, :], CONTRACT_LAST, preferred_element_type=F32)
        up_pre = lax.dot_general(x_ref[...], up_ref[0, part, :], CONTRACT_LAST, preferred_element_type=F32)
        sig = jax.nn.sigmoid(gate_pre)
        act = gate_pre * sig
        hid_ref[:, part] = (act * up_pre).astype(BF16)
        act_ref[:, part] = act
        scale_ref[:, part] = up_pre * (sig * (1.0 + gate_pre * (1.0 - sig)))
    project_back([(hid_ref, down_ref)], outs, chips, cores)


def backward_kernel(chips, cores, count, *refs):
    pieces, (gate_ref, up_ref, down_ref) = refs[:count], refs[count : count + 3]
    act_ref, scale_ref = refs[count + 3 : count + 5]
    outs, (x_ref, grad_gate_ref, grad_up_ref) = refs[count + 5 : 2 * count + 5], refs[2 * count + 5 :]
    gather_pieces(x_ref, pieces, chips, cores)
    for part in chunks_of(gate_ref.shape[1]):
        grad_hid = lax.dot_general(x_ref[...], down_ref[0, part, :], CONTRACT_LAST, preferred_element_type=F32)
        grad_gate_ref[:, part] = (grad_hid * scale_ref[:, part]).astype(BF16)
        grad_up_ref[:, part] = (grad_hid * act_ref[:, part]).astype(BF16)
    project_back([(grad_gate_ref, gate_ref), (grad_up_ref, up_ref)], outs, chips, cores)


def add_blocks_kernel(chips, cores, *refs):
    pieces, out_ref = refs[:-1], refs[-1]
    width = out_ref.shape[1]
    count = len(pieces) // cores
    _, core, _ = position(cores)
    column = pl.ds(pl.multiple_of(core * width, width), width)
    for dh in range(chips):
        for dc in range(cores):
            total = None
            for piece in pieces[dc * count + dh : (dc + 1) * count : chips]:
                term = piece[:, column].astype(F32)
                total = term if total is None else total + term
            row = (dh * cores + dc) * CAP
            out_ref[row : row + CAP, :] = total.astype(BF16)


def partner_column(e, dz, columns):
    if columns & (columns - 1) == 0:
        return e ^ dz
    return (e - dz + columns) % columns


def slot_experts(chips, cores, columns):
    chip, core, e = position(cores)
    experts = []
    for dz in range(columns):
        for dh in range(chips):
            for dc in range(cores):
                column = partner_column(e, dz, columns)
                owner = lax.rem(chip - dh + chips, chips)
                experts.append((column * chips + owner) * cores + lax.rem(core - dc + cores, cores))
    return experts


def weights_kernel(chips, cores, columns, routes_ref, gates_ref, key_ref, out_ref, gate_ref, all_ref):
    experts, rows = key_ref.shape
    ids = lax.broadcasted_iota(jnp.int32, (experts, rows), 0)
    gate = jnp.zeros((experts, rows), F32)
    for r in range(routes_ref.shape[0]):
        gate = gate + jnp.where(routes_ref[r : r + 1, :] == ids, gates_ref[r : r + 1, :], 0.0)
    gate_ref[...] = gate
    slot = lax.broadcasted_iota(jnp.int32, (CAP, rows), 0).astype(F32)
    for index, expert in enumerate(slot_experts(chips, cores, columns)):
        same = key_ref[pl.ds(expert, 1), :] == slot
        all_ref[index * CAP : (index + 1) * CAP, :] = jnp.where(same, gate_ref[pl.ds(expert, 1), :], 0.0)
    slots = all_ref.shape[0]
    step = LANES if slots % LANES == 0 else slots
    for start in range(0, slots, step):
        out_ref[:, start : start + step] = all_ref[start : start + step, :].T.astype(BF16)


def place_parts(parts, all_ref):
    height = parts[0].shape[0]
    for index, part in enumerate(parts):
        all_ref[index * height : (index + 1) * height, :] = part[...]


def combine_kernel(columns, weight_ref, *refs):
    parts, gates = refs[:columns], refs[columns:-3]
    out_ref, total_ref, all_ref = refs[-3:]
    place_parts(parts, all_ref)
    out_ref[...] = jnp.dot(weight_ref[...], all_ref[...], preferred_element_type=F32).astype(BF16)
    total = gates[0][...]
    for gate in gates[1:]:
        total = total + gate[...]
    total_ref[...] = total


def combine_gate_kernel(chips, cores, columns, weight_ref, routes_ref, key_ref, grads_ref, *refs):
    parts, (out_ref, gate_ref, all_ref, sum_ref) = refs[:-4], refs[-4:]
    place_parts(parts, all_ref)
    out_ref[...] = jnp.dot(weight_ref[...], all_ref[...], preferred_element_type=F32).astype(BF16)
    rows = key_ref.shape[1]
    slot = lax.broadcasted_iota(jnp.int32, (CAP, rows), 0).astype(F32)
    routes = routes_ref[...]
    sum_ref[...] = lax.dot_general(all_ref[...], grads_ref[...], CONTRACT_LAST, preferred_element_type=F32)
    total = jnp.zeros(gate_ref.shape, F32)
    for index, expert in enumerate(slot_experts(chips, cores, columns)):
        same = key_ref[pl.ds(expert, 1), :] == slot
        row = jnp.where(same, sum_ref[index * CAP : (index + 1) * CAP, :], 0.0)
        total = total + jnp.where(routes == expert, jnp.sum(row, axis=0, keepdims=True), 0.0)
    gate_ref[...] = total


def body(sizes, tokens, grad_out, routes, gates, gate_weight, up_weight, down_weight):
    n_dp, groups, columns = sizes
    cores = 2 if groups % 2 == 0 else 1
    chips = groups // cores
    experts = groups * columns
    rows, width = tokens.shape
    _, hid_dev, feats = gate_weight.shape
    count = n_dp * chips
    tall = n_dp * CAP
    slots = groups * CAP
    routes_t, gates_t = routes.T, gates.T

    def shape(height, length, dtype=BF16):
        return jax.ShapeDtypeStruct((height, length), dtype)

    def to_core(value, dc):
        if dc == 0:
            return value
        pairs = [(t, t // cores * cores + (t + dc) % cores) for t in range(groups)]
        return lax.ppermute(value, "tensor", pairs)

    def to_chip(value, db, dh):
        if (db, dh) == (0, 0):
            return value
        pairs = []
        for b in range(n_dp):
            for t in range(groups):
                target = (t // cores + dh) % chips * cores + t % cores
                pairs.append((b * groups + t, (b + db) % n_dp * groups + target))
        return lax.ppermute(value, ("dp", "tensor"), pairs)

    hops = [(db, dh) for db in range(n_dp) for dh in range(chips)]
    first = (n_dp - 1) * chips
    order = sorted(range(count), key=lambda index: (hops[index][0] == 0, -hops[index][1]))

    def dispatch(pieces):
        arrived = {index: to_chip(pieces[hops[index][1]], *hops[index]) for index in order}
        return [arrived[index] for index in range(count)]

    def give_back(pieces):
        arrived = {index: to_chip(pieces[index], *hops[index]) for index in order}
        return [arrived[index] for index in range(count)]

    def swap(pieces):
        return [to_core(piece, dc) for dc in range(cores) for piece in pieces]

    def add_blocks(pieces):
        return call(
            functools.partial(add_blocks_kernel, chips, cores),
            "add_blocks",
            shape(slots, width),
            pieces,
            2 * slots * width,
        )

    def across(parts, dz):
        if columns & (columns - 1) == 0:
            hop = dz & -dz
            return lax.ppermute(parts[dz - hop], "expert", [(z, z ^ hop) for z in range(columns)])
        return lax.ppermute(parts[0], "expert", [(z, (z + dz) % columns) for z in range(columns)])

    direct = [dz for dz in range(1, columns) if dz & (dz - 1) == 0][::-1]
    later = [dz for dz in range(1, columns) if dz not in direct]

    def pick(key, sources):
        return call(
            functools.partial(pick_kernel, cores),
            "pick",
            [shape(CAP, cores * width)] * chips,
            [key, *sources],
            EARLY,
        )

    token_sources = [to_core(tokens, dc) for dc in range(cores)]
    grad_sources = [to_core(grad_out, dc) for dc in range(cores)]
    key = call(number_kernel, "number", shape(experts, rows, F32), [routes_t], EARLY)
    tok_in = dispatch(pick(key, token_sources))
    tok_in[0], grad_pieces = lax.optimization_barrier((tok_in[0], pick(key, grad_sources)))
    grad_in = dispatch(grad_pieces)

    matmul_flops = 2 * tall * hid_dev * feats
    saved = [shape(tall, hid_dev, F32)] * 2
    piece = [shape(CAP, cores * width)] * count
    act, scale, *outs = call(
        functools.partial(forward_kernel, chips, cores, count),
        "forward",
        saved + piece,
        [*tok_in, gate_weight, up_weight, down_weight],
        3 * matmul_flops,
        [pltpu.VMEM((tall, feats), BF16), pltpu.VMEM((tall, hid_dev), BF16)],
        limit=24,
    )
    outs, grad_in = after(outs, grad_in)
    out_pieces = give_back(outs)
    backs = call(
        functools.partial(backward_kernel, chips, cores, count),
        "backward",
        piece,
        [*grad_in, gate_weight, up_weight, down_weight, act, scale],
        3 * matmul_flops,
        [pltpu.VMEM((tall, feats), BF16)] + [pltpu.VMEM((tall, hid_dev), BF16)] * 2,
        limit=24,
    )
    out_pieces[first], backs = after(out_pieces[first], backs)
    out_rows = add_blocks(swap(out_pieces))
    out_rows, backs = after(out_rows, backs)
    out_parts = {0: out_rows}
    for dz in direct:
        out_parts[dz] = across(out_parts, dz)
    back_pieces = give_back(backs)
    back_pieces[0], out_parts = after(back_pieces[0], out_parts)
    for dz in later:
        out_parts[dz] = across(out_parts, dz)
    back_rows = add_blocks(swap(back_pieces))
    back_parts = {0: back_rows}
    for dz in direct:
        back_parts[dz] = across(back_parts, dz)
    _, out_parts = after(back_rows, out_parts)

    weight_map = call(
        functools.partial(weights_kernel, chips, cores, columns),
        "weights",
        shape(rows, experts * CAP),
        [routes_t, gates_t, key],
        experts * CAP * rows,
        [pltpu.VMEM((experts, rows), F32), pltpu.VMEM((experts * CAP, rows), F32)],
        limit=16,
    )

    all_rows = pltpu.VMEM((experts * CAP, width), BF16)
    combine_flops = 2 * experts * CAP * rows * width
    mixed, gate_part = call(
        functools.partial(combine_gate_kernel, chips, cores, columns),
        "combine_gate",
        [shape(rows, width), shape(routes_t.shape[0], rows, F32)],
        [weight_map, routes_t, key, grad_out, *[out_parts[dz] for dz in range(columns)]],
        0,
        [all_rows, pltpu.VMEM((experts * CAP, rows), F32)],
        limit=24,
    )
    gate_parts = [gate_part]
    for dt in range(1, groups):
        pairs = [(t, (t + dt) % groups) for t in range(groups)]
        gate_parts.append(lax.ppermute(gate_part, "tensor", pairs))
    back_parts, gate_parts = after(back_parts, gate_parts)
    for dz in later:
        back_parts[dz] = across(back_parts, dz)
    grad_tokens, grad_gates = call(
        functools.partial(combine_kernel, columns),
        "combine",
        [shape(rows, width), shape(*gate_part.shape, F32)],
        [weight_map, *[back_parts[dz] for dz in range(columns)], *gate_parts],
        combine_flops,
        [all_rows],
        limit=16,
    )
    return (mixed, grad_tokens, grad_gates.T)


def solution(mesh):
    sizes = (mesh.shape["dp"], mesh.shape["tensor"], mesh.shape["expert"])
    return jax.shard_map(
        functools.partial(body, sizes),
        mesh=mesh,
        in_specs=(
            P("dp", "tensor"),
            P("dp", "tensor"),
            P("dp", None),
            P("dp", None),
            P(("expert", "tensor"), "dp", None),
            P(("expert", "tensor"), "dp", None),
            P(("expert", "tensor"), "dp", None),
        ),
        out_specs=(P("dp", "tensor"), P("dp", "tensor"), P("dp", None)),
        check_vma=False,
    )
```

```python
import functools

import jax
import jax.numpy as jnp
from jax import lax
from jax.experimental import pallas as pl
from jax.experimental.pallas import tpu as pltpu
from jax.sharding import PartitionSpec as P

CAP = 48
LANES = 128
MIB = 2**20
EARLY = 6e9
BF16 = jnp.bfloat16
F32 = jnp.float32
CONTRACT_LAST = (((1,), (1,)), ((), ()))


def call(kernel, name, out_shape, operands, flops, scratch=(), limit=8):
    outs = out_shape if isinstance(out_shape, list) else [out_shape]
    moved = sum(a.size * a.dtype.itemsize for a in [*operands, *outs])
    spec = pl.BlockSpec(memory_space=pltpu.VMEM)
    return pl.pallas_call(
        kernel,
        out_shape=out_shape,
        in_specs=[spec] * len(operands),
        out_specs=[spec] * len(outs) if isinstance(out_shape, list) else spec,
        scratch_shapes=list(scratch),
        compiler_params=pltpu.CompilerParams(vmem_limit_bytes=limit * MIB),
        cost_estimate=pl.CostEstimate(flops=int(flops), bytes_accessed=int(moved), transcendentals=0),
        name=name,
    )(*operands)


def after(values, earlier):
    return lax.optimization_barrier((values, earlier))


def number_kernel(routes_ref, key_ref):
    experts, rows = key_ref.shape
    ids = lax.broadcasted_iota(jnp.int32, (experts, rows), 0)
    hit = jnp.zeros((experts, rows), F32)
    for r in range(routes_ref.shape[0]):
        hit = hit + (routes_ref[r : r + 1, :] == ids).astype(F32)
    before = (
        lax.broadcasted_iota(jnp.int32, (LANES, LANES), 0) < lax.broadcasted_iota(jnp.int32, (LANES, LANES), 1)
    ).astype(BF16)
    offset = jnp.zeros((experts, 1), F32)
    for start in range(0, rows, LANES):
        part = hit[:, start : start + LANES]
        rank = jnp.dot(part.astype(BF16), before, preferred_element_type=F32) + offset
        offset = offset + jnp.sum(part, axis=1, keepdims=True)
        key_ref[:, start : start + LANES] = jnp.where(part > 0.0, rank, -1.0)


def position(cores):
    t = lax.axis_index("tensor")
    return lax.div(t, cores), lax.rem(t, cores), lax.axis_index("expert")


def pick_kernel(cores, key_ref, *refs):
    sources, pieces = refs[:cores], refs[cores:]
    chips = len(pieces)
    rows, width = sources[0].shape
    chip, core, e = position(cores)
    slot = lax.broadcasted_iota(jnp.int32, (CAP, rows), 0).astype(F32)
    masks = []
    for dh in range(chips):
        expert = (e * chips + lax.rem(chip + dh, chips)) * cores + core
        masks.append((key_ref[pl.ds(expert, 1), :] == slot).astype(BF16))
    mask = jnp.concatenate(masks, axis=0)
    for dc, source in enumerate(sources):
        picked = jnp.dot(mask, source[...], preferred_element_type=F32).astype(BF16)
        column = pl.multiple_of(lax.rem(core - dc + cores, cores) * width, width)
        for dh, piece in enumerate(pieces):
            piece[:, pl.ds(column, width)] = picked[dh * CAP : (dh + 1) * CAP]


def gather_pieces(x_ref, pieces, chips, cores):
    chip, _, _ = position(cores)
    width = pieces[0].shape[1]
    for index, piece in enumerate(pieces):
        db, dh = divmod(index, chips)
        column = pl.multiple_of(lax.rem(chip - dh + chips, chips) * width, width)
        x_ref[db * CAP : (db + 1) * CAP, pl.ds(column, width)] = piece[...]


def project_back(terms, pieces, chips, cores):
    chip, _, _ = position(cores)
    blocks = len(pieces) // chips
    width = pieces[0].shape[1]
    for dh in range(chips):
        column = pl.ds(pl.multiple_of(lax.rem(chip + dh, chips) * width, width), width)
        total = None
        for h_ref, w_ref in terms:
            term = jnp.dot(h_ref[...], w_ref[0, :, column], preferred_element_type=F32)
            total = term if total is None else total + term
        total = total.astype(BF16)
        for db in range(blocks):
            row = (-db) % blocks * CAP
            pieces[db * chips + dh][...] = total[row : row + CAP]


def chunks_of(hid_dev):
    size = 256 if hid_dev % 256 == 0 else hid_dev
    return [slice(start, start + size) for start in range(0, hid_dev, size)]


def forward_kernel(chips, cores, count, *refs):
    pieces, (gate_ref, up_ref, down_ref) = refs[:count], refs[count : count + 3]
    act_ref, scale_ref = refs[count + 3 : count + 5]
    outs, (x_ref, hid_ref) = refs[count + 5 : 2 * count + 5], refs[2 * count + 5 :]
    gather_pieces(x_ref, pieces, chips, cores)
    for part in chunks_of(gate_ref.shape[1]):
        gate_pre = lax.dot_general(x_ref[...], gate_ref[0, part, :], CONTRACT_LAST, preferred_element_type=F32)
        up_pre = lax.dot_general(x_ref[...], up_ref[0, part, :], CONTRACT_LAST, preferred_element_type=F32)
        sig = jax.nn.sigmoid(gate_pre)
        act = gate_pre * sig
        hid_ref[:, part] = (act * up_pre).astype(BF16)
        act_ref[:, part] = act
        scale_ref[:, part] = up_pre * (sig * (1.0 + gate_pre * (1.0 - sig)))
    project_back([(hid_ref, down_ref)], outs, chips, cores)


def backward_kernel(chips, cores, count, *refs):
    pieces, (gate_ref, up_ref, down_ref) = refs[:count], refs[count : count + 3]
    act_ref, scale_ref = refs[count + 3 : count + 5]
    outs, (x_ref, grad_gate_ref, grad_up_ref) = refs[count + 5 : 2 * count + 5], refs[2 * count + 5 :]
    gather_pieces(x_ref, pieces, chips, cores)
    for part in chunks_of(gate_ref.shape[1]):
        grad_hid = lax.dot_general(x_ref[...], down_ref[0, part, :], CONTRACT_LAST, preferred_element_type=F32)
        grad_gate_ref[:, part] = (grad_hid * scale_ref[:, part]).astype(BF16)
        grad_up_ref[:, part] = (grad_hid * act_ref[:, part]).astype(BF16)
    project_back([(grad_gate_ref, gate_ref), (grad_up_ref, up_ref)], outs, chips, cores)


def add_blocks_kernel(chips, cores, *refs):
    pieces, out_ref = refs[:-1], refs[-1]
    width = out_ref.shape[1]
    count = len(pieces) // cores
    _, core, _ = position(cores)
    column = pl.ds(pl.multiple_of(core * width, width), width)
    for dh in range(chips):
        for dc in range(cores):
            total = None
            for piece in pieces[dc * count + dh : (dc + 1) * count : chips]:
                term = piece[:, column].astype(F32)
                total = term if total is None else total + term
            row = (dh * cores + dc) * CAP
            out_ref[row : row + CAP, :] = total.astype(BF16)


def partner_column(e, dz, columns):
    if columns & (columns - 1) == 0:
        return e ^ dz
    return (e - dz + columns) % columns


def slot_experts(chips, cores, columns):
    chip, core, e = position(cores)
    experts = []
    for dz in range(columns):
        for dh in range(chips):
            for dc in range(cores):
                column = partner_column(e, dz, columns)
                owner = lax.rem(chip - dh + chips, chips)
                experts.append((column * chips + owner) * cores + lax.rem(core - dc + cores, cores))
    return experts


def weights_kernel(chips, cores, columns, routes_ref, gates_ref, key_ref, out_ref, gate_ref, all_ref):
    experts, rows = key_ref.shape
    ids = lax.broadcasted_iota(jnp.int32, (experts, rows), 0)
    gate = jnp.zeros((experts, rows), F32)
    for r in range(routes_ref.shape[0]):
        gate = gate + jnp.where(routes_ref[r : r + 1, :] == ids, gates_ref[r : r + 1, :], 0.0)
    gate_ref[...] = gate
    slot = lax.broadcasted_iota(jnp.int32, (CAP, rows), 0).astype(F32)
    for index, expert in enumerate(slot_experts(chips, cores, columns)):
        same = key_ref[pl.ds(expert, 1), :] == slot
        all_ref[index * CAP : (index + 1) * CAP, :] = jnp.where(same, gate_ref[pl.ds(expert, 1), :], 0.0)
    slots = all_ref.shape[0]
    step = LANES if slots % LANES == 0 else slots
    for start in range(0, slots, step):
        out_ref[:, start : start + step] = all_ref[start : start + step, :].T.astype(BF16)


def place_parts(parts, all_ref):
    height = parts[0].shape[0]
    for index, part in enumerate(parts):
        all_ref[index * height : (index + 1) * height, :] = part[...]


def combine_kernel(columns, weight_ref, *refs):
    parts, gates = refs[:columns], refs[columns:-3]
    out_ref, total_ref, all_ref = refs[-3:]
    place_parts(parts, all_ref)
    out_ref[...] = jnp.dot(weight_ref[...], all_ref[...], preferred_element_type=F32).astype(BF16)
    total = gates[0][...]
    for gate in gates[1:]:
        total = total + gate[...]
    total_ref[...] = total


def combine_gate_kernel(chips, cores, columns, weight_ref, routes_ref, key_ref, grads_ref, *refs):
    parts, (out_ref, gate_ref, all_ref, sum_ref) = refs[:-4], refs[-4:]
    place_parts(parts, all_ref)
    out_ref[...] = jnp.dot(weight_ref[...], all_ref[...], preferred_element_type=F32).astype(BF16)
    rows = key_ref.shape[1]
    slot = lax.broadcasted_iota(jnp.int32, (CAP, rows), 0).astype(F32)
    routes = routes_ref[...]
    sum_ref[...] = lax.dot_general(all_ref[...], grads_ref[...], CONTRACT_LAST, preferred_element_type=F32)
    total = jnp.zeros(gate_ref.shape, F32)
    for index, expert in enumerate(slot_experts(chips, cores, columns)):
        same = key_ref[pl.ds(expert, 1), :] == slot
        row = jnp.where(same, sum_ref[index * CAP : (index + 1) * CAP, :], 0.0)
        total = total + jnp.where(routes == expert, jnp.sum(row, axis=0, keepdims=True), 0.0)
    gate_ref[...] = total


def body(sizes, tokens, grad_out, routes, gates, gate_weight, up_weight, down_weight):
    n_dp, groups, columns = sizes
    cores = 2 if groups % 2 == 0 else 1
    chips = groups // cores
    experts = groups * columns
    rows, width = tokens.shape
    _, hid_dev, feats = gate_weight.shape
    count = n_dp * chips
    tall = n_dp * CAP
    slots = groups * CAP
    routes_t, gates_t = routes.T, gates.T

    def shape(height, length, dtype=BF16):
        return jax.ShapeDtypeStruct((height, length), dtype)

    def to_core(value, dc):
        if dc == 0:
            return value
        pairs = [(t, t // cores * cores + (t + dc) % cores) for t in range(groups)]
        return lax.ppermute(value, "tensor", pairs)

    def to_chip(value, db, dh):
        if (db, dh) == (0, 0):
            return value
        pairs = []
        for b in range(n_dp):
            for t in range(groups):
                target = (t // cores + dh) % chips * cores + t % cores
                pairs.append((b * groups + t, (b + db) % n_dp * groups + target))
        return lax.ppermute(value, ("dp", "tensor"), pairs)

    hops = [(db, dh) for db in range(n_dp) for dh in range(chips)]
    first = (n_dp - 1) * chips
    order = sorted(range(count), key=lambda index: (hops[index][0] == 0, -hops[index][1]))

    def dispatch(pieces):
        arrived = {index: to_chip(pieces[hops[index][1]], *hops[index]) for index in order}
        return [arrived[index] for index in range(count)]

    def give_back(pieces):
        arrived = {index: to_chip(pieces[index], *hops[index]) for index in order}
        return [arrived[index] for index in range(count)]

    def swap(pieces):
        return [to_core(piece, dc) for dc in range(cores) for piece in pieces]

    def add_blocks(pieces):
        return call(
            functools.partial(add_blocks_kernel, chips, cores),
            "add_blocks",
            shape(slots, width),
            pieces,
            2 * slots * width,
        )

    def across(parts, dz, first=0):
        pairs = [(partner_column(z, dz - first, columns), z) for z in range(columns)]
        return lax.ppermute(parts[first], "expert", pairs)

    direct = [dz for dz in range(1, columns) if dz & (dz - 1) == 0][::-1]
    later = [dz for dz in range(1, columns) if dz not in direct]

    def pick(key, sources):
        return call(
            functools.partial(pick_kernel, cores),
            "pick",
            [shape(CAP, cores * width)] * chips,
            [key, *sources],
            EARLY,
        )

    token_sources = [to_core(tokens, dc) for dc in range(cores)]
    grad_sources = [to_core(grad_out, dc) for dc in range(cores)]
    key = call(number_kernel, "number", shape(experts, rows, F32), [routes_t], EARLY)
    tok_in = dispatch(pick(key, token_sources))
    tok_in[0], grad_pieces = lax.optimization_barrier((tok_in[0], pick(key, grad_sources)))
    grad_in = dispatch(grad_pieces)

    matmul_flops = 2 * tall * hid_dev * feats
    saved = [shape(tall, hid_dev, F32)] * 2
    piece = [shape(CAP, cores * width)] * count
    act, scale, *outs = call(
        functools.partial(forward_kernel, chips, cores, count),
        "forward",
        saved + piece,
        [*tok_in, gate_weight, up_weight, down_weight],
        3 * matmul_flops,
        [pltpu.VMEM((tall, feats), BF16), pltpu.VMEM((tall, hid_dev), BF16)],
        limit=24,
    )
    outs, grad_in = after(outs, grad_in)
    out_pieces = give_back(outs)
    backs = call(
        functools.partial(backward_kernel, chips, cores, count),
        "backward",
        piece,
        [*grad_in, gate_weight, up_weight, down_weight, act, scale],
        3 * matmul_flops,
        [pltpu.VMEM((tall, feats), BF16)] + [pltpu.VMEM((tall, hid_dev), BF16)] * 2,
        limit=24,
    )
    out_pieces[first], backs = after(out_pieces[first], backs)
    out_rows = add_blocks(swap(out_pieces))
    out_rows, backs = after(out_rows, backs)
    out_parts = {0: out_rows}
    for dz in direct:
        out_parts[dz] = across(out_parts, dz)
    back_pieces = give_back(backs)
    back_pieces[0], out_parts = after(back_pieces[0], out_parts)
    for dz in later:
        out_parts[dz] = across(out_parts, dz, dz & (dz - 1))
    back_rows = add_blocks(swap(back_pieces))
    back_parts = {0: back_rows}
    for dz in direct + later:
        back_parts[dz] = across(back_parts, dz)
    _, out_parts = after(back_rows, out_parts)

    weight_map = call(
        functools.partial(weights_kernel, chips, cores, columns),
        "weights",
        shape(rows, experts * CAP),
        [routes_t, gates_t, key],
        experts * CAP * rows,
        [pltpu.VMEM((experts, rows), F32), pltpu.VMEM((experts * CAP, rows), F32)],
        limit=16,
    )

    all_rows = pltpu.VMEM((experts * CAP, width), BF16)
    combine_flops = 2 * experts * CAP * rows * width
    mixed, gate_part = call(
        functools.partial(combine_gate_kernel, chips, cores, columns),
        "combine_gate",
        [shape(rows, width), shape(routes_t.shape[0], rows, F32)],
        [weight_map, routes_t, key, grad_out, *[out_parts[dz] for dz in range(columns)]],
        0,
        [all_rows, pltpu.VMEM((experts * CAP, rows), F32)],
        limit=24,
    )
    gate_parts = [gate_part]
    for dt in range(1, groups):
        pairs = [(t, (t + dt) % groups) for t in range(groups)]
        gate_parts.append(lax.ppermute(gate_part, "tensor", pairs))
    grad_tokens, grad_gates = call(
        functools.partial(combine_kernel, columns),
        "combine",
        [shape(rows, width), shape(*gate_part.shape, F32)],
        [weight_map, *[back_parts[dz] for dz in range(columns)], *gate_parts],
        combine_flops,
        [all_rows],
        limit=16,
    )
    return (mixed, grad_tokens, grad_gates.T)


def solution(mesh):
    sizes = (mesh.shape["dp"], mesh.shape["tensor"], mesh.shape["expert"])
    return jax.shard_map(
        functools.partial(body, sizes),
        mesh=mesh,
        in_specs=(
            P("dp", "tensor"),
            P("dp", "tensor"),
            P("dp", None),
            P("dp", None),
            P(("expert", "tensor"), "dp", None),
            P(("expert", "tensor"), "dp", None),
            P(("expert", "tensor"), "dp", None),
        ),
        out_specs=(P("dp", "tensor"), P("dp", "tensor"), P("dp", None)),
        check_vma=False,
    )
```

```python
import functools

import jax
import jax.numpy as jnp
from jax import lax
from jax.experimental import pallas as pl
from jax.experimental.pallas import tpu as pltpu
from jax.sharding import PartitionSpec as P

CAP = 48
LANES = 128
MIB = 2**20
EARLY = 6e9
BF16 = jnp.bfloat16
F32 = jnp.float32
CONTRACT_LAST = (((1,), (1,)), ((), ()))


def call(kernel, name, out_shape, operands, flops, scratch=(), limit=8):
    outs = out_shape if isinstance(out_shape, list) else [out_shape]
    moved = sum(a.size * a.dtype.itemsize for a in [*operands, *outs])
    spec = pl.BlockSpec(memory_space=pltpu.VMEM)
    return pl.pallas_call(
        kernel,
        out_shape=out_shape,
        in_specs=[spec] * len(operands),
        out_specs=[spec] * len(outs) if isinstance(out_shape, list) else spec,
        scratch_shapes=list(scratch),
        compiler_params=pltpu.CompilerParams(vmem_limit_bytes=limit * MIB),
        cost_estimate=pl.CostEstimate(flops=int(flops), bytes_accessed=int(moved), transcendentals=0),
        name=name,
    )(*operands)


def after(values, earlier):
    return lax.optimization_barrier((values, earlier))


def number_kernel(routes_ref, key_ref):
    experts, rows = key_ref.shape
    ids = lax.broadcasted_iota(jnp.int32, (experts, rows), 0)
    hit = jnp.zeros((experts, rows), F32)
    for r in range(routes_ref.shape[0]):
        hit = hit + (routes_ref[r : r + 1, :] == ids).astype(F32)
    before = (
        lax.broadcasted_iota(jnp.int32, (LANES, LANES), 0) < lax.broadcasted_iota(jnp.int32, (LANES, LANES), 1)
    ).astype(BF16)
    offset = jnp.zeros((experts, 1), F32)
    for start in range(0, rows, LANES):
        part = hit[:, start : start + LANES]
        rank = jnp.dot(part.astype(BF16), before, preferred_element_type=F32) + offset
        offset = offset + jnp.sum(part, axis=1, keepdims=True)
        key_ref[:, start : start + LANES] = jnp.where(part > 0.0, rank, -1.0)


def position(cores):
    t = lax.axis_index("tensor")
    return lax.div(t, cores), lax.rem(t, cores), lax.axis_index("expert")


def pick_kernel(cores, key_ref, *refs):
    sources, pieces = refs[:cores], refs[cores:]
    chips = len(pieces)
    rows, width = sources[0].shape
    chip, core, e = position(cores)
    slot = lax.broadcasted_iota(jnp.int32, (CAP, rows), 0).astype(F32)
    masks = []
    for dh in range(chips):
        expert = (e * chips + lax.rem(chip + dh, chips)) * cores + core
        masks.append((key_ref[pl.ds(expert, 1), :] == slot).astype(BF16))
    mask = jnp.concatenate(masks, axis=0)
    for dc, source in enumerate(sources):
        picked = jnp.dot(mask, source[...], preferred_element_type=F32).astype(BF16)
        column = pl.multiple_of(lax.rem(core - dc + cores, cores) * width, width)
        for dh, piece in enumerate(pieces):
            piece[:, pl.ds(column, width)] = picked[dh * CAP : (dh + 1) * CAP]


def gather_pieces(x_ref, pieces, chips, cores):
    chip, _, _ = position(cores)
    width = pieces[0].shape[1]
    for index, piece in enumerate(pieces):
        db, dh = divmod(index, chips)
        column = pl.multiple_of(lax.rem(chip - dh + chips, chips) * width, width)
        x_ref[db * CAP : (db + 1) * CAP, pl.ds(column, width)] = piece[...]


def project_back(terms, pieces, chips, cores):
    chip, _, _ = position(cores)
    blocks = len(pieces) // chips
    width = pieces[0].shape[1]
    for dh in range(chips):
        column = pl.ds(pl.multiple_of(lax.rem(chip + dh, chips) * width, width), width)
        total = None
        for h_ref, w_ref in terms:
            term = jnp.dot(h_ref[...], w_ref[0, :, column], preferred_element_type=F32)
            total = term if total is None else total + term
        total = total.astype(BF16)
        for db in range(blocks):
            row = (-db) % blocks * CAP
            pieces[db * chips + dh][...] = total[row : row + CAP]


def chunks_of(hid_dev):
    size = 256 if hid_dev % 256 == 0 else hid_dev
    return [slice(start, start + size) for start in range(0, hid_dev, size)]


def forward_kernel(chips, cores, count, *refs):
    pieces, (gate_ref, up_ref, down_ref) = refs[:count], refs[count : count + 3]
    act_ref, scale_ref = refs[count + 3 : count + 5]
    outs, (x_ref, hid_ref) = refs[count + 5 : 2 * count + 5], refs[2 * count + 5 :]
    gather_pieces(x_ref, pieces, chips, cores)
    for part in chunks_of(gate_ref.shape[1]):
        gate_pre = lax.dot_general(x_ref[...], gate_ref[0, part, :], CONTRACT_LAST, preferred_element_type=F32)
        up_pre = lax.dot_general(x_ref[...], up_ref[0, part, :], CONTRACT_LAST, preferred_element_type=F32)
        sig = jax.nn.sigmoid(gate_pre)
        act = gate_pre * sig
        hid_ref[:, part] = (act * up_pre).astype(BF16)
        act_ref[:, part] = act
        scale_ref[:, part] = up_pre * (sig * (1.0 + gate_pre * (1.0 - sig)))
    project_back([(hid_ref, down_ref)], outs, chips, cores)


def backward_kernel(chips, cores, count, *refs):
    pieces, (gate_ref, up_ref, down_ref) = refs[:count], refs[count : count + 3]
    act_ref, scale_ref = refs[count + 3 : count + 5]
    outs, (x_ref, grad_gate_ref, grad_up_ref) = refs[count + 5 : 2 * count + 5], refs[2 * count + 5 :]
    gather_pieces(x_ref, pieces, chips, cores)
    for part in chunks_of(gate_ref.shape[1]):
        grad_hid = lax.dot_general(x_ref[...], down_ref[0, part, :], CONTRACT_LAST, preferred_element_type=F32)
        grad_gate_ref[:, part] = (grad_hid * scale_ref[:, part]).astype(BF16)
        grad_up_ref[:, part] = (grad_hid * act_ref[:, part]).astype(BF16)
    project_back([(grad_gate_ref, gate_ref), (grad_up_ref, up_ref)], outs, chips, cores)


def add_blocks_kernel(chips, cores, *refs):
    pieces, out_ref = refs[:-1], refs[-1]
    width = out_ref.shape[1]
    count = len(pieces) // cores
    _, core, _ = position(cores)
    column = pl.ds(pl.multiple_of(core * width, width), width)
    for dh in range(chips):
        for dc in range(cores):
            total = None
            for piece in pieces[dc * count + dh : (dc + 1) * count : chips]:
                term = piece[:, column].astype(F32)
                total = term if total is None else total + term
            row = (dh * cores + dc) * CAP
            out_ref[row : row + CAP, :] = total.astype(BF16)


def partner_column(e, dz, columns):
    if columns & (columns - 1) == 0:
        return e ^ dz
    return (e - dz + columns) % columns


def slot_experts(chips, cores, columns):
    chip, core, e = position(cores)
    experts = []
    for dz in range(columns):
        for dh in range(chips):
            for dc in range(cores):
                column = partner_column(e, dz, columns)
                owner = lax.rem(chip - dh + chips, chips)
                experts.append((column * chips + owner) * cores + lax.rem(core - dc + cores, cores))
    return experts


def weights_kernel(chips, cores, columns, routes_ref, gates_ref, key_ref, out_ref, gate_ref, all_ref):
    experts, rows = key_ref.shape
    ids = lax.broadcasted_iota(jnp.int32, (experts, rows), 0)
    gate = jnp.zeros((experts, rows), F32)
    for r in range(routes_ref.shape[0]):
        gate = gate + jnp.where(routes_ref[r : r + 1, :] == ids, gates_ref[r : r + 1, :], 0.0)
    gate_ref[...] = gate
    slot = lax.broadcasted_iota(jnp.int32, (CAP, rows), 0).astype(F32)
    for index, expert in enumerate(slot_experts(chips, cores, columns)):
        same = key_ref[pl.ds(expert, 1), :] == slot
        all_ref[index * CAP : (index + 1) * CAP, :] = jnp.where(same, gate_ref[pl.ds(expert, 1), :], 0.0)
    slots = all_ref.shape[0]
    step = LANES if slots % LANES == 0 else slots
    for start in range(0, slots, step):
        out_ref[:, start : start + step] = all_ref[start : start + step, :].T.astype(BF16)


def place_parts(parts, all_ref):
    height = parts[0].shape[0]
    for index, part in enumerate(parts):
        all_ref[index * height : (index + 1) * height, :] = part[...]


def combine_kernel(columns, weight_ref, *refs):
    parts, gates = refs[:columns], refs[columns:-3]
    out_ref, total_ref, all_ref = refs[-3:]
    place_parts(parts, all_ref)
    out_ref[...] = jnp.dot(weight_ref[...], all_ref[...], preferred_element_type=F32).astype(BF16)
    total = gates[0][...]
    for gate in gates[1:]:
        total = total + gate[...]
    total_ref[...] = total


def combine_gate_kernel(chips, cores, columns, weight_ref, routes_ref, key_ref, grads_ref, *refs):
    parts, (out_ref, gate_ref, all_ref, sum_ref) = refs[:-4], refs[-4:]
    place_parts(parts, all_ref)
    out_ref[...] = jnp.dot(weight_ref[...], all_ref[...], preferred_element_type=F32).astype(BF16)
    rows = key_ref.shape[1]
    slot = lax.broadcasted_iota(jnp.int32, (CAP, rows), 0).astype(F32)
    routes = routes_ref[...]
    sum_ref[...] = lax.dot_general(all_ref[...], grads_ref[...], CONTRACT_LAST, preferred_element_type=F32)
    total = jnp.zeros(gate_ref.shape, F32)
    for index, expert in enumerate(slot_experts(chips, cores, columns)):
        same = key_ref[pl.ds(expert, 1), :] == slot
        row = jnp.where(same, sum_ref[index * CAP : (index + 1) * CAP, :], 0.0)
        total = total + jnp.where(routes == expert, jnp.sum(row, axis=0, keepdims=True), 0.0)
    gate_ref[...] = total


def body(sizes, tokens, grad_out, routes, gates, gate_weight, up_weight, down_weight):
    n_dp, groups, columns = sizes
    cores = 2 if groups % 2 == 0 else 1
    chips = groups // cores
    experts = groups * columns
    rows, width = tokens.shape
    _, hid_dev, feats = gate_weight.shape
    count = n_dp * chips
    tall = n_dp * CAP
    slots = groups * CAP
    routes_t, gates_t = routes.T, gates.T

    def shape(height, length, dtype=BF16):
        return jax.ShapeDtypeStruct((height, length), dtype)

    def to_core(value, dc):
        if dc == 0:
            return value
        pairs = [(t, t // cores * cores + (t + dc) % cores) for t in range(groups)]
        return lax.ppermute(value, "tensor", pairs)

    def to_chip(value, db, dh):
        if (db, dh) == (0, 0):
            return value
        pairs = []
        for b in range(n_dp):
            for t in range(groups):
                target = (t // cores + dh) % chips * cores + t % cores
                pairs.append((b * groups + t, (b + db) % n_dp * groups + target))
        return lax.ppermute(value, ("dp", "tensor"), pairs)

    hops = [(db, dh) for db in range(n_dp) for dh in range(chips)]

    def dispatch(pieces):
        return [to_chip(pieces[dh], db, dh) for db, dh in hops]

    def give_back(pieces):
        arrived = [to_chip(piece, *hop) for piece, hop in zip(pieces, hops)]
        return arrived[:chips] + list(lax.optimization_barrier(tuple(arrived[chips:])))

    def swap(pieces):
        return [to_core(piece, dc) for dc in range(cores) for piece in pieces]

    def add_blocks(pieces):
        return call(
            functools.partial(add_blocks_kernel, chips, cores),
            "add_blocks",
            shape(slots, width),
            pieces,
            2 * slots * width,
        )

    def across(parts, dz, first=0):
        pairs = [(partner_column(z, dz - first, columns), z) for z in range(columns)]
        return lax.ppermute(parts[first], "expert", pairs)

    direct = [dz for dz in range(1, columns) if dz & (dz - 1) == 0][::-1]
    later = [dz for dz in range(1, columns) if dz not in direct]

    def pick(key, sources):
        return call(
            functools.partial(pick_kernel, cores),
            "pick",
            [shape(CAP, cores * width)] * chips,
            [key, *sources],
            EARLY,
        )

    token_sources = [to_core(tokens, dc) for dc in range(cores)]
    grad_sources = [to_core(grad_out, dc) for dc in range(cores)]
    key = call(number_kernel, "number", shape(experts, rows, F32), [routes_t], EARLY)
    tok_in = dispatch(pick(key, token_sources))
    tok_in[0], grad_pieces = lax.optimization_barrier((tok_in[0], pick(key, grad_sources)))
    grad_in = dispatch(grad_pieces)

    matmul_flops = 2 * tall * hid_dev * feats
    saved = [shape(tall, hid_dev, F32)] * 2
    piece = [shape(CAP, cores * width)] * count
    act, scale, *outs = call(
        functools.partial(forward_kernel, chips, cores, count),
        "forward",
        saved + piece,
        [*tok_in, gate_weight, up_weight, down_weight],
        3 * matmul_flops,
        [pltpu.VMEM((tall, feats), BF16), pltpu.VMEM((tall, hid_dev), BF16)],
        limit=24,
    )
    outs, grad_in = after(outs, grad_in)
    out_pieces = give_back(outs)
    backs = call(
        functools.partial(backward_kernel, chips, cores, count),
        "backward",
        piece,
        [*grad_in, gate_weight, up_weight, down_weight, act, scale],
        3 * matmul_flops,
        [pltpu.VMEM((tall, feats), BF16)] + [pltpu.VMEM((tall, hid_dev), BF16)] * 2,
        limit=24,
    )
    out_pieces[chips:], backs = after(out_pieces[chips:], backs)
    out_rows = add_blocks(swap(out_pieces))
    out_rows, backs = after(out_rows, backs)
    out_parts = {0: out_rows}
    for dz in direct:
        out_parts[dz] = across(out_parts, dz)
    back_pieces = give_back(backs)
    back_pieces[1], out_parts = after(back_pieces[1], out_parts)
    for dz in later:
        out_parts[dz] = across(out_parts, dz, dz & (dz - 1))
    back_rows = add_blocks(swap(back_pieces))
    back_parts = {0: back_rows}
    for dz in direct + later:
        back_parts[dz] = across(back_parts, dz)
    _, out_parts = after(back_rows, out_parts)

    weight_map = call(
        functools.partial(weights_kernel, chips, cores, columns),
        "weights",
        shape(rows, experts * CAP),
        [routes_t, gates_t, key],
        experts * CAP * rows,
        [pltpu.VMEM((experts, rows), F32), pltpu.VMEM((experts * CAP, rows), F32)],
        limit=16,
    )

    all_rows = pltpu.VMEM((experts * CAP, width), BF16)
    combine_flops = 2 * experts * CAP * rows * width
    mixed, gate_part = call(
        functools.partial(combine_gate_kernel, chips, cores, columns),
        "combine_gate",
        [shape(rows, width), shape(routes_t.shape[0], rows, F32)],
        [weight_map, routes_t, key, grad_out, *[out_parts[dz] for dz in range(columns)]],
        0,
        [all_rows, pltpu.VMEM((experts * CAP, rows), F32)],
        limit=24,
    )
    gate_parts = [gate_part]
    for dt in range(1, groups):
        pairs = [(t, (t + dt) % groups) for t in range(groups)]
        gate_parts.append(lax.ppermute(gate_part, "tensor", pairs))
    grad_tokens, grad_gates = call(
        functools.partial(combine_kernel, columns),
        "combine",
        [shape(rows, width), shape(*gate_part.shape, F32)],
        [weight_map, *[back_parts[dz] for dz in range(columns)], *gate_parts],
        combine_flops,
        [all_rows],
        limit=16,
    )
    return (mixed, grad_tokens, grad_gates.T)


def solution(mesh):
    sizes = (mesh.shape["dp"], mesh.shape["tensor"], mesh.shape["expert"])
    return jax.shard_map(
        functools.partial(body, sizes),
        mesh=mesh,
        in_specs=(
            P("dp", "tensor"),
            P("dp", "tensor"),
            P("dp", None),
            P("dp", None),
            P(("expert", "tensor"), "dp", None),
            P(("expert", "tensor"), "dp", None),
            P(("expert", "tensor"), "dp", None),
        ),
        out_specs=(P("dp", "tensor"), P("dp", "tensor"), P("dp", None)),
        check_vma=False,
    )
```

```python
import functools

import jax
import jax.numpy as jnp
from jax import lax
from jax.experimental import pallas as pl
from jax.experimental.pallas import tpu as pltpu
from jax.sharding import PartitionSpec as P

CAP = 48
LANES = 128
MIB = 2**20
EARLY = 6e9
BF16 = jnp.bfloat16
F32 = jnp.float32
CONTRACT_LAST = (((1,), (1,)), ((), ()))


def call(kernel, name, out_shape, operands, flops, scratch=(), limit=8):
    outs = out_shape if isinstance(out_shape, list) else [out_shape]
    moved = sum(a.size * a.dtype.itemsize for a in [*operands, *outs])
    spec = pl.BlockSpec(memory_space=pltpu.VMEM)
    return pl.pallas_call(
        kernel,
        out_shape=out_shape,
        in_specs=[spec] * len(operands),
        out_specs=[spec] * len(outs) if isinstance(out_shape, list) else spec,
        scratch_shapes=list(scratch),
        compiler_params=pltpu.CompilerParams(vmem_limit_bytes=limit * MIB),
        cost_estimate=pl.CostEstimate(flops=int(flops), bytes_accessed=int(moved), transcendentals=0),
        name=name,
    )(*operands)


def after(values, earlier):
    return lax.optimization_barrier((values, earlier))


def number_kernel(routes_ref, key_ref):
    experts, rows = key_ref.shape
    ids = lax.broadcasted_iota(jnp.int32, (experts, rows), 0)
    hit = jnp.zeros((experts, rows), F32)
    for r in range(routes_ref.shape[0]):
        hit = hit + (routes_ref[r : r + 1, :] == ids).astype(F32)
    before = (
        lax.broadcasted_iota(jnp.int32, (LANES, LANES), 0) < lax.broadcasted_iota(jnp.int32, (LANES, LANES), 1)
    ).astype(BF16)
    offset = jnp.zeros((experts, 1), F32)
    for start in range(0, rows, LANES):
        part = hit[:, start : start + LANES]
        rank = jnp.dot(part.astype(BF16), before, preferred_element_type=F32) + offset
        offset = offset + jnp.sum(part, axis=1, keepdims=True)
        key_ref[:, start : start + LANES] = jnp.where(part > 0.0, rank, -1.0)


def position(cores):
    t = lax.axis_index("tensor")
    return lax.div(t, cores), lax.rem(t, cores), lax.axis_index("expert")


def pick_kernel(cores, key_ref, *refs):
    sources, pieces = refs[:cores], refs[cores:]
    chips = len(pieces)
    rows, width = sources[0].shape
    chip, core, e = position(cores)
    slot = lax.broadcasted_iota(jnp.int32, (CAP, rows), 0).astype(F32)
    masks = []
    for dh in range(chips):
        expert = (e * chips + lax.rem(chip + dh, chips)) * cores + core
        masks.append((key_ref[pl.ds(expert, 1), :] == slot).astype(BF16))
    mask = jnp.concatenate(masks, axis=0)
    for dc, source in enumerate(sources):
        picked = jnp.dot(mask, source[...], preferred_element_type=F32).astype(BF16)
        column = pl.multiple_of(lax.rem(core - dc + cores, cores) * width, width)
        for dh, piece in enumerate(pieces):
            piece[:, pl.ds(column, width)] = picked[dh * CAP : (dh + 1) * CAP]


def gather_pieces(x_ref, pieces, chips, cores):
    chip, _, _ = position(cores)
    width = pieces[0].shape[1]
    for index, piece in enumerate(pieces):
        db, dh = divmod(index, chips)
        column = pl.multiple_of(lax.rem(chip - dh + chips, chips) * width, width)
        x_ref[db * CAP : (db + 1) * CAP, pl.ds(column, width)] = piece[...]


def project_back(terms, pieces, chips, cores):
    chip, _, _ = position(cores)
    blocks = len(pieces) // chips
    width = pieces[0].shape[1]
    for dh in range(chips):
        column = pl.ds(pl.multiple_of(lax.rem(chip + dh, chips) * width, width), width)
        total = None
        for h_ref, w_ref in terms:
            term = jnp.dot(h_ref[...], w_ref[0, :, column], preferred_element_type=F32)
            total = term if total is None else total + term
        total = total.astype(BF16)
        for db in range(blocks):
            row = (-db) % blocks * CAP
            pieces[db * chips + dh][...] = total[row : row + CAP]


def chunks_of(hid_dev):
    size = 256 if hid_dev % 256 == 0 else hid_dev
    return [slice(start, start + size) for start in range(0, hid_dev, size)]


def forward_kernel(chips, cores, count, *refs):
    pieces, (gate_ref, up_ref, down_ref) = refs[:count], refs[count : count + 3]
    act_ref, scale_ref = refs[count + 3 : count + 5]
    outs, (x_ref, hid_ref) = refs[count + 5 : 2 * count + 5], refs[2 * count + 5 :]
    gather_pieces(x_ref, pieces, chips, cores)
    for part in chunks_of(gate_ref.shape[1]):
        gate_pre = lax.dot_general(x_ref[...], gate_ref[0, part, :], CONTRACT_LAST, preferred_element_type=F32)
        up_pre = lax.dot_general(x_ref[...], up_ref[0, part, :], CONTRACT_LAST, preferred_element_type=F32)
        sig = jax.nn.sigmoid(gate_pre)
        act = gate_pre * sig
        hid_ref[:, part] = (act * up_pre).astype(BF16)
        act_ref[:, part] = act
        scale_ref[:, part] = up_pre * (sig * (1.0 + gate_pre * (1.0 - sig)))
    project_back([(hid_ref, down_ref)], outs, chips, cores)


def backward_kernel(chips, cores, count, *refs):
    pieces, (gate_ref, up_ref, down_ref) = refs[:count], refs[count : count + 3]
    act_ref, scale_ref = refs[count + 3 : count + 5]
    outs, (x_ref, grad_gate_ref, grad_up_ref) = refs[count + 5 : 2 * count + 5], refs[2 * count + 5 :]
    gather_pieces(x_ref, pieces, chips, cores)
    for part in chunks_of(gate_ref.shape[1]):
        grad_hid = lax.dot_general(x_ref[...], down_ref[0, part, :], CONTRACT_LAST, preferred_element_type=F32)
        grad_gate_ref[:, part] = (grad_hid * scale_ref[:, part]).astype(BF16)
        grad_up_ref[:, part] = (grad_hid * act_ref[:, part]).astype(BF16)
    project_back([(grad_gate_ref, gate_ref), (grad_up_ref, up_ref)], outs, chips, cores)


def add_blocks_kernel(chips, cores, *refs):
    pieces, out_ref = refs[:-1], refs[-1]
    width = out_ref.shape[1]
    count = len(pieces) // cores
    _, core, _ = position(cores)
    column = pl.ds(pl.multiple_of(core * width, width), width)
    for dh in range(chips):
        for dc in range(cores):
            total = None
            for piece in pieces[dc * count + dh : (dc + 1) * count : chips]:
                term = piece[:, column].astype(F32)
                total = term if total is None else total + term
            row = (dh * cores + dc) * CAP
            out_ref[row : row + CAP, :] = total.astype(BF16)


def partner_column(e, dz, columns):
    if columns & (columns - 1) == 0:
        return e ^ dz
    return (e - dz + columns) % columns


def slot_experts(chips, cores, columns):
    chip, core, e = position(cores)
    experts = []
    for dz in range(columns):
        for dh in range(chips):
            for dc in range(cores):
                column = partner_column(e, dz, columns)
                owner = lax.rem(chip - dh + chips, chips)
                experts.append((column * chips + owner) * cores + lax.rem(core - dc + cores, cores))
    return experts


def weights_kernel(chips, cores, columns, routes_ref, gates_ref, key_ref, out_ref, gate_ref, all_ref):
    experts, rows = key_ref.shape
    ids = lax.broadcasted_iota(jnp.int32, (experts, rows), 0)
    gate = jnp.zeros((experts, rows), F32)
    for r in range(routes_ref.shape[0]):
        gate = gate + jnp.where(routes_ref[r : r + 1, :] == ids, gates_ref[r : r + 1, :], 0.0)
    gate_ref[...] = gate
    slot = lax.broadcasted_iota(jnp.int32, (CAP, rows), 0).astype(F32)
    for index, expert in enumerate(slot_experts(chips, cores, columns)):
        same = key_ref[pl.ds(expert, 1), :] == slot
        all_ref[index * CAP : (index + 1) * CAP, :] = jnp.where(same, gate_ref[pl.ds(expert, 1), :], 0.0)
    slots = all_ref.shape[0]
    step = LANES if slots % LANES == 0 else slots
    for start in range(0, slots, step):
        out_ref[:, start : start + step] = all_ref[start : start + step, :].T.astype(BF16)


def place_parts(parts, all_ref):
    height = parts[0].shape[0]
    for index, part in enumerate(parts):
        all_ref[index * height : (index + 1) * height, :] = part[...]


def combine_kernel(columns, weight_ref, *refs):
    parts, gates = refs[:columns], refs[columns:-3]
    out_ref, total_ref, all_ref = refs[-3:]
    place_parts(parts, all_ref)
    out_ref[...] = jnp.dot(weight_ref[...], all_ref[...], preferred_element_type=F32).astype(BF16)
    total = gates[0][...]
    for gate in gates[1:]:
        total = total + gate[...]
    total_ref[...] = total


def combine_gate_kernel(chips, cores, columns, weight_ref, routes_ref, key_ref, grads_ref, *refs):
    parts, (out_ref, gate_ref, all_ref, sum_ref) = refs[:-4], refs[-4:]
    place_parts(parts, all_ref)
    out_ref[...] = jnp.dot(weight_ref[...], all_ref[...], preferred_element_type=F32).astype(BF16)
    rows = key_ref.shape[1]
    slot = lax.broadcasted_iota(jnp.int32, (CAP, rows), 0).astype(F32)
    routes = routes_ref[...]
    sum_ref[...] = lax.dot_general(all_ref[...], grads_ref[...], CONTRACT_LAST, preferred_element_type=F32)
    total = jnp.zeros(gate_ref.shape, F32)
    for index, expert in enumerate(slot_experts(chips, cores, columns)):
        same = key_ref[pl.ds(expert, 1), :] == slot
        row = jnp.where(same, sum_ref[index * CAP : (index + 1) * CAP, :], 0.0)
        total = total + jnp.where(routes == expert, jnp.sum(row, axis=0, keepdims=True), 0.0)
    gate_ref[...] = total


def body(sizes, tokens, grad_out, routes, gates, gate_weight, up_weight, down_weight):
    n_dp, groups, columns = sizes
    cores = 2 if groups % 2 == 0 else 1
    chips = groups // cores
    experts = groups * columns
    rows, width = tokens.shape
    _, hid_dev, feats = gate_weight.shape
    count = n_dp * chips
    tall = n_dp * CAP
    slots = groups * CAP
    routes_t, gates_t = routes.T, gates.T

    def shape(height, length, dtype=BF16):
        return jax.ShapeDtypeStruct((height, length), dtype)

    def to_core(value, dc):
        if dc == 0:
            return value
        pairs = [(t, t // cores * cores + (t + dc) % cores) for t in range(groups)]
        return lax.ppermute(value, "tensor", pairs)

    def to_chip(value, db, dh):
        if (db, dh) == (0, 0):
            return value
        pairs = []
        for b in range(n_dp):
            for t in range(groups):
                target = (t // cores + dh) % chips * cores + t % cores
                pairs.append((b * groups + t, (b + db) % n_dp * groups + target))
        return lax.ppermute(value, ("dp", "tensor"), pairs)

    hops = [(db, dh) for db in range(n_dp) for dh in range(chips)]
    first = (n_dp - 1) * chips
    order = sorted(range(count), key=lambda index: (hops[index][0] == 0, -hops[index][1]))

    def dispatch(pieces):
        arrived = {index: to_chip(pieces[hops[index][1]], *hops[index]) for index in order}
        return [arrived[index] for index in range(count)]

    def give_back(pieces):
        arrived = {index: to_chip(pieces[index], *hops[index]) for index in order}
        return [arrived[index] for index in range(count)]

    def swap(pieces):
        return [to_core(piece, dc) for dc in range(cores) for piece in pieces]

    def add_blocks(pieces):
        return call(
            functools.partial(add_blocks_kernel, chips, cores),
            "add_blocks",
            shape(slots, width),
            pieces,
            2 * slots * width,
        )

    def across(parts, dz, first=0):
        pairs = [(partner_column(z, dz - first, columns), z) for z in range(columns)]
        return lax.ppermute(parts[first], "expert", pairs)

    direct = [dz for dz in range(1, columns) if dz & (dz - 1) == 0][::-1]
    later = [dz for dz in range(1, columns) if dz not in direct]

    def pick(key, sources):
        return call(
            functools.partial(pick_kernel, cores),
            "pick",
            [shape(CAP, cores * width)] * chips,
            [key, *sources],
            EARLY,
        )

    token_sources = [to_core(tokens, dc) for dc in range(cores)]
    key = call(number_kernel, "number", shape(experts, rows, F32), [routes_t], EARLY)
    grads, key = after(grad_out, key)
    grad_sources = [to_core(grads, dc) for dc in range(cores)]
    tok_in = dispatch(pick(key, token_sources))
    tok_in[0], grad_pieces = lax.optimization_barrier((tok_in[0], pick(key, grad_sources)))
    grad_in = dispatch(grad_pieces)

    matmul_flops = 2 * tall * hid_dev * feats
    saved = [shape(tall, hid_dev, F32)] * 2
    piece = [shape(CAP, cores * width)] * count
    act, scale, *outs = call(
        functools.partial(forward_kernel, chips, cores, count),
        "forward",
        saved + piece,
        [*tok_in, gate_weight, up_weight, down_weight],
        3 * matmul_flops,
        [pltpu.VMEM((tall, feats), BF16), pltpu.VMEM((tall, hid_dev), BF16)],
        limit=24,
    )
    outs, grad_in = after(outs, grad_in)
    out_pieces = give_back(outs)
    backs = call(
        functools.partial(backward_kernel, chips, cores, count),
        "backward",
        piece,
        [*grad_in, gate_weight, up_weight, down_weight, act, scale],
        3 * matmul_flops,
        [pltpu.VMEM((tall, feats), BF16)] + [pltpu.VMEM((tall, hid_dev), BF16)] * 2,
        limit=24,
    )
    out_pieces[first], backs = after(out_pieces[first], backs)
    out_rows = add_blocks(swap(out_pieces))
    out_rows, backs = after(out_rows, backs)
    out_parts = {0: out_rows}
    for dz in direct:
        out_parts[dz] = across(out_parts, dz)
    back_pieces = give_back(backs)
    out_parts[direct[0]] = lax.optimization_barrier(out_parts[direct[0]])
    back_pieces[-1], out_parts = after(back_pieces[-1], out_parts)
    for dz in later:
        out_parts[dz] = across(out_parts, dz, dz & (dz - 1))
    back_rows = add_blocks(swap(back_pieces))
    back_parts = {0: back_rows}
    for dz in direct + later:
        back_parts[dz] = across(back_parts, dz)
    _, out_parts = after(back_rows, out_parts)

    weight_map = call(
        functools.partial(weights_kernel, chips, cores, columns),
        "weights",
        shape(rows, experts * CAP),
        [routes_t, gates_t, key],
        experts * CAP * rows,
        [pltpu.VMEM((experts, rows), F32), pltpu.VMEM((experts * CAP, rows), F32)],
        limit=16,
    )

    all_rows = pltpu.VMEM((experts * CAP, width), BF16)
    combine_flops = 2 * experts * CAP * rows * width
    mixed, gate_part = call(
        functools.partial(combine_gate_kernel, chips, cores, columns),
        "combine_gate",
        [shape(rows, width), shape(routes_t.shape[0], rows, F32)],
        [weight_map, routes_t, key, grad_out, *[out_parts[dz] for dz in range(columns)]],
        0,
        [all_rows, pltpu.VMEM((experts * CAP, rows), F32)],
        limit=24,
    )
    gate_parts = [gate_part]
    for dt in range(1, groups):
        pairs = [(t, (t + dt) % groups) for t in range(groups)]
        gate_parts.append(lax.ppermute(gate_part, "tensor", pairs))
    grad_tokens, grad_gates = call(
        functools.partial(combine_kernel, columns),
        "combine",
        [shape(rows, width), shape(*gate_part.shape, F32)],
        [weight_map, *[back_parts[dz] for dz in range(columns)], *gate_parts],
        combine_flops,
        [all_rows],
        limit=16,
    )
    return (mixed, grad_tokens, grad_gates.T)


def solution(mesh):
    sizes = (mesh.shape["dp"], mesh.shape["tensor"], mesh.shape["expert"])
    return jax.shard_map(
        functools.partial(body, sizes),
        mesh=mesh,
        in_specs=(
            P("dp", "tensor"),
            P("dp", "tensor"),
            P("dp", None),
            P("dp", None),
            P(("expert", "tensor"), "dp", None),
            P(("expert", "tensor"), "dp", None),
            P(("expert", "tensor"), "dp", None),
        ),
        out_specs=(P("dp", "tensor"), P("dp", "tensor"), P("dp", None)),
        check_vma=False,
    )
```

```python
import functools

import jax
import jax.numpy as jnp
from jax import lax
from jax.experimental import pallas as pl
from jax.experimental.pallas import tpu as pltpu
from jax.sharding import PartitionSpec as P

CAP = 48
LANES = 128
MIB = 2**20
EARLY = 6e9
BF16 = jnp.bfloat16
F32 = jnp.float32
CONTRACT_LAST = (((1,), (1,)), ((), ()))


def call(kernel, name, out_shape, operands, flops, scratch=(), limit=8):
    outs = out_shape if isinstance(out_shape, list) else [out_shape]
    moved = sum(a.size * a.dtype.itemsize for a in [*operands, *outs])
    spec = pl.BlockSpec(memory_space=pltpu.VMEM)
    return pl.pallas_call(
        kernel,
        out_shape=out_shape,
        in_specs=[spec] * len(operands),
        out_specs=[spec] * len(outs) if isinstance(out_shape, list) else spec,
        scratch_shapes=list(scratch),
        compiler_params=pltpu.CompilerParams(vmem_limit_bytes=limit * MIB),
        cost_estimate=pl.CostEstimate(flops=int(flops), bytes_accessed=int(moved), transcendentals=0),
        name=name,
    )(*operands)


def after(values, earlier):
    return lax.optimization_barrier((values, earlier))


def number_kernel(routes_ref, key_ref):
    experts, rows = key_ref.shape
    ids = lax.broadcasted_iota(jnp.int32, (experts, rows), 0)
    hit = jnp.zeros((experts, rows), F32)
    for r in range(routes_ref.shape[0]):
        hit = hit + (routes_ref[r : r + 1, :] == ids).astype(F32)
    before = (
        lax.broadcasted_iota(jnp.int32, (LANES, LANES), 0) < lax.broadcasted_iota(jnp.int32, (LANES, LANES), 1)
    ).astype(BF16)
    offset = jnp.zeros((experts, 1), F32)
    for start in range(0, rows, LANES):
        part = hit[:, start : start + LANES]
        rank = jnp.dot(part.astype(BF16), before, preferred_element_type=F32) + offset
        offset = offset + jnp.sum(part, axis=1, keepdims=True)
        key_ref[:, start : start + LANES] = jnp.where(part > 0.0, rank, -1.0)


def position(cores):
    t = lax.axis_index("tensor")
    return lax.div(t, cores), lax.rem(t, cores), lax.axis_index("expert")


def pick_kernel(cores, key_ref, *refs):
    sources, pieces = refs[:cores], refs[cores:]
    chips = len(pieces)
    rows, width = sources[0].shape
    chip, core, e = position(cores)
    slot = lax.broadcasted_iota(jnp.int32, (CAP, rows), 0).astype(F32)
    masks = []
    for dh in range(chips):
        expert = (e * chips + lax.rem(chip + dh, chips)) * cores + core
        masks.append((key_ref[pl.ds(expert, 1), :] == slot).astype(BF16))
    mask = jnp.concatenate(masks, axis=0)
    for dc, source in enumerate(sources):
        picked = jnp.dot(mask, source[...], preferred_element_type=F32).astype(BF16)
        column = pl.multiple_of(lax.rem(core - dc + cores, cores) * width, width)
        for dh, piece in enumerate(pieces):
            piece[:, pl.ds(column, width)] = picked[dh * CAP : (dh + 1) * CAP]


def gather_pieces(x_ref, pieces, chips, cores):
    chip, _, _ = position(cores)
    width = pieces[0].shape[1]
    for index, piece in enumerate(pieces):
        db, dh = divmod(index, chips)
        column = pl.multiple_of(lax.rem(chip - dh + chips, chips) * width, width)
        x_ref[db * CAP : (db + 1) * CAP, pl.ds(column, width)] = piece[...]


def project_back(terms, pieces, chips, cores):
    chip, _, _ = position(cores)
    blocks = len(pieces) // chips
    width = pieces[0].shape[1]
    for dh in range(chips):
        column = pl.ds(pl.multiple_of(lax.rem(chip + dh, chips) * width, width), width)
        total = None
        for h_ref, w_ref in terms:
            term = jnp.dot(h_ref[...], w_ref[0, :, column], preferred_element_type=F32)
            total = term if total is None else total + term
        total = total.astype(BF16)
        for db in range(blocks):
            row = (-db) % blocks * CAP
            pieces[db * chips + dh][...] = total[row : row + CAP]


def chunks_of(hid_dev):
    size = 256 if hid_dev % 256 == 0 else hid_dev
    return [slice(start, start + size) for start in range(0, hid_dev, size)]


def forward_kernel(chips, cores, count, *refs):
    pieces, (gate_ref, up_ref, down_ref) = refs[:count], refs[count : count + 3]
    act_ref, scale_ref = refs[count + 3 : count + 5]
    outs, (x_ref, hid_ref) = refs[count + 5 : 2 * count + 5], refs[2 * count + 5 :]
    gather_pieces(x_ref, pieces, chips, cores)
    for part in chunks_of(gate_ref.shape[1]):
        gate_pre = lax.dot_general(x_ref[...], gate_ref[0, part, :], CONTRACT_LAST, preferred_element_type=F32)
        up_pre = lax.dot_general(x_ref[...], up_ref[0, part, :], CONTRACT_LAST, preferred_element_type=F32)
        sig = jax.nn.sigmoid(gate_pre)
        act = gate_pre * sig
        hid_ref[:, part] = (act * up_pre).astype(BF16)
        act_ref[:, part] = act
        scale_ref[:, part] = up_pre * (sig * (1.0 + gate_pre * (1.0 - sig)))
    project_back([(hid_ref, down_ref)], outs, chips, cores)


def backward_kernel(chips, cores, count, *refs):
    pieces, (gate_ref, up_ref, down_ref) = refs[:count], refs[count : count + 3]
    act_ref, scale_ref = refs[count + 3 : count + 5]
    outs, (x_ref, grad_gate_ref, grad_up_ref) = refs[count + 5 : 2 * count + 5], refs[2 * count + 5 :]
    gather_pieces(x_ref, pieces, chips, cores)
    for part in chunks_of(gate_ref.shape[1]):
        grad_hid = lax.dot_general(x_ref[...], down_ref[0, part, :], CONTRACT_LAST, preferred_element_type=F32)
        grad_gate_ref[:, part] = (grad_hid * scale_ref[:, part]).astype(BF16)
        grad_up_ref[:, part] = (grad_hid * act_ref[:, part]).astype(BF16)
    project_back([(grad_gate_ref, gate_ref), (grad_up_ref, up_ref)], outs, chips, cores)


def add_blocks_kernel(chips, cores, *refs):
    pieces, out_ref = refs[:-1], refs[-1]
    width = out_ref.shape[1]
    count = len(pieces) // cores
    _, core, _ = position(cores)
    column = pl.ds(pl.multiple_of(core * width, width), width)
    for dh in range(chips):
        for dc in range(cores):
            total = None
            for piece in pieces[dc * count + dh : (dc + 1) * count : chips]:
                term = piece[:, column].astype(F32)
                total = term if total is None else total + term
            row = (dh * cores + dc) * CAP
            out_ref[row : row + CAP, :] = total.astype(BF16)


def partner_column(e, dz, columns):
    if columns & (columns - 1) == 0:
        return e ^ dz
    return (e - dz + columns) % columns


def slot_experts(chips, cores, columns):
    chip, core, e = position(cores)
    experts = []
    for dz in range(columns):
        for dh in range(chips):
            for dc in range(cores):
                column = partner_column(e, dz, columns)
                owner = lax.rem(chip - dh + chips, chips)
                experts.append((column * chips + owner) * cores + lax.rem(core - dc + cores, cores))
    return experts


def weights_kernel(chips, cores, columns, routes_ref, gates_ref, key_ref, out_ref, gate_ref, all_ref):
    experts, rows = key_ref.shape
    ids = lax.broadcasted_iota(jnp.int32, (experts, rows), 0)
    gate = jnp.zeros((experts, rows), F32)
    for r in range(routes_ref.shape[0]):
        gate = gate + jnp.where(routes_ref[r : r + 1, :] == ids, gates_ref[r : r + 1, :], 0.0)
    gate_ref[...] = gate
    slot = lax.broadcasted_iota(jnp.int32, (CAP, rows), 0).astype(F32)
    for index, expert in enumerate(slot_experts(chips, cores, columns)):
        same = key_ref[pl.ds(expert, 1), :] == slot
        all_ref[index * CAP : (index + 1) * CAP, :] = jnp.where(same, gate_ref[pl.ds(expert, 1), :], 0.0)
    slots = all_ref.shape[0]
    step = LANES if slots % LANES == 0 else slots
    for start in range(0, slots, step):
        out_ref[:, start : start + step] = all_ref[start : start + step, :].T.astype(BF16)


def place_parts(parts, all_ref):
    height = parts[0].shape[0]
    for index, part in enumerate(parts):
        all_ref[index * height : (index + 1) * height, :] = part[...]


def combine_kernel(columns, weight_ref, *refs):
    parts, gates = refs[:columns][::-1], refs[columns:-3]
    out_ref, total_ref, all_ref = refs[-3:]
    place_parts(parts, all_ref)
    out_ref[...] = jnp.dot(weight_ref[...], all_ref[...], preferred_element_type=F32).astype(BF16)
    total = gates[0][...]
    for gate in gates[1:]:
        total = total + gate[...]
    total_ref[...] = total


def combine_gate_kernel(chips, cores, columns, weight_ref, routes_ref, key_ref, grads_ref, *refs):
    parts, (out_ref, gate_ref, all_ref, sum_ref) = refs[:-4], refs[-4:]
    place_parts(parts, all_ref)
    out_ref[...] = jnp.dot(weight_ref[...], all_ref[...], preferred_element_type=F32).astype(BF16)
    rows = key_ref.shape[1]
    slot = lax.broadcasted_iota(jnp.int32, (CAP, rows), 0).astype(F32)
    routes = routes_ref[...]
    sum_ref[...] = lax.dot_general(all_ref[...], grads_ref[...], CONTRACT_LAST, preferred_element_type=F32)
    total = jnp.zeros(gate_ref.shape, F32)
    for index, expert in enumerate(slot_experts(chips, cores, columns)):
        same = key_ref[pl.ds(expert, 1), :] == slot
        row = jnp.where(same, sum_ref[index * CAP : (index + 1) * CAP, :], 0.0)
        total = total + jnp.where(routes == expert, jnp.sum(row, axis=0, keepdims=True), 0.0)
    gate_ref[...] = total


def body(sizes, tokens, grad_out, routes, gates, gate_weight, up_weight, down_weight):
    n_dp, groups, columns = sizes
    cores = 2 if groups % 2 == 0 else 1
    chips = groups // cores
    experts = groups * columns
    rows, width = tokens.shape
    _, hid_dev, feats = gate_weight.shape
    count = n_dp * chips
    tall = n_dp * CAP
    slots = groups * CAP
    routes_t, gates_t = routes.T, gates.T

    def shape(height, length, dtype=BF16):
        return jax.ShapeDtypeStruct((height, length), dtype)

    def to_core(value, dc):
        if dc == 0:
            return value
        pairs = [(t, t // cores * cores + (t + dc) % cores) for t in range(groups)]
        return lax.ppermute(value, "tensor", pairs)

    def to_chip(value, db, dh):
        if (db, dh) == (0, 0):
            return value
        pairs = []
        for b in range(n_dp):
            for t in range(groups):
                target = (t // cores + dh) % chips * cores + t % cores
                pairs.append((b * groups + t, (b + db) % n_dp * groups + target))
        return lax.ppermute(value, ("dp", "tensor"), pairs)

    hops = [(db, dh) for db in range(n_dp) for dh in range(chips)]
    first = (n_dp - 1) * chips
    order = sorted(range(count), key=lambda index: (hops[index][0] == 0, -hops[index][1]))

    def dispatch(pieces):
        arrived = {index: to_chip(pieces[hops[index][1]], *hops[index]) for index in order}
        return [arrived[index] for index in range(count)]

    def give_back(pieces):
        arrived = {index: to_chip(pieces[index], *hops[index]) for index in order}
        return [arrived[index] for index in range(count)]

    def swap(pieces):
        return [to_core(piece, dc) for dc in range(cores) for piece in pieces]

    def add_blocks(pieces):
        return call(
            functools.partial(add_blocks_kernel, chips, cores),
            "add_blocks",
            shape(slots, width),
            pieces,
            2 * slots * width,
        )

    def across(parts, dz, first=0):
        pairs = [(partner_column(z, dz - first, columns), z) for z in range(columns)]
        return lax.ppermute(parts[first], "expert", pairs)

    direct = [dz for dz in range(1, columns) if dz & (dz - 1) == 0][::-1]
    later = [dz for dz in range(1, columns) if dz not in direct]

    def pick(key, sources):
        return call(
            functools.partial(pick_kernel, cores),
            "pick",
            [shape(CAP, cores * width)] * chips,
            [key, *sources],
            EARLY,
        )

    token_sources = [to_core(tokens, dc) for dc in range(cores)]
    key = call(number_kernel, "number", shape(experts, rows, F32), [routes_t], EARLY)
    grads, key = after(grad_out, key)
    grad_sources = [to_core(grads, dc) for dc in range(cores)]
    tok_in = dispatch(pick(key, token_sources))
    tok_in[0], grad_pieces = lax.optimization_barrier((tok_in[0], pick(key, grad_sources)))
    grad_in = dispatch(grad_pieces)

    matmul_flops = 2 * tall * hid_dev * feats
    saved = [shape(tall, hid_dev, F32)] * 2
    piece = [shape(CAP, cores * width)] * count
    act, scale, *outs = call(
        functools.partial(forward_kernel, chips, cores, count),
        "forward",
        saved + piece,
        [*tok_in, gate_weight, up_weight, down_weight],
        3 * matmul_flops,
        [pltpu.VMEM((tall, feats), BF16), pltpu.VMEM((tall, hid_dev), BF16)],
        limit=24,
    )
    outs, grad_in = after(outs, grad_in)
    out_pieces = give_back(outs)
    backs = call(
        functools.partial(backward_kernel, chips, cores, count),
        "backward",
        piece,
        [*grad_in, gate_weight, up_weight, down_weight, act, scale],
        3 * matmul_flops,
        [pltpu.VMEM((tall, feats), BF16)] + [pltpu.VMEM((tall, hid_dev), BF16)] * 2,
        limit=24,
    )
    out_pieces[first], backs = after(out_pieces[first], backs)
    out_rows = add_blocks(swap(out_pieces))
    out_rows, backs = after(out_rows, backs)
    out_parts = {0: out_rows}
    for dz in direct:
        out_parts[dz] = across(out_parts, dz)
    back_pieces = give_back(backs)
    out_parts[direct[0]] = lax.optimization_barrier(out_parts[direct[0]])
    back_pieces[-1], out_parts = after(back_pieces[-1], out_parts)
    for dz in later:
        out_parts[dz] = across(out_parts, dz, dz & (dz - 1))
    back_rows = add_blocks(swap(back_pieces))
    back_parts = {0: back_rows}
    for dz in later + direct:
        back_parts[dz] = across(back_parts, dz)
    _, out_parts = after(back_rows, out_parts)

    weight_map = call(
        functools.partial(weights_kernel, chips, cores, columns),
        "weights",
        shape(rows, experts * CAP),
        [routes_t, gates_t, key],
        experts * CAP * rows,
        [pltpu.VMEM((experts, rows), F32), pltpu.VMEM((experts * CAP, rows), F32)],
        limit=16,
    )

    all_rows = pltpu.VMEM((experts * CAP, width), BF16)
    combine_flops = 2 * experts * CAP * rows * width
    mixed, gate_part = call(
        functools.partial(combine_gate_kernel, chips, cores, columns),
        "combine_gate",
        [shape(rows, width), shape(routes_t.shape[0], rows, F32)],
        [weight_map, routes_t, key, grad_out, *[out_parts[dz] for dz in range(columns)]],
        0,
        [all_rows, pltpu.VMEM((experts * CAP, rows), F32)],
        limit=24,
    )
    gate_parts = [gate_part]
    for dt in range(1, groups):
        pairs = [(t, (t + dt) % groups) for t in range(groups)]
        gate_parts.append(lax.ppermute(gate_part, "tensor", pairs))
    grad_tokens, grad_gates = call(
        functools.partial(combine_kernel, columns),
        "combine",
        [shape(rows, width), shape(*gate_part.shape, F32)],
        [weight_map, *[back_parts[dz] for dz in reversed(range(columns))], *gate_parts],
        combine_flops,
        [all_rows],
        limit=16,
    )
    return (mixed, grad_tokens, grad_gates.T)


def solution(mesh):
    sizes = (mesh.shape["dp"], mesh.shape["tensor"], mesh.shape["expert"])
    return jax.shard_map(
        functools.partial(body, sizes),
        mesh=mesh,
        in_specs=(
            P("dp", "tensor"),
            P("dp", "tensor"),
            P("dp", None),
            P("dp", None),
            P(("expert", "tensor"), "dp", None),
            P(("expert", "tensor"), "dp", None),
            P(("expert", "tensor"), "dp", None),
        ),
        out_specs=(P("dp", "tensor"), P("dp", "tensor"), P("dp", None)),
        check_vma=False,
    )
```

```python
import functools

import jax
import jax.numpy as jnp
from jax import lax
from jax.experimental import pallas as pl
from jax.experimental.pallas import tpu as pltpu
from jax.sharding import PartitionSpec as P

CAP = 48
LANES = 128
MIB = 2**20
EARLY = 6e9
BF16 = jnp.bfloat16
F32 = jnp.float32
CONTRACT_LAST = (((1,), (1,)), ((), ()))


def call(kernel, name, out_shape, operands, flops, scratch=(), limit=8):
    outs = out_shape if isinstance(out_shape, list) else [out_shape]
    moved = sum(a.size * a.dtype.itemsize for a in [*operands, *outs])
    spec = pl.BlockSpec(memory_space=pltpu.VMEM)
    return pl.pallas_call(
        kernel,
        out_shape=out_shape,
        in_specs=[spec] * len(operands),
        out_specs=[spec] * len(outs) if isinstance(out_shape, list) else spec,
        scratch_shapes=list(scratch),
        compiler_params=pltpu.CompilerParams(vmem_limit_bytes=limit * MIB),
        cost_estimate=pl.CostEstimate(flops=int(flops), bytes_accessed=int(moved), transcendentals=0),
        name=name,
    )(*operands)


def after(values, earlier):
    return lax.optimization_barrier((values, earlier))


def number_kernel(routes_ref, key_ref):
    experts, rows = key_ref.shape
    ids = lax.broadcasted_iota(jnp.int32, (experts, rows), 0)
    hit = jnp.zeros((experts, rows), F32)
    for r in range(routes_ref.shape[0]):
        hit = hit + (routes_ref[r : r + 1, :] == ids).astype(F32)
    before = (
        lax.broadcasted_iota(jnp.int32, (LANES, LANES), 0) < lax.broadcasted_iota(jnp.int32, (LANES, LANES), 1)
    ).astype(BF16)
    offset = jnp.zeros((experts, 1), F32)
    for start in range(0, rows, LANES):
        part = hit[:, start : start + LANES]
        rank = jnp.dot(part.astype(BF16), before, preferred_element_type=F32) + offset
        offset = offset + jnp.sum(part, axis=1, keepdims=True)
        key_ref[:, start : start + LANES] = jnp.where(part > 0.0, rank, -1.0)


def position(cores):
    t = lax.axis_index("tensor")
    return lax.div(t, cores), lax.rem(t, cores), lax.axis_index("expert")


def pick_kernel(cores, key_ref, *refs):
    sources, pieces = refs[:cores], refs[cores:]
    chips = len(pieces)
    rows, width = sources[0].shape
    chip, core, e = position(cores)
    slot = lax.broadcasted_iota(jnp.int32, (CAP, rows), 0).astype(F32)
    masks = []
    for dh in range(chips):
        expert = (e * chips + lax.rem(chip + dh, chips)) * cores + core
        masks.append((key_ref[pl.ds(expert, 1), :] == slot).astype(BF16))
    mask = jnp.concatenate(masks, axis=0)
    for dc, source in enumerate(sources):
        picked = jnp.dot(mask, source[...], preferred_element_type=F32).astype(BF16)
        column = pl.multiple_of(lax.rem(core - dc + cores, cores) * width, width)
        for dh, piece in enumerate(pieces):
            piece[:, pl.ds(column, width)] = picked[dh * CAP : (dh + 1) * CAP]


def gather_pieces(x_ref, pieces, chips, cores):
    chip, _, _ = position(cores)
    width = pieces[0].shape[1]
    for index, piece in enumerate(pieces):
        db, dh = divmod(index, chips)
        column = pl.multiple_of(lax.rem(chip - dh + chips, chips) * width, width)
        x_ref[db * CAP : (db + 1) * CAP, pl.ds(column, width)] = piece[...]


def project_back(terms, pieces, chips, cores):
    chip, _, _ = position(cores)
    blocks = len(pieces) // chips
    width = pieces[0].shape[1]
    for dh in range(chips):
        column = pl.ds(pl.multiple_of(lax.rem(chip + dh, chips) * width, width), width)
        total = None
        for h_ref, w_ref in terms:
            term = jnp.dot(h_ref[...], w_ref[0, :, column], preferred_element_type=F32)
            total = term if total is None else total + term
        total = total.astype(BF16)
        for db in range(blocks):
            row = (-db) % blocks * CAP
            pieces[db * chips + dh][...] = total[row : row + CAP]


def chunks_of(hid_dev):
    size = 256 if hid_dev % 256 == 0 else hid_dev
    return [slice(start, start + size) for start in range(0, hid_dev, size)]


def forward_kernel(chips, cores, count, *refs):
    pieces, (gate_ref, up_ref, down_ref) = refs[:count], refs[count : count + 3]
    act_ref, scale_ref = refs[count + 3 : count + 5]
    outs, (x_ref, hid_ref) = refs[count + 5 : 2 * count + 5], refs[2 * count + 5 :]
    gather_pieces(x_ref, pieces, chips, cores)
    for part in chunks_of(gate_ref.shape[1]):
        gate_pre = lax.dot_general(x_ref[...], gate_ref[0, part, :], CONTRACT_LAST, preferred_element_type=F32)
        up_pre = lax.dot_general(x_ref[...], up_ref[0, part, :], CONTRACT_LAST, preferred_element_type=F32)
        sig = jax.nn.sigmoid(gate_pre)
        act = gate_pre * sig
        hid_ref[:, part] = (act * up_pre).astype(BF16)
        act_ref[:, part] = act
        scale_ref[:, part] = up_pre * (sig * (1.0 + gate_pre * (1.0 - sig)))
    project_back([(hid_ref, down_ref)], outs, chips, cores)


def backward_kernel(chips, cores, count, *refs):
    pieces, (gate_ref, up_ref, down_ref) = refs[:count], refs[count : count + 3]
    act_ref, scale_ref = refs[count + 3 : count + 5]
    outs, (x_ref, grad_gate_ref, grad_up_ref) = refs[count + 5 : 2 * count + 5], refs[2 * count + 5 :]
    gather_pieces(x_ref, pieces, chips, cores)
    for part in chunks_of(gate_ref.shape[1]):
        grad_hid = lax.dot_general(x_ref[...], down_ref[0, part, :], CONTRACT_LAST, preferred_element_type=F32)
        grad_gate_ref[:, part] = (grad_hid * scale_ref[:, part]).astype(BF16)
        grad_up_ref[:, part] = (grad_hid * act_ref[:, part]).astype(BF16)
    project_back([(grad_gate_ref, gate_ref), (grad_up_ref, up_ref)], outs, chips, cores)


def add_blocks_kernel(chips, cores, *refs):
    pieces, out_ref, halves = refs[:-3], refs[-3], refs[-2:]
    height, width = halves[0].shape
    count = len(pieces) // cores
    _, core, _ = position(cores)
    column = pl.ds(pl.multiple_of(core * width, width), width)
    for dh in range(chips):
        for dc in range(cores):
            total = None
            for piece in pieces[dc * count + dh : (dc + 1) * count : chips]:
                term = piece[:, column].astype(F32)
                total = term if total is None else total + term
            row = (dh * cores + dc) * CAP
            out_ref[row : row + CAP, :] = total.astype(BF16)
    for index, half in enumerate(halves):
        half[...] = out_ref[index * height : (index + 1) * height, :]


def partner_column(e, dz, columns):
    if columns & (columns - 1) == 0:
        return e ^ dz
    return (e - dz + columns) % columns


def slot_experts(chips, cores, columns):
    chip, core, e = position(cores)
    experts = []
    for dz in range(columns):
        for dh in range(chips):
            for dc in range(cores):
                column = partner_column(e, dz, columns)
                owner = lax.rem(chip - dh + chips, chips)
                experts.append((column * chips + owner) * cores + lax.rem(core - dc + cores, cores))
    return experts


def weights_kernel(chips, cores, columns, routes_ref, gates_ref, key_ref, out_ref, gate_ref, all_ref):
    experts, rows = key_ref.shape
    ids = lax.broadcasted_iota(jnp.int32, (experts, rows), 0)
    gate = jnp.zeros((experts, rows), F32)
    for r in range(routes_ref.shape[0]):
        gate = gate + jnp.where(routes_ref[r : r + 1, :] == ids, gates_ref[r : r + 1, :], 0.0)
    gate_ref[...] = gate
    slot = lax.broadcasted_iota(jnp.int32, (CAP, rows), 0).astype(F32)
    for index, expert in enumerate(slot_experts(chips, cores, columns)):
        same = key_ref[pl.ds(expert, 1), :] == slot
        all_ref[index * CAP : (index + 1) * CAP, :] = jnp.where(same, gate_ref[pl.ds(expert, 1), :], 0.0)
    slots = all_ref.shape[0]
    step = LANES if slots % LANES == 0 else slots
    for start in range(0, slots, step):
        out_ref[:, start : start + step] = all_ref[start : start + step, :].T.astype(BF16)


def place_parts(parts, all_ref):
    height = parts[0].shape[0]
    for index, part in enumerate(parts):
        all_ref[index * height : (index + 1) * height, :] = part[...]


def combine_kernel(starts, weight_ref, *refs):
    parts, gates = refs[: len(starts)], refs[len(starts) : -3]
    out_ref, total_ref, all_ref = refs[-3:]
    for start, part in zip(starts, parts):
        all_ref[start : start + part.shape[0], :] = part[...]
    out_ref[...] = jnp.dot(weight_ref[...], all_ref[...], preferred_element_type=F32).astype(BF16)
    total = gates[0][...]
    for gate in gates[1:]:
        total = total + gate[...]
    total_ref[...] = total


def combine_gate_kernel(chips, cores, columns, weight_ref, routes_ref, key_ref, grads_ref, *refs):
    parts, (out_ref, gate_ref, all_ref, sum_ref) = refs[:-4], refs[-4:]
    place_parts(parts, all_ref)
    out_ref[...] = jnp.dot(weight_ref[...], all_ref[...], preferred_element_type=F32).astype(BF16)
    rows = key_ref.shape[1]
    slot = lax.broadcasted_iota(jnp.int32, (CAP, rows), 0).astype(F32)
    routes = routes_ref[...]
    sum_ref[...] = lax.dot_general(all_ref[...], grads_ref[...], CONTRACT_LAST, preferred_element_type=F32)
    total = jnp.zeros(gate_ref.shape, F32)
    for index, expert in enumerate(slot_experts(chips, cores, columns)):
        same = key_ref[pl.ds(expert, 1), :] == slot
        row = jnp.where(same, sum_ref[index * CAP : (index + 1) * CAP, :], 0.0)
        total = total + jnp.where(routes == expert, jnp.sum(row, axis=0, keepdims=True), 0.0)
    gate_ref[...] = total


def body(sizes, tokens, grad_out, routes, gates, gate_weight, up_weight, down_weight):
    n_dp, groups, columns = sizes
    cores = 2 if groups % 2 == 0 else 1
    chips = groups // cores
    experts = groups * columns
    rows, width = tokens.shape
    _, hid_dev, feats = gate_weight.shape
    count = n_dp * chips
    tall = n_dp * CAP
    slots = groups * CAP
    routes_t, gates_t = routes.T, gates.T

    def shape(height, length, dtype=BF16):
        return jax.ShapeDtypeStruct((height, length), dtype)

    def to_core(value, dc):
        if dc == 0:
            return value
        pairs = [(t, t // cores * cores + (t + dc) % cores) for t in range(groups)]
        return lax.ppermute(value, "tensor", pairs)

    def to_chip(value, db, dh):
        if (db, dh) == (0, 0):
            return value
        pairs = []
        for b in range(n_dp):
            for t in range(groups):
                target = (t // cores + dh) % chips * cores + t % cores
                pairs.append((b * groups + t, (b + db) % n_dp * groups + target))
        return lax.ppermute(value, ("dp", "tensor"), pairs)

    hops = [(db, dh) for db in range(n_dp) for dh in range(chips)]
    first = (n_dp - 1) * chips
    order = sorted(range(count), key=lambda index: (hops[index][0] == 0, -hops[index][1]))

    def dispatch(pieces):
        arrived = {index: to_chip(pieces[hops[index][1]], *hops[index]) for index in order}
        return [arrived[index] for index in range(count)]

    def give_back(pieces):
        arrived = {index: to_chip(pieces[index], *hops[index]) for index in order}
        return [arrived[index] for index in range(count)]

    def swap(pieces):
        return [to_core(piece, dc) for dc in range(cores) for piece in pieces]

    def add_blocks(pieces):
        return call(
            functools.partial(add_blocks_kernel, chips, cores),
            "add_blocks",
            [shape(slots, width)] + [shape(slots // 2, width)] * 2,
            pieces,
            2 * slots * width,
        )

    def across(parts, dz, first=0):
        pairs = [(partner_column(z, dz - first, columns), z) for z in range(columns)]
        return lax.ppermute(parts[first], "expert", pairs)

    direct = [dz for dz in range(1, columns) if dz & (dz - 1) == 0][::-1]
    later = [dz for dz in range(1, columns) if dz not in direct]

    def pick(key, sources):
        return call(
            functools.partial(pick_kernel, cores),
            "pick",
            [shape(CAP, cores * width)] * chips,
            [key, *sources],
            EARLY,
        )

    token_sources = [to_core(tokens, dc) for dc in range(cores)]
    key = call(number_kernel, "number", shape(experts, rows, F32), [routes_t], EARLY)
    grads, key = after(grad_out, key)
    grad_sources = [to_core(grads, dc) for dc in range(cores)]
    tok_in = dispatch(pick(key, token_sources))
    tok_in[0], grad_pieces = lax.optimization_barrier((tok_in[0], pick(key, grad_sources)))
    grad_in = dispatch(grad_pieces)

    matmul_flops = 2 * tall * hid_dev * feats
    saved = [shape(tall, hid_dev, F32)] * 2
    piece = [shape(CAP, cores * width)] * count
    act, scale, *outs = call(
        functools.partial(forward_kernel, chips, cores, count),
        "forward",
        saved + piece,
        [*tok_in, gate_weight, up_weight, down_weight],
        3 * matmul_flops,
        [pltpu.VMEM((tall, feats), BF16), pltpu.VMEM((tall, hid_dev), BF16)],
        limit=24,
    )
    outs, grad_in = after(outs, grad_in)
    out_pieces = give_back(outs)
    backs = call(
        functools.partial(backward_kernel, chips, cores, count),
        "backward",
        piece,
        [*grad_in, gate_weight, up_weight, down_weight, act, scale],
        3 * matmul_flops,
        [pltpu.VMEM((tall, feats), BF16)] + [pltpu.VMEM((tall, hid_dev), BF16)] * 2,
        limit=24,
    )
    out_pieces[first], backs = after(out_pieces[first], backs)
    out_rows, _, _ = add_blocks(swap(out_pieces))
    out_rows, backs = after(out_rows, backs)
    out_parts = {0: out_rows}
    for dz in direct:
        out_parts[dz] = across(out_parts, dz)
    back_pieces = give_back(backs)
    out_parts[direct[0]] = lax.optimization_barrier(out_parts[direct[0]])
    back_pieces[-1], out_parts = after(back_pieces[-1], out_parts)
    for dz in later:
        out_parts[dz] = across(out_parts, dz, dz & (dz - 1))
    back_rows, low, high = add_blocks(swap(back_pieces))
    lows, highs = {0: low}, {0: high}
    for dz in range(2, columns):
        lows[dz] = across(lows, dz, dz & (dz - 1))
        highs[dz] = across(highs, dz)
    back_parts = [(lows[dz], dz * slots) for dz in direct if dz > 1]
    back_parts += [(highs[dz], dz * slots + slots // 2) for dz in reversed(range(2, columns))]
    back_parts += [(across({0: back_rows}, 1), slots)] if columns > 1 else []
    back_parts += [(back_rows, 0)] + [(lows[dz], dz * slots) for dz in later]
    _, out_parts = after(back_rows, out_parts)

    weight_map = call(
        functools.partial(weights_kernel, chips, cores, columns),
        "weights",
        shape(rows, experts * CAP),
        [routes_t, gates_t, key],
        experts * CAP * rows,
        [pltpu.VMEM((experts, rows), F32), pltpu.VMEM((experts * CAP, rows), F32)],
        limit=16,
    )

    all_rows = pltpu.VMEM((experts * CAP, width), BF16)
    combine_flops = 2 * experts * CAP * rows * width
    mixed, gate_part = call(
        functools.partial(combine_gate_kernel, chips, cores, columns),
        "combine_gate",
        [shape(rows, width), shape(routes_t.shape[0], rows, F32)],
        [weight_map, routes_t, key, grad_out, *[out_parts[dz] for dz in range(columns)]],
        0,
        [all_rows, pltpu.VMEM((experts * CAP, rows), F32)],
        limit=24,
    )
    chip_part = gate_part
    for dc in range(1, cores):
        chip_part = chip_part + to_core(gate_part, dc)
    gate_parts = [to_chip(chip_part, 0, dh) for dh in range(chips)]
    grad_tokens, grad_gates = call(
        functools.partial(combine_kernel, [start for _, start in back_parts]),
        "combine",
        [shape(rows, width), shape(*gate_part.shape, F32)],
        [weight_map, *[part for part, _ in back_parts], *gate_parts],
        combine_flops,
        [all_rows],
        limit=16,
    )
    return (mixed, grad_tokens, grad_gates.T)


def solution(mesh):
    sizes = (mesh.shape["dp"], mesh.shape["tensor"], mesh.shape["expert"])
    return jax.shard_map(
        functools.partial(body, sizes),
        mesh=mesh,
        in_specs=(
            P("dp", "tensor"),
            P("dp", "tensor"),
            P("dp", None),
            P("dp", None),
            P(("expert", "tensor"), "dp", None),
            P(("expert", "tensor"), "dp", None),
            P(("expert", "tensor"), "dp", None),
        ),
        out_specs=(P("dp", "tensor"), P("dp", "tensor"), P("dp", None)),
        check_vma=False,
    )
```

```python
import functools

import jax
import jax.numpy as jnp
from jax import lax
from jax.experimental import pallas as pl
from jax.experimental.pallas import tpu as pltpu
from jax.sharding import PartitionSpec as P

CAP = 48
LANES = 128
MIB = 2**20
EARLY = 6e9
BF16 = jnp.bfloat16
F32 = jnp.float32
CONTRACT_LAST = (((1,), (1,)), ((), ()))


def call(kernel, name, out_shape, operands, flops, scratch=(), limit=8, copied=0):
    outs = out_shape if isinstance(out_shape, list) else [out_shape]
    moved = sum(a.size * a.dtype.itemsize for a in [*operands, *outs])
    spec = pl.BlockSpec(memory_space=pltpu.VMEM)
    return pl.pallas_call(
        kernel,
        out_shape=out_shape,
        in_specs=[spec] * len(operands),
        out_specs=[pl.BlockSpec(memory_space=pl.ANY)] * copied + [spec] * (len(outs) - copied)
        if isinstance(out_shape, list)
        else spec,
        scratch_shapes=list(scratch),
        compiler_params=pltpu.CompilerParams(vmem_limit_bytes=limit * MIB),
        cost_estimate=pl.CostEstimate(flops=int(flops), bytes_accessed=int(moved), transcendentals=0),
        name=name,
    )(*operands)


def after(values, earlier):
    return lax.optimization_barrier((values, earlier))


def number_kernel(routes_ref, key_ref):
    experts, rows = key_ref.shape
    ids = lax.broadcasted_iota(jnp.int32, (experts, rows), 0)
    hit = jnp.zeros((experts, rows), F32)
    for r in range(routes_ref.shape[0]):
        hit = hit + (routes_ref[r : r + 1, :] == ids).astype(F32)
    before = (
        lax.broadcasted_iota(jnp.int32, (LANES, LANES), 0) < lax.broadcasted_iota(jnp.int32, (LANES, LANES), 1)
    ).astype(BF16)
    offset = jnp.zeros((experts, 1), F32)
    for start in range(0, rows, LANES):
        part = hit[:, start : start + LANES]
        rank = jnp.dot(part.astype(BF16), before, preferred_element_type=F32) + offset
        offset = offset + jnp.sum(part, axis=1, keepdims=True)
        key_ref[:, start : start + LANES] = jnp.where(part > 0.0, rank, -1.0)


def position(cores):
    t = lax.axis_index("tensor")
    return lax.div(t, cores), lax.rem(t, cores), lax.axis_index("expert")


def pick_kernel(cores, key_ref, *refs):
    sources, pieces = refs[:cores], refs[cores:]
    chips = len(pieces)
    rows, width = sources[0].shape
    chip, core, e = position(cores)
    slot = lax.broadcasted_iota(jnp.int32, (CAP, rows), 0).astype(F32)
    masks = []
    for dh in range(chips):
        expert = (e * chips + lax.rem(chip + dh, chips)) * cores + core
        masks.append((key_ref[pl.ds(expert, 1), :] == slot).astype(BF16))
    mask = jnp.concatenate(masks, axis=0)
    for dc, source in enumerate(sources):
        picked = jnp.dot(mask, source[...], preferred_element_type=F32).astype(BF16)
        column = pl.multiple_of(lax.rem(core - dc + cores, cores) * width, width)
        for dh, piece in enumerate(pieces):
            piece[:, pl.ds(column, width)] = picked[dh * CAP : (dh + 1) * CAP]


def gather_pieces(x_ref, pieces, chips, cores):
    chip, _, _ = position(cores)
    width = pieces[0].shape[1]
    for index, piece in enumerate(pieces):
        db, dh = divmod(index, chips)
        column = pl.multiple_of(lax.rem(chip - dh + chips, chips) * width, width)
        x_ref[db * CAP : (db + 1) * CAP, pl.ds(column, width)] = piece[...]


def project_back(terms, pieces, chips, cores):
    chip, _, _ = position(cores)
    blocks = len(pieces) // chips
    width = pieces[0].shape[1]
    for dh in range(chips):
        column = pl.ds(pl.multiple_of(lax.rem(chip + dh, chips) * width, width), width)
        total = None
        for h_ref, w_ref in terms:
            term = jnp.dot(h_ref[...], w_ref[0, :, column], preferred_element_type=F32)
            total = term if total is None else total + term
        total = total.astype(BF16)
        for db in range(blocks):
            row = (-db) % blocks * CAP
            pieces[db * chips + dh][...] = total[row : row + CAP]


def chunks_of(hid_dev):
    size = 256 if hid_dev % 256 == 0 else hid_dev
    return [slice(start, start + size) for start in range(0, hid_dev, size)]


def forward_kernel(chips, cores, count, *refs):
    pieces, (gate_ref, up_ref, down_ref) = refs[:count], refs[count : count + 3]
    act_ref, scale_ref = refs[count + 3 : count + 5]
    outs, (x_ref, hid_ref) = refs[count + 5 : 2 * count + 5], refs[2 * count + 5 :]
    gather_pieces(x_ref, pieces, chips, cores)
    for part in chunks_of(gate_ref.shape[1]):
        gate_pre = lax.dot_general(x_ref[...], gate_ref[0, part, :], CONTRACT_LAST, preferred_element_type=F32)
        up_pre = lax.dot_general(x_ref[...], up_ref[0, part, :], CONTRACT_LAST, preferred_element_type=F32)
        sig = jax.nn.sigmoid(gate_pre)
        act = gate_pre * sig
        hid_ref[:, part] = (act * up_pre).astype(BF16)
        act_ref[:, part] = act
        scale_ref[:, part] = up_pre * (sig * (1.0 + gate_pre * (1.0 - sig)))
    project_back([(hid_ref, down_ref)], outs, chips, cores)


def backward_kernel(chips, cores, count, *refs):
    pieces, (gate_ref, up_ref, down_ref) = refs[:count], refs[count : count + 3]
    act_ref, scale_ref = refs[count + 3 : count + 5]
    outs, (x_ref, grad_gate_ref, grad_up_ref) = refs[count + 5 : 2 * count + 5], refs[2 * count + 5 :]
    gather_pieces(x_ref, pieces, chips, cores)
    for part in chunks_of(gate_ref.shape[1]):
        grad_hid = lax.dot_general(x_ref[...], down_ref[0, part, :], CONTRACT_LAST, preferred_element_type=F32)
        grad_gate_ref[:, part] = (grad_hid * scale_ref[:, part]).astype(BF16)
        grad_up_ref[:, part] = (grad_hid * act_ref[:, part]).astype(BF16)
    project_back([(grad_gate_ref, gate_ref), (grad_up_ref, up_ref)], outs, chips, cores)


def add_blocks_kernel(chips, cores, *refs):
    pieces, out_ref = refs[:-1], refs[-1]
    width = out_ref.shape[1]
    count = len(pieces) // cores
    _, core, _ = position(cores)
    column = pl.ds(pl.multiple_of(core * width, width), width)
    for dh in range(chips):
        for dc in range(cores):
            total = None
            for piece in pieces[dc * count + dh : (dc + 1) * count : chips]:
                term = piece[:, column].astype(F32)
                total = term if total is None else total + term
            row = (dh * cores + dc) * CAP
            out_ref[row : row + CAP, :] = total.astype(BF16)


def partner_column(e, dz, columns):
    if columns & (columns - 1) == 0:
        return e ^ dz
    return (e - dz + columns) % columns


def slot_experts(chips, cores, columns):
    chip, core, e = position(cores)
    experts = []
    for dz in range(columns):
        for dh in range(chips):
            for dc in range(cores):
                column = partner_column(e, dz, columns)
                owner = lax.rem(chip - dh + chips, chips)
                experts.append((column * chips + owner) * cores + lax.rem(core - dc + cores, cores))
    return experts


def weights_kernel(chips, cores, columns, routes_ref, gates_ref, key_ref, out_ref, gate_ref, all_ref):
    experts, rows = key_ref.shape
    ids = lax.broadcasted_iota(jnp.int32, (experts, rows), 0)
    gate = jnp.zeros((experts, rows), F32)
    for r in range(routes_ref.shape[0]):
        gate = gate + jnp.where(routes_ref[r : r + 1, :] == ids, gates_ref[r : r + 1, :], 0.0)
    gate_ref[...] = gate
    slot = lax.broadcasted_iota(jnp.int32, (CAP, rows), 0).astype(F32)
    for index, expert in enumerate(slot_experts(chips, cores, columns)):
        same = key_ref[pl.ds(expert, 1), :] == slot
        all_ref[index * CAP : (index + 1) * CAP, :] = jnp.where(same, gate_ref[pl.ds(expert, 1), :], 0.0)
    slots = all_ref.shape[0]
    step = LANES if slots % LANES == 0 else slots
    for start in range(0, slots, step):
        out_ref[:, start : start + step] = all_ref[start : start + step, :].T.astype(BF16)


def place_parts(parts, all_ref):
    height = parts[0].shape[0]
    for index, part in enumerate(parts):
        all_ref[index * height : (index + 1) * height, :] = part[...]


def combine_kernel(columns, weight_ref, *refs):
    parts, gates = refs[:columns], refs[columns:-5]
    out_ref, total_ref, all_ref, rows_ref, sem = refs[-5:]
    place_parts(parts, all_ref)
    height = rows_ref.shape[1]
    copies = []
    for index in range(rows_ref.shape[0]):
        some = slice(index * height, (index + 1) * height)
        rows_ref[index] = jnp.dot(weight_ref[some, :], all_ref[...], preferred_element_type=F32).astype(BF16)
        copy = pltpu.make_async_copy(rows_ref.at[index], out_ref.at[pl.ds(index * height, height)], sem.at[index])
        copy.start()
        copies.append(copy)
    total = gates[0][...]
    for gate in gates[1:]:
        total = total + gate[...]
    total_ref[...] = total
    for copy in copies:
        copy.wait()


def combine_gate_kernel(chips, cores, columns, weight_ref, routes_ref, key_ref, grads_ref, *refs):
    parts, (out_ref, gate_ref, all_ref, sum_ref) = refs[:-4], refs[-4:]
    place_parts(parts, all_ref)
    out_ref[...] = jnp.dot(weight_ref[...], all_ref[...], preferred_element_type=F32).astype(BF16)
    rows = key_ref.shape[1]
    slot = lax.broadcasted_iota(jnp.int32, (CAP, rows), 0).astype(F32)
    routes = routes_ref[...]
    sum_ref[...] = lax.dot_general(all_ref[...], grads_ref[...], CONTRACT_LAST, preferred_element_type=F32)
    total = jnp.zeros(gate_ref.shape, F32)
    for index, expert in enumerate(slot_experts(chips, cores, columns)):
        same = key_ref[pl.ds(expert, 1), :] == slot
        row = jnp.where(same, sum_ref[index * CAP : (index + 1) * CAP, :], 0.0)
        total = total + jnp.where(routes == expert, jnp.sum(row, axis=0, keepdims=True), 0.0)
    gate_ref[...] = total


def body(sizes, tokens, grad_out, routes, gates, gate_weight, up_weight, down_weight):
    n_dp, groups, columns = sizes
    cores = 2 if groups % 2 == 0 else 1
    chips = groups // cores
    experts = groups * columns
    rows, width = tokens.shape
    _, hid_dev, feats = gate_weight.shape
    count = n_dp * chips
    tall = n_dp * CAP
    slots = groups * CAP
    routes_t, gates_t = routes.T, gates.T

    def shape(height, length, dtype=BF16):
        return jax.ShapeDtypeStruct((height, length), dtype)

    def to_core(value, dc):
        if dc == 0:
            return value
        pairs = [(t, t // cores * cores + (t + dc) % cores) for t in range(groups)]
        return lax.ppermute(value, "tensor", pairs)

    def to_chip(value, db, dh):
        if (db, dh) == (0, 0):
            return value
        pairs = []
        for b in range(n_dp):
            for t in range(groups):
                target = (t // cores + dh) % chips * cores + t % cores
                pairs.append((b * groups + t, (b + db) % n_dp * groups + target))
        return lax.ppermute(value, ("dp", "tensor"), pairs)

    hops = [(db, dh) for db in range(n_dp) for dh in range(chips)]
    first = (n_dp - 1) * chips
    order = sorted(range(count), key=lambda index: (hops[index][0] == 0, -hops[index][1]))

    def dispatch(pieces):
        arrived = {index: to_chip(pieces[hops[index][1]], *hops[index]) for index in order}
        return [arrived[index] for index in range(count)]

    def give_back(pieces):
        arrived = {index: to_chip(pieces[index], *hops[index]) for index in order}
        return [arrived[index] for index in range(count)]

    def swap(pieces):
        return [to_core(piece, dc) for dc in range(cores) for piece in pieces]

    def add_blocks(pieces):
        return call(
            functools.partial(add_blocks_kernel, chips, cores),
            "add_blocks",
            shape(slots, width),
            pieces,
            2 * slots * width,
        )

    def across(parts, dz, first=0):
        pairs = [(partner_column(z, dz - first, columns), z) for z in range(columns)]
        return lax.ppermute(parts[first], "expert", pairs)

    direct = [dz for dz in range(1, columns) if dz & (dz - 1) == 0][::-1]
    later = [dz for dz in range(1, columns) if dz not in direct]

    def pick(key, sources):
        return call(
            functools.partial(pick_kernel, cores),
            "pick",
            [shape(CAP, cores * width)] * chips,
            [key, *sources],
            EARLY,
        )

    token_sources = [to_core(tokens, dc) for dc in range(cores)]
    key = call(number_kernel, "number", shape(experts, rows, F32), [routes_t], EARLY)
    grad_sources = [to_core(grad_out, dc) for dc in range(cores)]
    tok_in = dispatch(pick(key, token_sources))
    tok_in[0], grad_pieces = lax.optimization_barrier((tok_in[0], pick(key, grad_sources)))
    grad_in = dispatch(grad_pieces)

    matmul_flops = 2 * tall * hid_dev * feats
    saved = [shape(tall, hid_dev, F32)] * 2
    piece = [shape(CAP, cores * width)] * count
    act, scale, *outs = call(
        functools.partial(forward_kernel, chips, cores, count),
        "forward",
        saved + piece,
        [*tok_in, gate_weight, up_weight, down_weight],
        3 * matmul_flops,
        [pltpu.VMEM((tall, feats), BF16), pltpu.VMEM((tall, hid_dev), BF16)],
        limit=24,
    )
    outs, grad_in = after(outs, grad_in)
    out_pieces = give_back(outs)
    backs = call(
        functools.partial(backward_kernel, chips, cores, count),
        "backward",
        piece,
        [*grad_in, gate_weight, up_weight, down_weight, act, scale],
        3 * matmul_flops,
        [pltpu.VMEM((tall, feats), BF16)] + [pltpu.VMEM((tall, hid_dev), BF16)] * 2,
        limit=24,
    )
    out_pieces[first], backs = after(out_pieces[first], backs)
    out_rows = add_blocks(swap(out_pieces))
    out_rows, backs = after(out_rows, backs)
    out_parts = {0: out_rows}
    for dz in direct:
        out_parts[dz] = across(out_parts, dz)
    back_pieces = give_back(backs)
    out_parts[direct[0]] = lax.optimization_barrier(out_parts[direct[0]])
    back_pieces[-1], out_parts = after(back_pieces[-1], out_parts)
    for dz in later:
        out_parts[dz] = across(out_parts, dz, dz & (dz - 1))
    back_rows = add_blocks(swap(back_pieces))
    back_parts = {0: back_rows}
    for dz in direct + later:
        back_parts[dz] = across(back_parts, dz)
    _, out_parts = after(back_rows, out_parts)

    weight_map = call(
        functools.partial(weights_kernel, chips, cores, columns),
        "weights",
        shape(rows, experts * CAP),
        [routes_t, gates_t, key],
        experts * CAP * rows,
        [pltpu.VMEM((experts, rows), F32), pltpu.VMEM((experts * CAP, rows), F32)],
        limit=16,
    )

    all_rows = pltpu.VMEM((experts * CAP, width), BF16)
    combine_flops = 2 * experts * CAP * rows * width
    mixed, gate_part = call(
        functools.partial(combine_gate_kernel, chips, cores, columns),
        "combine_gate",
        [shape(rows, width), shape(routes_t.shape[0], rows, F32)],
        [weight_map, routes_t, key, grad_out, *[out_parts[dz] for dz in range(columns)]],
        0,
        [all_rows, pltpu.VMEM((experts * CAP, rows), F32)],
        limit=24,
    )
    chip_part = gate_part
    for dc in range(1, cores):
        chip_part = chip_part + to_core(gate_part, dc)
    gate_parts = [to_chip(chip_part, 0, dh) for dh in range(chips)]
    grad_tokens, grad_gates = call(
        functools.partial(combine_kernel, columns),
        "combine",
        [shape(rows, width), shape(*gate_part.shape, F32)],
        [weight_map, *[back_parts[dz] for dz in range(columns)], *gate_parts],
        combine_flops,
        [all_rows, pltpu.VMEM((2, rows // 2, width), BF16), pltpu.SemaphoreType.DMA((2,))],
        limit=16,
        copied=1,
    )
    return (mixed, grad_tokens, grad_gates.T)


def solution(mesh):
    sizes = (mesh.shape["dp"], mesh.shape["tensor"], mesh.shape["expert"])
    return jax.shard_map(
        functools.partial(body, sizes),
        mesh=mesh,
        in_specs=(
            P("dp", "tensor"),
            P("dp", "tensor"),
            P("dp", None),
            P("dp", None),
            P(("expert", "tensor"), "dp", None),
            P(("expert", "tensor"), "dp", None),
            P(("expert", "tensor"), "dp", None),
        ),
        out_specs=(P("dp", "tensor"), P("dp", "tensor"), P("dp", None)),
        check_vma=False,
    )
```

```python
import functools

import jax
import jax.numpy as jnp
from jax import lax
from jax.experimental import pallas as pl
from jax.experimental.pallas import tpu as pltpu
from jax.sharding import PartitionSpec as P

CAP = 48
LANES = 128
MIB = 2**20
EARLY = 6e9
BF16 = jnp.bfloat16
F32 = jnp.float32
CONTRACT_LAST = (((1,), (1,)), ((), ()))


def call(kernel, name, out_shape, operands, flops, scratch=(), limit=8):
    outs = out_shape if isinstance(out_shape, list) else [out_shape]
    moved = sum(a.size * a.dtype.itemsize for a in [*operands, *outs])
    spec = pl.BlockSpec(memory_space=pltpu.VMEM)
    return pl.pallas_call(
        kernel,
        out_shape=out_shape,
        in_specs=[spec] * len(operands),
        out_specs=[spec] * len(outs) if isinstance(out_shape, list) else spec,
        scratch_shapes=list(scratch),
        compiler_params=pltpu.CompilerParams(vmem_limit_bytes=limit * MIB),
        cost_estimate=pl.CostEstimate(flops=int(flops), bytes_accessed=int(moved), transcendentals=0),
        name=name,
    )(*operands)


def after(values, earlier):
    return lax.optimization_barrier((values, earlier))


def number_kernel(routes_ref, key_ref):
    experts, rows = key_ref.shape
    ids = lax.broadcasted_iota(jnp.int32, (experts, rows), 0)
    hit = jnp.zeros((experts, rows), F32)
    for r in range(routes_ref.shape[0]):
        hit = hit + (routes_ref[r : r + 1, :] == ids).astype(F32)
    before = (
        lax.broadcasted_iota(jnp.int32, (LANES, LANES), 0) < lax.broadcasted_iota(jnp.int32, (LANES, LANES), 1)
    ).astype(BF16)
    offset = jnp.zeros((experts, 1), F32)
    for start in range(0, rows, LANES):
        part = hit[:, start : start + LANES]
        rank = jnp.dot(part.astype(BF16), before, preferred_element_type=F32) + offset
        offset = offset + jnp.sum(part, axis=1, keepdims=True)
        key_ref[:, start : start + LANES] = jnp.where(part > 0.0, rank, -1.0)


def position(cores):
    t = lax.axis_index("tensor")
    return lax.div(t, cores), lax.rem(t, cores), lax.axis_index("expert")


def pick_kernel(cores, key_ref, *refs):
    sources, pieces = refs[:cores], refs[cores:]
    chips = len(pieces)
    rows, width = sources[0].shape
    chip, core, e = position(cores)
    slot = lax.broadcasted_iota(jnp.int32, (CAP, rows), 0).astype(F32)
    masks = []
    for dh in range(chips):
        expert = (e * chips + lax.rem(chip + dh, chips)) * cores + core
        masks.append((key_ref[pl.ds(expert, 1), :] == slot).astype(BF16))
    mask = jnp.concatenate(masks, axis=0)
    for dc, source in enumerate(sources):
        picked = jnp.dot(mask, source[...], preferred_element_type=F32).astype(BF16)
        column = pl.multiple_of(lax.rem(core - dc + cores, cores) * width, width)
        for dh, piece in enumerate(pieces):
            piece[:, pl.ds(column, width)] = picked[dh * CAP : (dh + 1) * CAP]


def gather_pieces(x_ref, pieces, chips, cores):
    chip, _, _ = position(cores)
    width = pieces[0].shape[1]
    for index, piece in enumerate(pieces):
        db, dh = divmod(index, chips)
        column = pl.multiple_of(lax.rem(chip - dh + chips, chips) * width, width)
        x_ref[db * CAP : (db + 1) * CAP, pl.ds(column, width)] = piece[...]


def project_back(terms, pieces, chips, cores):
    chip, _, _ = position(cores)
    blocks = len(pieces) // chips
    width = pieces[0].shape[1]
    for dh in range(chips):
        column = pl.ds(pl.multiple_of(lax.rem(chip + dh, chips) * width, width), width)
        total = None
        for h_ref, w_ref in terms:
            term = jnp.dot(h_ref[...], w_ref[0, :, column], preferred_element_type=F32)
            total = term if total is None else total + term
        total = total.astype(BF16)
        for db in range(blocks):
            row = (-db) % blocks * CAP
            pieces[db * chips + dh][...] = total[row : row + CAP]


def chunks_of(hid_dev):
    size = 256 if hid_dev % 256 == 0 else hid_dev
    return [slice(start, start + size) for start in range(0, hid_dev, size)]


def forward_kernel(chips, cores, count, *refs):
    pieces, (gate_ref, up_ref, down_ref) = refs[:count], refs[count : count + 3]
    act_ref, scale_ref = refs[count + 3 : count + 5]
    outs, (x_ref, hid_ref) = refs[count + 5 : 2 * count + 5], refs[2 * count + 5 :]
    gather_pieces(x_ref, pieces, chips, cores)
    for part in chunks_of(gate_ref.shape[1]):
        gate_pre = lax.dot_general(x_ref[...], gate_ref[0, part, :], CONTRACT_LAST, preferred_element_type=F32)
        up_pre = lax.dot_general(x_ref[...], up_ref[0, part, :], CONTRACT_LAST, preferred_element_type=F32)
        sig = jax.nn.sigmoid(gate_pre)
        act = gate_pre * sig
        hid_ref[:, part] = (act * up_pre).astype(BF16)
        act_ref[:, part] = act
        scale_ref[:, part] = up_pre * (sig * (1.0 + gate_pre * (1.0 - sig)))
    project_back([(hid_ref, down_ref)], outs, chips, cores)


def backward_kernel(chips, cores, count, *refs):
    pieces, (gate_ref, up_ref, down_ref) = refs[:count], refs[count : count + 3]
    act_ref, scale_ref = refs[count + 3 : count + 5]
    outs, (x_ref, grad_gate_ref, grad_up_ref) = refs[count + 5 : 2 * count + 5], refs[2 * count + 5 :]
    gather_pieces(x_ref, pieces, chips, cores)
    for part in chunks_of(gate_ref.shape[1]):
        grad_hid = lax.dot_general(x_ref[...], down_ref[0, part, :], CONTRACT_LAST, preferred_element_type=F32)
        grad_gate_ref[:, part] = (grad_hid * scale_ref[:, part]).astype(BF16)
        grad_up_ref[:, part] = (grad_hid * act_ref[:, part]).astype(BF16)
    project_back([(grad_gate_ref, gate_ref), (grad_up_ref, up_ref)], outs, chips, cores)


def add_blocks_kernel(chips, cores, *refs):
    pieces, out_ref = refs[:-1], refs[-1]
    width = out_ref.shape[1]
    count = len(pieces) // cores
    _, core, _ = position(cores)
    column = pl.ds(pl.multiple_of(core * width, width), width)
    for dh in range(chips):
        for dc in range(cores):
            total = None
            for piece in pieces[dc * count + dh : (dc + 1) * count : chips]:
                term = piece[:, column].astype(F32)
                total = term if total is None else total + term
            row = (dh * cores + dc) * CAP
            out_ref[row : row + CAP, :] = total.astype(BF16)


def partner_column(e, dz, columns):
    if columns & (columns - 1) == 0:
        return e ^ dz
    return (e - dz + columns) % columns


def slot_experts(chips, cores, columns):
    chip, core, e = position(cores)
    experts = []
    for dz in range(columns):
        for dh in range(chips):
            for dc in range(cores):
                column = partner_column(e, dz, columns)
                owner = lax.rem(chip - dh + chips, chips)
                experts.append((column * chips + owner) * cores + lax.rem(core - dc + cores, cores))
    return experts


def weights_kernel(chips, cores, columns, routes_ref, gates_ref, key_ref, out_ref, gate_ref, all_ref):
    experts, rows = key_ref.shape
    ids = lax.broadcasted_iota(jnp.int32, (experts, rows), 0)
    gate = jnp.zeros((experts, rows), F32)
    for r in range(routes_ref.shape[0]):
        gate = gate + jnp.where(routes_ref[r : r + 1, :] == ids, gates_ref[r : r + 1, :], 0.0)
    gate_ref[...] = gate
    slot = lax.broadcasted_iota(jnp.int32, (CAP, rows), 0).astype(F32)
    for index, expert in enumerate(slot_experts(chips, cores, columns)):
        same = key_ref[pl.ds(expert, 1), :] == slot
        all_ref[index * CAP : (index + 1) * CAP, :] = jnp.where(same, gate_ref[pl.ds(expert, 1), :], 0.0)
    slots = all_ref.shape[0]
    step = LANES if slots % LANES == 0 else slots
    for start in range(0, slots, step):
        out_ref[:, start : start + step] = all_ref[start : start + step, :].T.astype(BF16)


def place_parts(parts, all_ref):
    height = parts[0].shape[0]
    for index, part in enumerate(parts):
        all_ref[index * height : (index + 1) * height, :] = part[...]


def combine_kernel(columns, weight_ref, *refs):
    parts, gates = refs[:columns][::-1], refs[columns:-3]
    out_ref, total_ref, all_ref = refs[-3:]
    place_parts(parts, all_ref)
    out_ref[...] = jnp.dot(weight_ref[...], all_ref[...], preferred_element_type=F32).astype(BF16)
    total = gates[0][...]
    for gate in gates[1:]:
        total = total + gate[...]
    total_ref[...] = total


def combine_gate_kernel(chips, cores, columns, weight_ref, routes_ref, key_ref, grads_ref, *refs):
    parts, (out_ref, gate_ref, all_ref, sum_ref) = refs[:-4], refs[-4:]
    place_parts(parts, all_ref)
    out_ref[...] = jnp.dot(weight_ref[...], all_ref[...], preferred_element_type=F32).astype(BF16)
    rows = key_ref.shape[1]
    slot = lax.broadcasted_iota(jnp.int32, (CAP, rows), 0).astype(F32)
    routes = routes_ref[...]
    sum_ref[...] = lax.dot_general(all_ref[...], grads_ref[...], CONTRACT_LAST, preferred_element_type=F32)
    total = jnp.zeros(gate_ref.shape, F32)
    for index, expert in enumerate(slot_experts(chips, cores, columns)):
        same = key_ref[pl.ds(expert, 1), :] == slot
        row = jnp.where(same, sum_ref[index * CAP : (index + 1) * CAP, :], 0.0)
        total = total + jnp.where(routes == expert, jnp.sum(row, axis=0, keepdims=True), 0.0)
    gate_ref[...] = total


def body(sizes, tokens, grad_out, routes, gates, gate_weight, up_weight, down_weight):
    n_dp, groups, columns = sizes
    cores = 2 if groups % 2 == 0 else 1
    chips = groups // cores
    experts = groups * columns
    rows, width = tokens.shape
    _, hid_dev, feats = gate_weight.shape
    count = n_dp * chips
    tall = n_dp * CAP
    slots = groups * CAP
    routes_t, gates_t = routes.T, gates.T

    def shape(height, length, dtype=BF16):
        return jax.ShapeDtypeStruct((height, length), dtype)

    def to_core(value, dc):
        if dc == 0:
            return value
        pairs = [(t, t // cores * cores + (t + dc) % cores) for t in range(groups)]
        return lax.ppermute(value, "tensor", pairs)

    def to_chip(value, db, dh):
        if (db, dh) == (0, 0):
            return value
        pairs = []
        for b in range(n_dp):
            for t in range(groups):
                target = (t // cores + dh) % chips * cores + t % cores
                pairs.append((b * groups + t, (b + db) % n_dp * groups + target))
        return lax.ppermute(value, ("dp", "tensor"), pairs)

    hops = [(db, dh) for db in range(n_dp) for dh in range(chips)]
    first = (n_dp - 1) * chips
    order = sorted(range(count), key=lambda index: (hops[index][0] == 0, -hops[index][1]))

    def dispatch(pieces):
        arrived = {index: to_chip(pieces[hops[index][1]], *hops[index]) for index in order}
        return [arrived[index] for index in range(count)]

    def give_back(pieces):
        arrived = {index: to_chip(pieces[index], *hops[index]) for index in order}
        return [arrived[index] for index in range(count)]

    def swap(pieces):
        return [to_core(piece, dc) for dc in range(cores) for piece in pieces]

    def add_blocks(pieces):
        return call(
            functools.partial(add_blocks_kernel, chips, cores),
            "add_blocks",
            shape(slots, width),
            pieces,
            2 * slots * width,
        )

    def across(parts, dz, first=0):
        pairs = [(partner_column(z, dz - first, columns), z) for z in range(columns)]
        return lax.ppermute(parts[first], "expert", pairs)

    direct = [dz for dz in range(1, columns) if dz & (dz - 1) == 0][::-1]
    later = [dz for dz in range(1, columns) if dz not in direct]

    def pick(key, sources):
        return call(
            functools.partial(pick_kernel, cores),
            "pick",
            [shape(CAP, cores * width)] * chips,
            [key, *sources],
            EARLY,
        )

    token_sources = [to_core(tokens, dc) for dc in range(cores)]
    key = call(number_kernel, "number", shape(experts, rows, F32), [routes_t], EARLY)
    grad_sources = [to_core(grad_out, dc) for dc in range(cores)]
    tok_in = dispatch(pick(key, token_sources))
    tok_in[0], grad_pieces = lax.optimization_barrier((tok_in[0], pick(key, grad_sources)))
    grad_in = dispatch(grad_pieces)

    matmul_flops = 2 * tall * hid_dev * feats
    saved = [shape(tall, hid_dev, F32)] * 2
    piece = [shape(CAP, cores * width)] * count
    act, scale, *outs = call(
        functools.partial(forward_kernel, chips, cores, count),
        "forward",
        saved + piece,
        [*tok_in, gate_weight, up_weight, down_weight],
        3 * matmul_flops,
        [pltpu.VMEM((tall, feats), BF16), pltpu.VMEM((tall, hid_dev), BF16)],
        limit=24,
    )
    outs, grad_in = after(outs, grad_in)
    out_pieces = give_back(outs)
    backs = call(
        functools.partial(backward_kernel, chips, cores, count),
        "backward",
        piece,
        [*grad_in, gate_weight, up_weight, down_weight, act, scale],
        3 * matmul_flops,
        [pltpu.VMEM((tall, feats), BF16)] + [pltpu.VMEM((tall, hid_dev), BF16)] * 2,
        limit=24,
    )
    out_pieces[first], backs = after(out_pieces[first], backs)
    out_rows = add_blocks(swap(out_pieces))
    out_rows, backs = after(out_rows, backs)
    out_parts = {0: out_rows}
    for dz in direct:
        out_parts[dz] = across(out_parts, dz)
    back_pieces = give_back(backs)
    out_parts[direct[0]] = lax.optimization_barrier(out_parts[direct[0]])
    back_pieces[-1], out_parts = after(back_pieces[-1], out_parts)
    for dz in later:
        out_parts[dz] = across(out_parts, dz, dz & (dz - 1))
    back_rows = add_blocks(swap(back_pieces))
    back_parts = {0: back_rows}
    for dz in later + direct:
        back_parts[dz] = across(back_parts, dz)
    _, out_parts = after(back_rows, out_parts)

    weight_map = call(
        functools.partial(weights_kernel, chips, cores, columns),
        "weights",
        shape(rows, experts * CAP),
        [routes_t, gates_t, key],
        experts * CAP * rows,
        [pltpu.VMEM((experts, rows), F32), pltpu.VMEM((experts * CAP, rows), F32)],
        limit=16,
    )

    all_rows = pltpu.VMEM((experts * CAP, width), BF16)
    combine_flops = 2 * experts * CAP * rows * width
    mixed, gate_part = call(
        functools.partial(combine_gate_kernel, chips, cores, columns),
        "combine_gate",
        [shape(rows, width), shape(routes_t.shape[0], rows, F32)],
        [weight_map, routes_t, key, grad_out, *[out_parts[dz] for dz in range(columns)]],
        0,
        [all_rows, pltpu.VMEM((experts * CAP, rows), F32)],
        limit=24,
    )
    chip_part = gate_part
    for dc in range(1, cores):
        chip_part = chip_part + to_core(gate_part, dc)
    gate_parts = [to_chip(chip_part, 0, dh) for dh in range(chips)]
    grad_tokens, grad_gates = call(
        functools.partial(combine_kernel, columns),
        "combine",
        [shape(rows, width), shape(*gate_part.shape, F32)],
        [weight_map, *[back_parts[dz] for dz in reversed(range(columns))], *gate_parts],
        combine_flops,
        [all_rows],
        limit=16,
    )
    return (mixed, grad_tokens, grad_gates.T)


def solution(mesh):
    sizes = (mesh.shape["dp"], mesh.shape["tensor"], mesh.shape["expert"])
    return jax.shard_map(
        functools.partial(body, sizes),
        mesh=mesh,
        in_specs=(
            P("dp", "tensor"),
            P("dp", "tensor"),
            P("dp", None),
            P("dp", None),
            P(("expert", "tensor"), "dp", None),
            P(("expert", "tensor"), "dp", None),
            P(("expert", "tensor"), "dp", None),
        ),
        out_specs=(P("dp", "tensor"), P("dp", "tensor"), P("dp", None)),
        check_vma=False,
    )
```
